32 devices in a mesh: dp: 8 (over y, x, core), tensor: 4 (over z).
Axes of the slice: x: 2, y: 2, z: 4, core: 2. Of those that a mesh axis runs over, the one named last changes fastest.
Arguments:
- tokens: bfloat16 [8192, 2048], P(('dp', 'tensor')), may hold values from -6 to 6
- segments: int32 [8192], P('dp'), may hold values from 0 to 2, as said below
- positions: int32 [8192], P('dp'), may hold values from 0 to 2047, as said below
- attn_gain: bfloat16 [2048], P('dp'), may hold values from 0.099609375 to 1.8984375
- w_query: bfloat16 [2048, 2048], P('dp', 'tensor'), may hold values from -0.125 to 0.125
- w_key: bfloat16 [2048, 512], P('dp', 'tensor'), may hold values from -0.125 to 0.125
- w_value: bfloat16 [2048, 512], P('dp', 'tensor'), may hold values from -0.125 to 0.125
- w_out: bfloat16 [2048, 2048], P('tensor', 'dp'), may hold values from -1.5 to 1.5
- mlp_gain: bfloat16 [2048], P('dp'), may hold values from 0.099609375 to 1.8984375
- w_gate: bfloat16 [2048, 8192], P('dp', 'tensor'), may hold values from -0.125 to 0.125
- w_up: bfloat16 [2048, 8192], P('dp', 'tensor'), may hold values from -0.125 to 0.125
- w_down: bfloat16 [8192, 2048], P('tensor', 'dp'), may hold values from -0.0625 to 0.0625
- grad_out: bfloat16 [8192, 2048], P(('dp', 'tensor')), may hold values from -6 to 6
Outputs:
- block_out: bfloat16 [8192, 2048], P(('dp', 'tensor'))
- grad_tokens: float32 [8192, 2048], P(('dp', 'tensor'))
- grad_attn_gain: float32 [2048], P('dp')
- grad_query: float32 [2048, 2048], P('dp', 'tensor')
- grad_key: float32 [2048, 512], P('dp', 'tensor')
- grad_value: float32 [2048, 512], P('dp', 'tensor')
- grad_out_proj: float32 [2048, 2048], P('tensor', 'dp')
- grad_mlp_gain: float32 [2048], P('dp')
- grad_gate: float32 [2048, 8192], P('dp', 'tensor')
- grad_up: float32 [2048, 8192], P('dp', 'tensor')
- grad_down: float32 [8192, 2048], P('tensor', 'dp')
The draws below stay inside these ranges and needn't reach their ends.
Inputs may be any that keep to these rules, and one draw needn't show every extreme that they name: `segments`: each sequence of 1024 tokens holds three documents numbered 0, 1, 2 in order: document 0 ends before token 256 and document 1 ends after token 768 and at least 64 tokens before the sequence's end. Within a document positions rise by one from token to token; each document's first position is below 2048.
All inputs are finite; a program needn't handle non-finite values.
Results may differ from the reference program's by a relative error of at most 0.013.
Values may be sent and summed in bfloat16 or wider, within the bound.
A program may use at most 256 MiB of HBM per device.

```python
import math
import jax
import jax.numpy as jnp
from jax import lax

D = 2048
H = 32
KV = 8
HD = 64
FF = 8192
SEQ = 1024
TOKENS = 8192


def document_bounds(key):
    sequences = TOKENS // SEQ
    first_end = jax.random.randint(jax.random.fold_in(key, 11), (sequences, 1), SEQ // 64 + 1, SEQ // 4 - SEQ // 32)
    second_end = jax.random.randint(jax.random.fold_in(key, 12), (sequences, 1), 3 * SEQ // 4 + 1, SEQ - SEQ // 16 + 1)
    places = jnp.arange(SEQ, dtype=jnp.int32)[None, :]
    return (first_end, second_end, places)


def draw_segments(key, part):
    first_end, second_end, places = document_bounds(key)
    numbers = (places >= first_end).astype(jnp.int32) + (places >= second_end).astype(jnp.int32)
    return numbers.reshape(TOKENS)


def draw_positions(key, part):
    first_end, second_end, places = document_bounds(key)
    key = jax.random.fold_in(key, 5)
    sequences = TOKENS // SEQ
    beginnings = jax.random.randint(key, (sequences, 3), 0, SEQ)
    sequence_ids = jnp.arange(sequences, dtype=jnp.int32)[:, None]
    forced = 2 * SEQ - (second_end - first_end)
    second_begin = jnp.where(sequence_ids == 0, forced, beginnings[:, 1:2])
    in_second = places >= first_end
    in_third = places >= second_end
    begin_at = jnp.where(in_third, second_end, jnp.where(in_second, first_end, 0))
    offset = jnp.where(in_third, beginnings[:, 2:3], jnp.where(in_second, second_begin, beginnings[:, 0:1]))
    return (offset + places - begin_at).astype(jnp.int32).reshape(TOKENS)


def spiked(values, rng, source, target, blocks, factor):
    def block_of(position):
        return (jnp.arange(values.shape[position]) // (values.shape[position] // blocks)).reshape((-1,) + (1,) * (values.ndim - 1 - position))

    near = jax.random.permutation(rng, blocks)[block_of(target)]
    far = (block_of(target) + blocks // 2) % blocks
    return jnp.where((block_of(source) == near) | (block_of(source) == far), factor * values, values)


def steps_of(rng, dims, shards, least, top_value):
    def one(dim, shards_of):
        draws = jax.random.uniform(jax.random.fold_in(jax.random.fold_in(rng, 6), dim), (shards_of,), jnp.float32, least / len(shards), top_value / len(shards))
        return jnp.repeat(jnp.exp(draws), dims[dim] // shards_of).reshape((-1,) + (1,) * (len(dims) - dim - 1))

    loudness = one(*shards[0])
    for cut in shards[1:]:
        loudness = loudness * one(*cut)
    return loudness


def noise(stream_key, dims, spread, reach, pieces=(), held_as=jnp.bfloat16):
    loudness = steps_of(stream_key, dims, pieces, -0.22, 0.18) if pieces else 1.0
    drawn = jax.random.normal(stream_key, dims, jnp.float32) * spread * loudness
    return jnp.minimum(jnp.maximum(drawn, -reach), reach).astype(held_as)


def bell_draw_with(own_key, extent, spread, most, pieces, heavy, kind=jnp.bfloat16):
    values = spread * jax.random.normal(own_key, extent, jnp.float32)
    if pieces:
        values = values * steps_of(own_key, extent, pieces, -0.22, 0.18)
    return jnp.clip(spiked(values, jax.random.fold_in(own_key, 3), *heavy), -most, most).astype(kind)


def setup_inputs(seed: int = 0) -> dict:
    keys = jax.random.split(jax.random.key(seed), 14)
    return {
        "tokens": bell_draw_with(keys[0], (TOKENS, D), 1.0, 6.0, ((0, 32),), (0, 1, 32, 2.75)),
        "segments": draw_segments(jax.random.fold_in(keys[13], 71), 0),
        "positions": draw_positions(jax.random.fold_in(keys[13], 71), 0),
        "attn_gain": jnp.clip(1.0 + 0.18 * jax.random.normal(keys[3], (D,), jnp.float32), 0.099609375, 1.8984375).astype(jnp.bfloat16),
        "w_query": noise(keys[4], (D, H * HD), D ** -0.5, 0.125, ((0, 8), (1, 4))),
        "w_key": noise(keys[5], (D, KV * HD), D ** -0.5, 0.125, ((0, 8), (1, 4))),
        "w_value": noise(keys[6], (D, KV * HD), D ** -0.5, 0.125, ((0, 8), (1, 4))),
        "w_out": noise(keys[7], (H * HD, D), (max(D // 128, 1)) ** -0.5, 1.5, ((0, 4), (1, 8))),
        "mlp_gain": jnp.clip(1.0 + 0.18 * jax.random.normal(keys[8], (D,), jnp.float32), 0.099609375, 1.8984375).astype(jnp.bfloat16),
        "w_gate": noise(keys[9], (D, FF), D ** -0.5, 0.125, ((0, 8), (1, 4))),
        "w_up": noise(keys[10], (D, FF), D ** -0.5, 0.125, ((0, 8), (1, 4))),
        "w_down": noise(keys[11], (FF, D), FF ** -0.5, 0.0625, ((0, 4), (1, 8))),
        "grad_out": bell_draw_with(keys[12], (TOKENS, D), 1.0, 6.0, ((0, 32),), (0, 1, 32, 2.75)),
    }


EPSILON = 1e-05
MASKED = -1e+30

@jax.custom_vjp
def low(v):
    return lax.optimization_barrier(v.astype(jnp.bfloat16)).astype(jnp.float32)

@jax.custom_vjp
def low_back(v):
    return v

def low_keep(v):
    return (low(v), None)

def low_pass(kept, grad):
    return (grad,)

def back_keep(v):
    return (v, None)

def back_low(kept, grad):
    return (low(grad),)
low.defvjp(low_keep, low_pass)
low_back.defvjp(back_keep, back_low)

def frequencies(head_size):
    inverse = 1.0 / 500000.0 ** (jnp.arange(head_size // 2, dtype=jnp.float32) * 2.0 / head_size)
    wavelength = 2.0 * math.pi / inverse
    smooth = (8192.0 / wavelength - 1.0) / 3.0
    blended = (1.0 - smooth) * inverse / 32.0 + smooth * inverse
    return jnp.where(wavelength > 8192.0, inverse / 32.0, jnp.where(wavelength < 2048.0, inverse, blended))

def tables(places, head_size):
    angles = places.astype(jnp.float32)[:, None] * frequencies(head_size)[None, :]
    cosine_table = jnp.cos(angles)
    sine_table = jnp.sin(angles)
    return (jnp.concatenate([cosine_table, cosine_table], -1), jnp.concatenate([sine_table, sine_table], -1))

def rotate(values, cosine_table, sine_table, sign):
    middle = values.shape[-1] // 2
    turned = jnp.concatenate([-values[..., middle:], values[..., :middle]], axis=-1)
    return values * cosine_table + sign * turned * sine_table

def matmul(left_side, right_side):
    return jnp.einsum('psd,de->pse', left_side, right_side, precision=lax.Precision.HIGHEST)

def attend_block(query_block, offset, key_rows, value_rows, segments):
    length = query_block.shape[0]
    raw_scores = low_back(jnp.einsum('qkgd,skd->kgqs', query_block, key_rows, precision=lax.Precision.HIGHEST))
    query_places = offset + lax.iota(jnp.int32, length)
    key_places = lax.iota(jnp.int32, key_rows.shape[0])
    query_segs = lax.dynamic_slice_in_dim(segments, offset, length)
    allowed = (key_places[None, :] <= query_places[:, None]) & (query_segs[:, None] == segments[None, :])
    scaled = jnp.where(allowed[None, None], 0.125 * raw_scores, MASKED)
    highest = lax.optimization_barrier(jnp.max(scaled, -1, keepdims=True))
    exponents = jnp.exp(scaled - highest)
    softmax_out = exponents / lax.optimization_barrier(jnp.sum(exponents, -1, keepdims=True))
    mixed_rows = jnp.einsum('kgqs,skd->qkgd', low(softmax_out), value_rows, precision=lax.Precision.HIGHEST)
    return low(low_back(mixed_rows))

def attend_sequence(element):
    query, key_lin, value, segments, places = element
    length = query.shape[0]
    cosine_table, sine_table = tables(places, HD)
    cosine_table = cosine_table[:, None, :]
    sine_table = sine_table[:, None, :]
    queries = low(rotate(query.reshape(length, H, HD), cosine_table, sine_table, 1.0)).reshape(length, KV, H // KV, HD)
    key_rows = low(rotate(key_lin.reshape(length, KV, HD), cosine_table, sine_table, 1.0))
    value_rows = value.reshape(length, KV, HD)
    block_rows = min(512, length)
    blocks = length // block_rows
    offsets = lax.iota(jnp.int32, blocks) * block_rows
    query_blocks = queries.reshape(blocks, block_rows, KV, H // KV, HD)

    def one_block(couple):
        return jax.checkpoint(attend_block)(couple[0], couple[1], key_rows, value_rows, segments)
    mixed_all = lax.map(one_block, (query_blocks, offsets))
    return mixed_all.reshape(length, H * HD)

def layer(rows, segments, places, params):
    attn_gain, w_query, w_key, w_value, w_out, mlp_gain, w_gate, w_up, w_down = params
    normed_one = low(rows * lax.rsqrt(lax.optimization_barrier(jnp.mean(rows * rows, -1, keepdims=True)) + EPSILON) * attn_gain)
    query = low_back(matmul(normed_one, w_query))
    key_lin = low_back(matmul(normed_one, w_key))
    value = low(low_back(matmul(normed_one, w_value)))
    attended = lax.map(attend_sequence, (query, key_lin, value, segments, places))
    residual = rows + low_back(matmul(attended, w_out))
    normed_two = low(residual * lax.rsqrt(lax.optimization_barrier(jnp.mean(residual * residual, -1, keepdims=True)) + EPSILON) * mlp_gain)
    gate_values = low_back(matmul(normed_two, w_gate))
    up_values = low_back(matmul(normed_two, w_up))
    product = low(jax.nn.silu(gate_values) * up_values)
    return residual + matmul(product, w_down)

def reference(tokens, segments, positions, attn_gain, w_query, w_key, w_value, w_out, mlp_gain, w_gate, w_up, w_down, grad_out):
    params = tuple((weight.astype(jnp.float32) for weight in (attn_gain, w_query, w_key, w_value, w_out, mlp_gain, w_gate, w_up, w_down)))
    sequences = tokens.shape[0] // SEQ
    per_group = math.gcd(sequences, max(1, 4096 // SEQ))
    groups = sequences // per_group
    inputs = tokens.astype(jnp.float32).reshape(groups, per_group, SEQ, D)
    cotangents = grad_out.astype(jnp.float32).reshape(groups, per_group, SEQ, D)
    seg_groups = segments.astype(jnp.int32).reshape(groups, per_group, SEQ)
    place_groups = positions.astype(jnp.int32).reshape(groups, per_group, SEQ)

    def group_step(running, element):
        rows, seg_rows, place_rows, backward = element

        def forward(rows_in, params_in):
            return layer(rows_in, seg_rows, place_rows, params_in)
        result, pullback = jax.vjp(forward, rows, params)
        grad_rows, grad_params = pullback(backward)
        running = jax.tree.map(lambda first, second: first + second, running, grad_params)
        return (running, (result.astype(jnp.bfloat16), grad_rows))
    starting = tuple((jnp.zeros(weight.shape, jnp.float32) for weight in params))
    totals, (outputs, grad_inputs) = lax.scan(group_step, starting, (inputs, seg_groups, place_groups, cotangents))
    block_out = outputs.reshape(TOKENS, D)
    grad_tokens = grad_inputs.reshape(TOKENS, D)
    return (block_out, grad_tokens, totals[0], totals[1], totals[2], totals[3], totals[4], totals[5], totals[6], totals[7], totals[8])
```

```python
import functools
import math

import jax
import jax.numpy as jnp
from jax import lax
from jax.experimental import pallas as pl
from jax.experimental.pallas import tpu as pltpu
from jax.sharding import PartitionSpec as P

HD = 64
EPSILON = 1e-05
MASKED = -1e30
F32 = jnp.float32
BF = jnp.bfloat16

def turn_t(values, cosine, sine, sign):
    half=values.shape[0]//2
    first, second = values[:half], values[half:]
    return jnp.concatenate([first*cosine - sign*second*sine, second*cosine + sign*first*sine],0)

def block_bias(segs_col, segs_row, start, block):
    keys=start+block
    key_places=lax.broadcasted_iota(jnp.int32,(keys,block),0)
    query_places=start+lax.broadcasted_iota(jnp.int32,(keys,block),1)
    allowed=(key_places<=query_places)&(segs_col[0:keys,:]==segs_row[0:1,start:start+block])
    return jnp.where(allowed,0.0,MASKED).astype(F32)

def attend_kernel(heads, groups, block, lin_ref, cos_ref, sin_ref, segc_ref, segr_ref,
                  mixed_ref, lse_ref, q_ref, kt_ref, k_ref, vt_ref, v_ref, bias_ref):
    length=lin_ref.shape[1]
    per=heads//groups
    cosine, sine = cos_ref[...], sin_ref[...]
    def rope(h,_):
        rows=pl.ds(pl.multiple_of(h*HD,HD),HD)
        q_ref[rows,:]=(turn_t(lin_ref[rows,:],cosine,sine,1.0).astype(BF)*jnp.asarray(0.125,BF))
        return 0
    lax.fori_loop(0,heads,rope,0)
    kv=groups*HD
    turned=[turn_t(lin_ref[(heads+g)*HD:(heads+g+1)*HD,:],cosine,sine,1.0) for g in range(groups)]
    keys_t=jnp.concatenate(turned,0)
    kt_ref[...]=keys_t.astype(BF)
    vals_t=lin_ref[(heads+groups)*HD:(heads+2*groups)*HD,:]
    vt_ref[...]=vals_t.astype(BF)
    keys_n=keys_t.T.astype(BF)
    vals_n=vals_t.T.astype(BF)
    for g in range(groups):
        k_ref[g]=keys_n[:,g*HD:(g+1)*HD]
        v_ref[g]=vals_n[:,g*HD:(g+1)*HD]
    for start in range(0,length,block):
        keys=start+block
        bias_ref[0:keys,:]=block_bias(segc_ref,segr_ref,start,block)
        def head(h,_):
            g=h//per
            rows=pl.ds(pl.multiple_of(h*HD,HD),HD)
            grows=pl.ds(pl.multiple_of(g*HD,HD),HD)
            scores=jnp.dot(k_ref[g,0:keys,:],q_ref[rows,start:start+block],preferred_element_type=F32)
            scores=scores+bias_ref[0:keys,:]
            top=jnp.max(scores,0,keepdims=True)
            weights=jnp.exp(scores-top)
            total=jnp.sum(weights,0,keepdims=True)
            out=jnp.dot(vt_ref[grows,0:keys],weights.astype(BF),preferred_element_type=F32)
            mixed_ref[rows,start:start+block]=(out/total).astype(BF)
            lse_ref[h,:,start:start+block]=top+jnp.log(total)
            return 0
        lax.fori_loop(0,heads,head,0)

def attend(lin, cosine, sine, segments, heads, groups):
    length=lin.shape[1]
    block=min(256,length)
    sds=jax.ShapeDtypeStruct
    vm=pl.BlockSpec(memory_space=pltpu.VMEM)
    return pl.pallas_call(functools.partial(attend_kernel,heads,groups,block),
        out_shape=(sds((heads*HD,length),BF),sds((heads,1,length),F32),sds((heads*HD,length),BF),
            sds((groups*HD,length),BF),sds((groups,length,HD),BF),sds((groups*HD,length),BF),sds((groups,length,HD),BF)),
        in_specs=[vm]*5,out_specs=(vm,)*7,
        scratch_shapes=[pltpu.VMEM((length,block),F32)],
        cost_estimate=pl.CostEstimate(flops=30_000_000_000,bytes_accessed=10_000_000,transcendentals=8_000_000),
        compiler_params=pltpu.CompilerParams(vmem_limit_bytes=48*1024*1024),
    )(lin,cosine,sine,segments.reshape(length,1),segments.reshape(1,length))

def attend_back_kernel(heads, groups, block, q_ref, kt_ref, k_ref, v_ref, lse_ref, gm_ref, cos_ref, sin_ref, segc_ref, segr_ref,
                  out_ref, bias_ref, qn_ref, gn_ref, dq_ref, dk_ref, dv_ref):
    length=q_ref.shape[1]
    per=heads//groups
    cosine, sine = cos_ref[...], sin_ref[...]
    def flip(p,_):
        rows=pl.ds(pl.multiple_of(p*2*HD,2*HD),2*HD)
        qn=q_ref[rows,:].astype(F32).T.astype(BF)
        gn=gm_ref[rows,:].astype(F32).T.astype(BF)
        qn_ref[2*p]=qn[:,:HD]
        qn_ref[2*p+1]=qn[:,HD:]
        gn_ref[2*p]=gn[:,:HD]
        gn_ref[2*p+1]=gn[:,HD:]
        return 0
    lax.fori_loop(0,heads//2,flip,0)
    dk_ref[...]=jnp.zeros_like(dk_ref)
    dv_ref[...]=jnp.zeros_like(dv_ref)
    for start in range(0,length,block):
        keys=start+block
        cols=slice(start,start+block)
        bias_ref[0:keys,:]=block_bias(segc_ref,segr_ref,start,block)
        def head(h,_):
            g=h//per
            rows=pl.ds(pl.multiple_of(h*HD,HD),HD)
            grows=pl.ds(pl.multiple_of(g*HD,HD),HD)
            scores=jnp.dot(k_ref[g,0:keys,:],q_ref[rows,cols],preferred_element_type=F32)
            probs=jnp.exp(scores+bias_ref[0:keys,:]-lse_ref[h,:,cols])
            dv_ref[g,0:keys,:]+=jnp.dot(probs.astype(BF),gn_ref[h,cols,:],preferred_element_type=F32)
            gp=jnp.dot(v_ref[g,0:keys,:],gm_ref[rows,cols],preferred_element_type=F32)
            weighted=probs*gp
            centre=jnp.sum(weighted,0,keepdims=True)
            gs=(weighted-probs*centre).astype(BF)
            dk_ref[g,0:keys,:]+=jnp.dot(gs,qn_ref[h,cols,:],preferred_element_type=F32)
            dq_ref[rows,cols]=0.125*jnp.dot(kt_ref[grows,0:keys],gs,preferred_element_type=F32)
            return 0
        lax.fori_loop(0,heads,head,0)
    def back(h,_):
        rows=pl.ds(pl.multiple_of(h*HD,HD),HD)
        out_ref[rows,:]=turn_t(dq_ref[rows,:],cosine,sine,-1.0).astype(BF)
        return 0
    lax.fori_loop(0,heads,back,0)
    dk=jnp.concatenate([dk_ref[g] for g in range(groups)],1).T
    dv=jnp.concatenate([dv_ref[g] for g in range(groups)],1).T
    for g in range(groups):
        out_ref[(heads+g)*HD:(heads+g+1)*HD,:]=turn_t(dk[g*HD:(g+1)*HD],cosine,sine,-1.0).astype(BF)
    out_ref[(heads+groups)*HD:,:]=dv.astype(BF)

def attend_back(q,kt,k,v,lse,gm,cosine,sine,segments,heads,groups):
    length=q.shape[1]
    block=min(256,length)
    vm=pl.BlockSpec(memory_space=pltpu.VMEM)
    return pl.pallas_call(functools.partial(attend_back_kernel,heads,groups,block),
        out_shape=jax.ShapeDtypeStruct(((heads+2*groups)*HD,length),BF),
        in_specs=[vm]*10,out_specs=vm,
        scratch_shapes=[pltpu.VMEM((length,block),F32),pltpu.VMEM((heads,length,HD),BF),pltpu.VMEM((heads,length,HD),BF),
            pltpu.VMEM((heads*HD,length),F32),pltpu.VMEM((groups,length,HD),F32),pltpu.VMEM((groups,length,HD),F32)],
        cost_estimate=pl.CostEstimate(flops=60_000_000_000,bytes_accessed=10_000_000,transcendentals=8_000_000),
        compiler_params=pltpu.CompilerParams(vmem_limit_bytes=48*1024*1024),
    )(q,kt,k,v,lse,gm,cosine,sine,segments.reshape(length,1),segments.reshape(1,length))


AXIS="tensor"
MESH=pl.DeviceIdType.MESH

def greet(here, count):
    barrier=pltpu.get_barrier_semaphore()
    @pl.when(here>0)
    def _(): pl.semaphore_signal(barrier,inc=1,device_id={AXIS:here-1},device_id_type=MESH)
    @pl.when(here<count-1)
    def _(): pl.semaphore_signal(barrier,inc=1,device_id={AXIS:here+1},device_id_type=MESH)
    pl.semaphore_wait(barrier,jnp.where((here>0)&(here<count-1),2,1))

def remote(src,dst,send,recv,target):
    return pltpu.make_async_remote_copy(src_ref=src,dst_ref=dst,send_sem=send,recv_sem=recv,
        device_id={AXIS:target},device_id_type=MESH)

class Line:
    def __init__(self,count,pieces,rows,part=None,sums=None,sum_sems=None,held=None,held_sems=None):
        self.n,self.pieces,self.rows=count,pieces,rows
        self.sub=rows//pieces
        self.here=lax.axis_index(AXIS)
        self.part,self.sums,self.sum_sems=part,sums,sum_sems
        self.held,self.held_sems=held,held_sems
    def span(self,u): return pl.ds(pl.multiple_of(u*self.sub,self.sub),self.sub)
    def fits(self,u): return (u>=0)&(u<self.pieces)
    def _target(self,way):
        return lax.min(self.here+1,self.n-1) if way==0 else lax.max(self.here-1,0)
    def sum_copy(self,way,j,u,first):
        sends,recvs=self.sum_sems
        dst=self.sums.at[way,j,self.span(u)]
        src=self.part.at[j,self.span(u)] if first else dst
        return remote(src,dst,sends.at[way,j,u],recvs.at[way,j,u],self._target(way))
    def send_sums(self,t):
        here,n=self.here,self.n
        for k in range(n-1):
            for way,j in ((0,n-1-k),(1,k)):
                u=t-here if way==0 else t-(n-1-here)
                ok=self.fits(u)
                u=jnp.clip(u,0,self.pieces-1)
                begins=(here==0) if way==0 else (here==n-1)
                passes=((here>0)&(here<j)) if way==0 else ((here<n-1)&(here>j))
                @pl.when(ok&begins)
                def _(): self.sum_copy(way,j,u,True).start()
                @pl.when(ok&passes)
                def _():
                    copy=self.sum_copy(way,j,u,False)
                    copy.wait_recv()
                    ref=self.sums.at[way,j,self.span(u)]
                    ref[...]=(ref[...].astype(F32)+self.part[j,self.span(u)].astype(F32)).astype(BF)
                    copy.start()
    def own_sum(self,u,total):
        here,n=self.here,self.n
        total[...]=self.part[here,self.span(u)].astype(F32)
        for way in (0,1):
            @pl.when(here>0 if way==0 else here<n-1)
            def _():
                self.sum_copy(way,here,u,False).wait_recv()
                total[...]+=self.sums[way,here,self.span(u)].astype(F32)
    def end_sums(self):
        here,n=self.here,self.n
        def one(u,_):
            for k in range(n-1):
                for way,j in ((0,n-1-k),(1,k)):
                    @pl.when((here<j) if way==0 else (here>j))
                    def _(): self.sum_copy(way,j,u,False).wait_send()
            return 0
        lax.fori_loop(0,self.pieces,one,0)
    def piece_copy(self,way,c,u,src=None):
        sends,recvs=self.held_sems
        dst=self.held.at[c,self.span(u)]
        return remote(dst if src is None else src,dst,sends.at[way,c,u],recvs.at[way,c,u],self._target(way))
    def send_own(self,u,src=None):
        here,n=self.here,self.n
        for way in (0,1):
            @pl.when(here<n-1 if way==0 else here>0)
            def _(): self.piece_copy(way,here,u,src).start()
    def pass_pieces(self,t):
        here,n=self.here,self.n
        for k in range(1,n):
            u=t-k
            ok=self.fits(u)
            u=jnp.clip(u,0,self.pieces-1)
            for way in (0,1):
                c=here-k if way==0 else here+k
                there=ok&((c>=0) if way==0 else (c<n))
                c=jnp.clip(c,0,n-1)
                @pl.when(there)
                def _(): self.piece_copy(way,c,u).wait_recv()
                @pl.when(there&(here<n-1 if way==0 else here>0))
                def _(): self.piece_copy(way,c,u).start()
    def end_pieces(self):
        here,n=self.here,self.n
        def one(u,_):
            for k in range(n):
                for way in (0,1):
                    c=here-k if way==0 else here+k
                    there=(c>=0) if way==0 else (c<n)
                    c=jnp.clip(c,0,n-1)
                    @pl.when(there&(here<n-1 if way==0 else here>0))
                    def _(): self.piece_copy(way,c,u).wait_send()
            return 0
        lax.fori_loop(0,self.pieces,one,0)

def turn_over(finish, count, pieces, n_in, n_out, gather, *refs):
    part=refs[0]; ins=refs[1:1+n_in]; outs=refs[1+n_in:1+n_in+n_out]
    rest=refs[1+n_in+n_out:]
    if gather:
        whole,sums,total,ss,sr,held,hs,hr,ws=rest
    else:
        sums,total,ss,sr=rest; held=hs=hr=None
    rows=part.shape[1]
    line=Line(count,pieces,rows,part,sums,(ss,sr),held,(hs,hr))
    greet(line.here,count)
    far=count-1
    def step(t,_):
        line.send_sums(t)
        if gather: line.pass_pieces(t-far)
        u=t-far
        @pl.when(line.fits(u))
        def _():
            line.own_sum(u,total)
            low=finish(line.span(u),total,ins,outs)
            if gather:
                held[line.here,line.span(u)]=low
                line.send_own(u)
        return 0
    lax.fori_loop(0,pieces+(2*far if gather else far),step,0)
    if gather:
        copy=pltpu.make_async_copy(held,whole,ws); copy.start()
    line.end_sums()
    if gather:
        line.end_pieces()
        copy.wait()

def sum_and_finish(part,ins,out_shapes,finish,gather,cid,pieces,tensor):
    n=tensor; rows=part.shape[0]//n; D=part.shape[1]
    vm=pl.BlockSpec(memory_space=pltpu.VMEM)
    outs=list(out_shapes); out_specs=[vm]*len(outs)
    scratch=[pltpu.VMEM((2,n,rows,D),BF),pltpu.VMEM((rows//pieces,D),F32),
        pltpu.SemaphoreType.DMA((2,n,pieces)),pltpu.SemaphoreType.DMA((2,n,pieces))]
    if gather:
        outs.append(jax.ShapeDtypeStruct((n,rows,D),BF)); out_specs.append(pl.BlockSpec(memory_space=pl.ANY))
        scratch+=[pltpu.VMEM((n,rows,D),BF),pltpu.SemaphoreType.DMA((2,n,pieces)),pltpu.SemaphoreType.DMA((2,n,pieces)),pltpu.SemaphoreType.DMA]
    res=pl.pallas_call(functools.partial(turn_over,finish,n,pieces,len(ins),len(out_shapes),gather),
        out_shape=tuple(outs),in_specs=[vm]*(1+len(ins)),out_specs=tuple(out_specs),scratch_shapes=scratch,
        cost_estimate=pl.CostEstimate(flops=0,bytes_accessed=270_000_000,transcendentals=0),
        compiler_params=pltpu.CompilerParams(collective_id=cid,has_side_effects=True,vmem_limit_bytes=56*1024*1024),
    )(part.reshape(n,rows,D),*ins)
    return res


def frequencies(head_size):
    inverse = 1.0 / 500000.0 ** (jnp.arange(head_size // 2, dtype=jnp.float32) * 2.0 / head_size)
    wavelength = 2.0 * math.pi / inverse
    smooth = (8192.0 / wavelength - 1.0) / 3.0
    blended = (1.0 - smooth) * inverse / 32.0 + smooth * inverse
    return jnp.where(
        wavelength > 8192.0, inverse / 32.0, jnp.where(wavelength < 2048.0, inverse, blended)
    )


def dot(left_side, right_side, left_dim, right_dim):
    return lax.dot_general(
        left_side, right_side, (((left_dim,), (right_dim,)), ((), ())), preferred_element_type=F32
    )


def norm_kernel(count, pieces, tokens_ref, gain_ref, whole, held, hs, hr, ws):
    line = Line(count, pieces, tokens_ref.shape[0], held=held, held_sems=(hs, hr))
    greet(line.here, count)

    def step(t, _):
        line.pass_pieces(t)
        u = jnp.clip(t, 0, pieces - 1)

        @pl.when(t < pieces)
        def _():
            stream = tokens_ref[line.span(u), :].astype(F32)
            scale = lax.rsqrt(jnp.mean(stream * stream, -1, keepdims=True) + EPSILON)
            held[line.here, line.span(u)] = (stream * scale * gain_ref[...]).astype(BF)
            line.send_own(u)

        return 0

    lax.fori_loop(0, pieces + count - 1, step, 0)
    copy = pltpu.make_async_copy(held, whole, ws)
    copy.start()
    line.end_pieces()
    copy.wait()


def norm_and_gather(tokens, gain, cid, pieces, count):
    rows, width = tokens.shape
    vm = pl.BlockSpec(memory_space=pltpu.VMEM)
    return pl.pallas_call(
        functools.partial(norm_kernel, count, pieces),
        out_shape=jax.ShapeDtypeStruct((count, rows, width), BF),
        in_specs=[vm, vm],
        out_specs=pl.BlockSpec(memory_space=pl.ANY),
        scratch_shapes=[
            pltpu.VMEM((count, rows, width), BF),
            pltpu.SemaphoreType.DMA((2, count, pieces)),
            pltpu.SemaphoreType.DMA((2, count, pieces)),
            pltpu.SemaphoreType.DMA,
        ],
        cost_estimate=pl.CostEstimate(flops=0, bytes_accessed=270_000_000, transcendentals=0),
        compiler_params=pltpu.CompilerParams(
            collective_id=cid, has_side_effects=True, vmem_limit_bytes=40 * 1024 * 1024
        ),
    )(tokens, gain).reshape(count * rows, width)


def finish_attention(span, total, ins, outs):
    tokens, gain = ins
    residual = total[...] + tokens[span, :].astype(F32)
    outs[0][span, :] = residual
    scale = lax.rsqrt(jnp.mean(residual * residual, -1, keepdims=True) + EPSILON)
    return (residual * scale * gain[...]).astype(BF)


def finish_residual(span, total, ins, outs):
    residual_ref, grad_out, gain, start = ins
    residual = residual_ref[span, :]
    scale = lax.rsqrt(jnp.mean(residual * residual, -1, keepdims=True) + EPSILON)
    unit = residual * scale
    grads = total[...]
    outs[1][span, :] = grads * unit
    scaled = grads * gain[...]
    grad_residual = grad_out[span, :].astype(F32) + scale * (
        scaled - unit * jnp.mean(scaled * unit, -1, keepdims=True)
    )
    outs[0][span, :] = grad_residual
    return grad_residual.astype(BF)


def finish_tokens(span, total, ins, outs):
    tokens, grad_residual, gain = ins
    stream = tokens[span, :].astype(F32)
    scale = lax.rsqrt(jnp.mean(stream * stream, -1, keepdims=True) + EPSILON)
    unit = stream * scale
    grads = total[...]
    outs[1][span, :] = grads * unit
    scaled = grads * gain[...]
    outs[0][span, :] = grad_residual[span, :] + scale * (
        scaled - unit * jnp.mean(scaled * unit, -1, keepdims=True)
    )


def ring_gather(piece, count):
    rows, width = piece.shape
    half = rows // 2
    here = lax.axis_index(AXIS)
    right = [(k, (k + 1) % count) for k in range(count)]
    left = [(k, (k - 1) % count) for k in range(count)]
    one, two = piece[:half], piece[half:]
    whole = jnp.zeros((count, rows, width), piece.dtype)
    whole = lax.dynamic_update_slice(whole, piece[None], (here, 0, 0))
    for step in range(1, count):
        one = lax.ppermute(one, AXIS, right)
        two = lax.ppermute(two, AXIS, left)
        whole = lax.dynamic_update_slice(whole, one[None], ((here - step) % count, 0, 0))
        whole = lax.dynamic_update_slice(whole, two[None], ((here + step) % count, half, 0))
    return whole.reshape(count * rows, width)


def ring_sum(part, count):
    width = part.shape[1]
    half = part.shape[0] // count // 2
    here = lax.axis_index(AXIS)
    right = [(k, (k + 1) % count) for k in range(count)]
    left = [(k, (k - 1) % count) for k in range(count)]
    cut = part.reshape(count, 2, half, width)

    def term(owner, side):
        return lax.dynamic_slice(cut, (owner % count, side, 0, 0), (1, 1, half, width))[0, 0]

    one, two = term(here - 1, 0), term(here + 1, 1)
    for step in range(1, count):
        one = lax.ppermute(one, AXIS, right)
        two = lax.ppermute(two, AXIS, left)
        last = step == count - 1
        one = one.astype(F32) + term(here - step - 1, 0).astype(F32)
        two = two.astype(F32) + term(here + step + 1, 1).astype(F32)
        if not last:
            one, two = one.astype(BF), two.astype(BF)
    return jnp.concatenate([one, two], 0)


def body(
    count,
    tokens,
    segments,
    positions,
    attn_gain,
    w_query,
    w_key,
    w_value,
    w_out,
    mlp_gain,
    w_gate,
    w_up,
    w_down,
    grad_out,
):
    rows, width = tokens.shape
    heads = w_query.shape[1] // HD
    groups = w_key.shape[1] // HD
    gains = lax.all_gather(jnp.stack([attn_gain, mlp_gain]).astype(F32), "dp", axis=1, tiled=True)
    gain_one, gain_two = gains[0:1], gains[1:2]
    mix = lax.all_gather(jnp.concatenate([w_query, w_key, w_value], 1), "dp", axis=0, tiled=True)
    full_out = lax.all_gather(w_out, "dp", axis=1, tiled=True)
    full_gate = lax.all_gather(w_gate, "dp", axis=0, tiled=True)
    full_up = lax.all_gather(w_up, "dp", axis=0, tiled=True)
    full_down = lax.all_gather(w_down, "dp", axis=1, tiled=True)

    normed_one = norm_and_gather(tokens, gain_one, 1, 4, count)
    angles = frequencies(HD)[:, None] * positions.astype(F32)[None, :]
    cosine, sine = jnp.cos(angles), jnp.sin(angles)
    lin = dot(mix, normed_one, 0, 1)
    mixed, lse, q, kt, k, vt, v = attend(lin, cosine, sine, segments, heads, groups)
    grad_late, normed_late = lax.optimization_barrier((grad_out, normed_one))
    grad_rows = ring_gather(grad_late, count)

    part = dot(mixed, full_out, 0, 0).astype(BF)
    residual, normed_two = sum_and_finish(
        part, (tokens, gain_two), (jax.ShapeDtypeStruct((rows, width), F32),),
        finish_attention, True, 2, 16, count,
    )
    normed_two = normed_two.reshape(count * rows, width)
    gate_values = dot(normed_two, full_gate, 1, 0)
    up_values = dot(normed_two, full_up, 1, 0)
    sigmoid_gate = jax.nn.sigmoid(gate_values)
    activated = gate_values * sigmoid_gate
    product = (activated * up_values).astype(BF)
    down = ring_sum(dot(product, full_down, 1, 0).astype(BF), count)
    block_out = (residual + down).astype(BF)
    grad_product = dot(grad_rows, full_down, 1, 1)
    grad_gated = (
        grad_product * up_values * sigmoid_gate * (1.0 + gate_values * (1.0 - sigmoid_gate))
    ).astype(BF)
    grad_lifted = (grad_product * activated).astype(BF)
    part = (dot(grad_gated, full_gate, 1, 1) + dot(grad_lifted, full_up, 1, 1)).astype(BF)
    grad_down = lax.psum_scatter(dot(product, grad_rows, 0, 0).astype(BF), "dp", scatter_dimension=1, tiled=True)
    grad_gate = lax.psum_scatter(dot(normed_two, grad_gated, 0, 0).astype(BF), "dp", scatter_dimension=0, tiled=True)
    grad_up = lax.psum_scatter(dot(normed_two, grad_lifted, 0, 0).astype(BF), "dp", scatter_dimension=0, tiled=True)
    wide = jax.ShapeDtypeStruct((rows, width), F32)
    grad_residual, terms_two, grad_low = sum_and_finish(
        part, (residual, grad_out, gain_two, gain_two), (wide, wide), finish_residual, True, 3, 16, count
    )
    grad_low = grad_low.reshape(count * rows, width)
    grad_mixed = dot(full_out, grad_low, 1, 1).astype(BF)
    grad_out_proj = lax.psum_scatter(dot(mixed, grad_low, 1, 0).astype(BF), "dp", scatter_dimension=1, tiled=True)
    turned = attend_back(q, kt, k, v, lse, grad_mixed, cosine, sine, segments, heads, groups)
    part = dot(turned, mix, 0, 1).astype(BF)
    grad_mix = lax.psum_scatter(dot(normed_one, turned, 0, 1).astype(BF), "dp", scatter_dimension=0, tiled=True)
    grad_tokens, terms_one = sum_and_finish(
        part, (tokens, grad_residual, gain_one), (wide, wide), finish_tokens, False, 4, 4, count
    )
    sums = lax.psum(jnp.stack([jnp.sum(terms_one, 0), jnp.sum(terms_two, 0)]), ("dp", AXIS))
    place = lax.axis_index("dp") * attn_gain.shape[0]
    sums = lax.dynamic_slice(sums, (0, place), (2, attn_gain.shape[0]))
    edges = (heads * HD, (heads + groups) * HD)
    grad_query, grad_key, grad_value = jnp.split(grad_mix.astype(F32), edges, 1)
    return (
        block_out,
        grad_tokens,
        sums[0],
        grad_query,
        grad_key,
        grad_value,
        grad_out_proj.astype(F32),
        sums[1],
        grad_gate.astype(F32),
        grad_up.astype(F32),
        grad_down.astype(F32),
    )


def solution(mesh):
    placed = (
        P(("dp", "tensor"), None),
        P("dp"),
        P("dp"),
        P("dp"),
        P("dp", "tensor"),
        P("dp", "tensor"),
        P("dp", "tensor"),
        P("tensor", "dp"),
        P("dp"),
        P("dp", "tensor"),
        P("dp", "tensor"),
        P("tensor", "dp"),
        P(("dp", "tensor"), None),
    )
    return jax.shard_map(
        functools.partial(body, mesh.shape["tensor"]),
        mesh=mesh,
        in_specs=placed,
        out_specs=(
            P(("dp", "tensor"), None),
            P(("dp", "tensor"), None),
            P("dp"),
            P("dp", "tensor"),
            P("dp", "tensor"),
            P("dp", "tensor"),
            P("tensor", "dp"),
            P("dp"),
            P("dp", "tensor"),
            P("dp", "tensor"),
            P("tensor", "dp"),
        ),
        check_vma=False,
    )
```

```python
import functools
import math

import jax
import jax.numpy as jnp
from jax import lax
from jax.experimental import pallas as pl
from jax.experimental.pallas import tpu as pltpu
from jax.sharding import PartitionSpec as P

HD = 64
EPSILON = 1e-05
MASKED = -1e30
F32 = jnp.float32
BF = jnp.bfloat16

def turn_t(values, cosine, sine, sign):
    half=values.shape[0]//2
    first, second = values[:half], values[half:]
    return jnp.concatenate([first*cosine - sign*second*sine, second*cosine + sign*first*sine],0)

def block_bias(segs_col, segs_row, start, block):
    keys=start+block
    key_places=lax.broadcasted_iota(jnp.int32,(keys,block),0)
    query_places=start+lax.broadcasted_iota(jnp.int32,(keys,block),1)
    allowed=(key_places<=query_places)&(segs_col[0:keys,:]==segs_row[0:1,start:start+block])
    return jnp.where(allowed,0.0,MASKED).astype(F32)

def attend_kernel(heads, groups, block, lin_ref, cos_ref, sin_ref, segc_ref, segr_ref,
                  mixed_ref, lse_ref, q_ref, kt_ref, k_ref, vt_ref, v_ref, bias_ref):
    length=lin_ref.shape[1]
    per=heads//groups
    cosine, sine = cos_ref[...], sin_ref[...]
    def rope(h,_):
        rows=pl.ds(pl.multiple_of(h*HD,HD),HD)
        q_ref[rows,:]=(turn_t(lin_ref[rows,:],cosine,sine,1.0).astype(BF)*jnp.asarray(0.125,BF))
        return 0
    lax.fori_loop(0,heads,rope,0)
    kv=groups*HD
    turned=[turn_t(lin_ref[(heads+g)*HD:(heads+g+1)*HD,:],cosine,sine,1.0) for g in range(groups)]
    keys_t=jnp.concatenate(turned,0)
    kt_ref[...]=keys_t.astype(BF)
    vals_t=lin_ref[(heads+groups)*HD:(heads+2*groups)*HD,:]
    vt_ref[...]=vals_t.astype(BF)
    keys_n=keys_t.T.astype(BF)
    vals_n=vals_t.T.astype(BF)
    for g in range(groups):
        k_ref[g]=keys_n[:,g*HD:(g+1)*HD]
        v_ref[g]=vals_n[:,g*HD:(g+1)*HD]
    for start in range(0,length,block):
        keys=start+block
        bias_ref[0:keys,:]=block_bias(segc_ref,segr_ref,start,block)
        def head(h,_):
            g=h//per
            rows=pl.ds(pl.multiple_of(h*HD,HD),HD)
            grows=pl.ds(pl.multiple_of(g*HD,HD),HD)
            scores=jnp.dot(k_ref[g,0:keys,:],q_ref[rows,start:start+block],preferred_element_type=F32)
            scores=scores+bias_ref[0:keys,:]
            top=jnp.max(scores,0,keepdims=True)
            weights=jnp.exp(scores-top)
            total=jnp.sum(weights,0,keepdims=True)
            out=jnp.dot(vt_ref[grows,0:keys],weights.astype(BF),preferred_element_type=F32)
            mixed_ref[rows,start:start+block]=(out/total).astype(BF)
            lse_ref[h,:,start:start+block]=top+jnp.log(total)
            return 0
        lax.fori_loop(0,heads,head,0)

def attend(lin, cosine, sine, segments, heads, groups):
    length=lin.shape[1]
    block=min(256,length)
    sds=jax.ShapeDtypeStruct
    vm=pl.BlockSpec(memory_space=pltpu.VMEM)
    return pl.pallas_call(functools.partial(attend_kernel,heads,groups,block),
        out_shape=(sds((heads*HD,length),BF),sds((heads,1,length),F32),sds((heads*HD,length),BF),
            sds((groups*HD,length),BF),sds((groups,length,HD),BF),sds((groups*HD,length),BF),sds((groups,length,HD),BF)),
        in_specs=[vm]*5,out_specs=(vm,)*7,
        scratch_shapes=[pltpu.VMEM((length,block),F32)],
        cost_estimate=pl.CostEstimate(flops=30_000_000_000,bytes_accessed=10_000_000,transcendentals=8_000_000),
        compiler_params=pltpu.CompilerParams(vmem_limit_bytes=48*1024*1024),
    )(lin,cosine,sine,segments.reshape(length,1),segments.reshape(1,length))

def attend_back_kernel(heads, groups, block, q_ref, kt_ref, k_ref, v_ref, lse_ref, gm_ref, cos_ref, sin_ref, segc_ref, segr_ref,
                  out_ref, bias_ref, qn_ref, gn_ref, dq_ref, dk_ref, dv_ref):
    length=q_ref.shape[1]
    per=heads//groups
    cosine, sine = cos_ref[...], sin_ref[...]
    def flip(p,_):
        rows=pl.ds(pl.multiple_of(p*2*HD,2*HD),2*HD)
        qn=q_ref[rows,:].astype(F32).T.astype(BF)
        gn=gm_ref[rows,:].astype(F32).T.astype(BF)
        qn_ref[2*p]=qn[:,:HD]
        qn_ref[2*p+1]=qn[:,HD:]
        gn_ref[2*p]=gn[:,:HD]
        gn_ref[2*p+1]=gn[:,HD:]
        return 0
    lax.fori_loop(0,heads//2,flip,0)
    dk_ref[...]=jnp.zeros_like(dk_ref)
    dv_ref[...]=jnp.zeros_like(dv_ref)
    for start in range(0,length,block):
        keys=start+block
        cols=slice(start,start+block)
        bias_ref[0:keys,:]=block_bias(segc_ref,segr_ref,start,block)
        def head(h,_):
            g=h//per
            rows=pl.ds(pl.multiple_of(h*HD,HD),HD)
            grows=pl.ds(pl.multiple_of(g*HD,HD),HD)
            scores=jnp.dot(k_ref[g,0:keys,:],q_ref[rows,cols],preferred_element_type=F32)
            probs=jnp.exp(scores+bias_ref[0:keys,:]-lse_ref[h,:,cols])
            dv_ref[g,0:keys,:]+=jnp.dot(probs.astype(BF),gn_ref[h,cols,:],preferred_element_type=F32)
            gp=jnp.dot(v_ref[g,0:keys,:],gm_ref[rows,cols],preferred_element_type=F32)
            weighted=probs*gp
            centre=jnp.sum(weighted,0,keepdims=True)
            gs=(weighted-probs*centre).astype(BF)
            dk_ref[g,0:keys,:]+=jnp.dot(gs,qn_ref[h,cols,:],preferred_element_type=F32)
            dq_ref[rows,cols]=0.125*jnp.dot(kt_ref[grows,0:keys],gs,preferred_element_type=F32)
            return 0
        lax.fori_loop(0,heads,head,0)
    def back(h,_):
        rows=pl.ds(pl.multiple_of(h*HD,HD),HD)
        out_ref[rows,:]=turn_t(dq_ref[rows,:],cosine,sine,-1.0).astype(BF)
        return 0
    lax.fori_loop(0,heads,back,0)
    dk=jnp.concatenate([dk_ref[g] for g in range(groups)],1).T
    dv=jnp.concatenate([dv_ref[g] for g in range(groups)],1).T
    for g in range(groups):
        out_ref[(heads+g)*HD:(heads+g+1)*HD,:]=turn_t(dk[g*HD:(g+1)*HD],cosine,sine,-1.0).astype(BF)
    out_ref[(heads+groups)*HD:,:]=dv.astype(BF)

def attend_back(q,kt,k,v,lse,gm,cosine,sine,segments,heads,groups):
    length=q.shape[1]
    block=min(256,length)
    vm=pl.BlockSpec(memory_space=pltpu.VMEM)
    return pl.pallas_call(functools.partial(attend_back_kernel,heads,groups,block),
        out_shape=jax.ShapeDtypeStruct(((heads+2*groups)*HD,length),BF),
        in_specs=[vm]*10,out_specs=vm,
        scratch_shapes=[pltpu.VMEM((length,block),F32),pltpu.VMEM((heads,length,HD),BF),pltpu.VMEM((heads,length,HD),BF),
            pltpu.VMEM((heads*HD,length),F32),pltpu.VMEM((groups,length,HD),F32),pltpu.VMEM((groups,length,HD),F32)],
        cost_estimate=pl.CostEstimate(flops=60_000_000_000,bytes_accessed=10_000_000,transcendentals=8_000_000),
        compiler_params=pltpu.CompilerParams(vmem_limit_bytes=48*1024*1024),
    )(q,kt,k,v,lse,gm,cosine,sine,segments.reshape(length,1),segments.reshape(1,length))


AXIS="tensor"
DP="dp"
MESH=pl.DeviceIdType.MESH

def greet(here, count, plane=0):
    barrier=pltpu.get_barrier_semaphore()
    if plane:
        def call(k,_):
            pl.semaphore_signal(barrier,inc=1,device_id={DP:lax.rem(lax.axis_index(DP)+k,plane)},device_id_type=MESH)
            return 0
        lax.fori_loop(1,plane,call,0)
        for k in range(1,count):
            pl.semaphore_signal(barrier,inc=1,device_id={AXIS:lax.rem(here+k,count)},device_id_type=MESH)
        pl.semaphore_wait(barrier,plane+count-2)
    else:
        @pl.when(here>0)
        def _(): pl.semaphore_signal(barrier,inc=1,device_id={AXIS:here-1},device_id_type=MESH)
        @pl.when(here<count-1)
        def _(): pl.semaphore_signal(barrier,inc=1,device_id={AXIS:here+1},device_id_type=MESH)
        pl.semaphore_wait(barrier,jnp.where((here>0)&(here<count-1),2,1))

def swap(axis, count, source, landing, sends, recvs):
    me=lax.axis_index(axis)
    def copy(peer, slot, k):
        return pltpu.make_async_remote_copy(src_ref=source(peer),dst_ref=landing.at[slot],send_sem=sends.at[k],
            recv_sem=recvs.at[slot],device_id={axis:peer},device_id_type=MESH)
    def begin(k,_):
        copy(lax.rem(me+k,count),me,k).start()
        return 0
    def end(k,_):
        peer=lax.rem(me+k,count)
        copy(peer,peer,k).wait_recv()
        copy(peer,me,k).wait_send()
        return 0
    return (lambda: lax.fori_loop(1,count,begin,0)),(lambda: lax.fori_loop(1,count,end,0))

def remote(src,dst,send,recv,target):
    return pltpu.make_async_remote_copy(src_ref=src,dst_ref=dst,send_sem=send,recv_sem=recv,
        device_id={AXIS:target},device_id_type=MESH)

class Line:
    def __init__(self,count,pieces,rows,part=None,sums=None,sum_sems=None,held=None,held_sems=None):
        self.n,self.pieces,self.rows=count,pieces,rows
        self.sub=rows//pieces
        self.here=lax.axis_index(AXIS)
        self.part,self.sums,self.sum_sems=part,sums,sum_sems
        self.held,self.held_sems=held,held_sems
    def span(self,u): return pl.ds(pl.multiple_of(u*self.sub,self.sub),self.sub)
    def fits(self,u): return (u>=0)&(u<self.pieces)
    def _target(self,way):
        return lax.min(self.here+1,self.n-1) if way==0 else lax.max(self.here-1,0)
    def sum_copy(self,way,j,u,first):
        sends,recvs=self.sum_sems
        dst=self.sums.at[way,j,self.span(u)]
        src=self.part.at[j,self.span(u)] if first else dst
        return remote(src,dst,sends.at[way,j,u],recvs.at[way,j,u],self._target(way))
    def send_sums(self,t):
        here,n=self.here,self.n
        for k in range(n-1):
            for way,j in ((0,n-1-k),(1,k)):
                u=t-here if way==0 else t-(n-1-here)
                ok=self.fits(u)
                u=jnp.clip(u,0,self.pieces-1)
                begins=(here==0) if way==0 else (here==n-1)
                passes=((here>0)&(here<j)) if way==0 else ((here<n-1)&(here>j))
                @pl.when(ok&begins)
                def _(): self.sum_copy(way,j,u,True).start()
                @pl.when(ok&passes)
                def _():
                    copy=self.sum_copy(way,j,u,False)
                    copy.wait_recv()
                    ref=self.sums.at[way,j,self.span(u)]
                    ref[...]=(ref[...].astype(F32)+self.part[j,self.span(u)].astype(F32)).astype(BF)
                    copy.start()
    def own_sum(self,u,total):
        here,n=self.here,self.n
        total[...]=self.part[here,self.span(u)].astype(F32)
        for way in (0,1):
            @pl.when(here>0 if way==0 else here<n-1)
            def _():
                self.sum_copy(way,here,u,False).wait_recv()
                total[...]+=self.sums[way,here,self.span(u)].astype(F32)
    def end_sums(self):
        here,n=self.here,self.n
        def one(u,_):
            for k in range(n-1):
                for way,j in ((0,n-1-k),(1,k)):
                    @pl.when((here<j) if way==0 else (here>j))
                    def _(): self.sum_copy(way,j,u,False).wait_send()
            return 0
        lax.fori_loop(0,self.pieces,one,0)
    def piece_copy(self,way,c,u,src=None):
        sends,recvs=self.held_sems
        dst=self.held.at[c,self.span(u)]
        return remote(dst if src is None else src,dst,sends.at[way,c,u],recvs.at[way,c,u],self._target(way))
    def send_own(self,u,src=None):
        here,n=self.here,self.n
        for way in (0,1):
            @pl.when(here<n-1 if way==0 else here>0)
            def _(): self.piece_copy(way,here,u,src).start()
    def pass_pieces(self,t):
        here,n=self.here,self.n
        for k in range(1,n):
            u=t-k
            ok=self.fits(u)
            u=jnp.clip(u,0,self.pieces-1)
            for way in (0,1):
                c=here-k if way==0 else here+k
                there=ok&((c>=0) if way==0 else (c<n))
                c=jnp.clip(c,0,n-1)
                @pl.when(there)
                def _(): self.piece_copy(way,c,u).wait_recv()
                @pl.when(there&(here<n-1 if way==0 else here>0))
                def _(): self.piece_copy(way,c,u).start()
    def end_pieces(self):
        here,n=self.here,self.n
        def one(u,_):
            for k in range(n):
                for way in (0,1):
                    c=here-k if way==0 else here+k
                    there=(c>=0) if way==0 else (c<n)
                    c=jnp.clip(c,0,n-1)
                    @pl.when(there&(here<n-1 if way==0 else here>0))
                    def _(): self.piece_copy(way,c,u).wait_send()
            return 0
        lax.fori_loop(0,self.pieces,one,0)

def turn_over(finish, count, plane, pieces, n_in, n_out, gather, share, *refs):
    part,other=refs[:2]; ins=refs[2:2+n_in]; outs=refs[2+n_in:2+n_in+n_out]
    rest=list(refs[2+n_in+n_out:])
    acc_out=rest.pop(0)
    whole=rest.pop(0) if gather else None
    sums,total,ss,sr,acc=rest[:5]; rest=rest[5:]
    held=hs=hr=None
    if gather: held,hs,hr,ws=rest[:4]; rest=rest[4:]
    if share: cut,landed,level,stacked,ds,dr,zs,zr=rest
    rows=part.shape[1]
    line=Line(count,pieces,rows,part,sums,(ss,sr),held,(hs,hr))
    greet(line.here,count,plane if share else 0)
    far=count-1
    acc[...]=jnp.zeros_like(acc)
    width=part.shape[2]
    def terms(t):
        def some(k,_):
            span=pl.ds(pl.multiple_of(k*16,16),16)
            both=part[t,span].astype(F32)*other[t,span].astype(F32)
            acc[...]+=both[:8]+both[8:]
            return 0
        lax.fori_loop(0,rows//16,some,0)
    if share:
        me=lax.axis_index(DP)
        piece=width//plane
        begin_dp,end_dp=swap(DP,plane,lambda p: cut.at[p],landed,ds,dr)
        begin_z,end_z=swap(AXIS,count,lambda p: level,stacked,zs,zr)
    def step(t,_):
        line.send_sums(t)
        if gather: line.pass_pieces(t-far)
        u=t-far
        @pl.when(line.fits(u))
        def _():
            line.own_sum(u,total)
            low=finish(line.span(u),total,ins,outs)
            if gather:
                held[line.here,line.span(u)]=low
                line.send_own(u)
        @pl.when(t<count)
        def _(): terms(jnp.clip(t,0,count-1))
        if share:
            @pl.when(t==count-1)
            def _():
                for p in range(plane):
                    cut[p,0:8,:]=acc[:,p*piece:(p+1)*piece]
                    cut[p,8:16,:]=ins[-1][:,p*piece:(p+1)*piece]
                landed[me]=cut[me]
                begin_dp()
            @pl.when(t==count)
            def _():
                end_dp()
                level[...]=jnp.sum(landed[...],0)
                stacked[line.here]=level[...]
                begin_z()
        return 0
    steps=pieces+(2*far if gather else far)
    lax.fori_loop(0,steps,step,0)
    if gather:
        copy=pltpu.make_async_copy(held,whole,ws); copy.start()
    if share:
        end_z()
        acc_out[...]=jnp.sum(stacked[...],0)
    else:
        acc_out[...]=acc[...]
    line.end_sums()
    if gather:
        line.end_pieces()
        copy.wait()

def sum_and_finish(part,other,ins,out_shapes,finish,gather,share,cid,pieces,tensor,plane):
    n=tensor; rows=part.shape[0]//n; D=part.shape[1]
    assert pieces>=2
    vm=pl.BlockSpec(memory_space=pltpu.VMEM)
    outs=list(out_shapes); out_specs=[vm]*len(outs)
    sds=jax.ShapeDtypeStruct
    outs.append(sds((16,D//plane) if share else (8,D),F32)); out_specs.append(vm)
    sem=pltpu.SemaphoreType.DMA
    scratch=[pltpu.VMEM((2,n,rows,D),BF),pltpu.VMEM((rows//pieces,D),F32),sem((2,n,pieces)),sem((2,n,pieces)),pltpu.VMEM((8,D),F32)]
    if gather:
        outs.append(sds((n,rows,D),BF)); out_specs.append(pl.BlockSpec(memory_space=pl.ANY))
        scratch+=[pltpu.VMEM((n,rows,D),BF),sem((2,n,pieces)),sem((2,n,pieces)),sem]
    if share:
        w=D//plane
        scratch+=[pltpu.VMEM((plane,16,w),F32),pltpu.VMEM((plane,16,w),F32),pltpu.VMEM((16,w),F32),pltpu.VMEM((n,16,w),F32),
            sem((plane,)),sem((plane,)),sem((n,)),sem((n,))]
    res=pl.pallas_call(functools.partial(turn_over,finish,n,plane,pieces,len(ins),len(out_shapes),gather,share),
        out_shape=tuple(outs),in_specs=[vm]*(2+len(ins)),out_specs=tuple(out_specs),scratch_shapes=scratch,
        cost_estimate=pl.CostEstimate(flops=0,bytes_accessed=270_000_000,transcendentals=0),
        compiler_params=pltpu.CompilerParams(collective_id=cid,has_side_effects=True,vmem_limit_bytes=56*1024*1024),
    )(part.reshape(n,rows,D),other.reshape(n,rows,D),*ins)
    return res


def frequencies(head_size):
    inverse = 1.0 / 500000.0 ** (jnp.arange(head_size // 2, dtype=jnp.float32) * 2.0 / head_size)
    wavelength = 2.0 * math.pi / inverse
    smooth = (8192.0 / wavelength - 1.0) / 3.0
    blended = (1.0 - smooth) * inverse / 32.0 + smooth * inverse
    return jnp.where(
        wavelength > 8192.0, inverse / 32.0, jnp.where(wavelength < 2048.0, inverse, blended)
    )


def dot(left_side, right_side, left_dim, right_dim):
    return lax.dot_general(
        left_side, right_side, (((left_dim,), (right_dim,)), ((), ())), preferred_element_type=F32
    )


def norm_kernel(count, plane, pieces, tokens_ref, gains_ref, whole, gains_out, held, landed, hs, hr, ws, ds, dr):
    line = Line(count, pieces, tokens_ref.shape[0], held=held, held_sems=(hs, hr))
    greet(line.here, count, plane)
    me = lax.axis_index(DP)
    landed[me] = gains_ref[...]
    begin, end = swap(DP, plane, lambda p: gains_ref, landed, ds, dr)
    begin()
    end()
    piece = gains_ref.shape[1]
    for p in range(plane):
        gains_out[:, p * piece : (p + 1) * piece] = landed[p]

    def step(t, _):
        line.pass_pieces(t)
        u = jnp.clip(t, 0, pieces - 1)

        @pl.when(t < pieces)
        def _():
            stream = tokens_ref[line.span(u), :].astype(F32)
            scale = lax.rsqrt(jnp.mean(stream * stream, -1, keepdims=True) + EPSILON)
            held[line.here, line.span(u)] = (stream * scale * gains_out[0:1, :]).astype(BF)
            line.send_own(u)

        return 0

    lax.fori_loop(0, pieces + count - 1, step, 0)
    copy = pltpu.make_async_copy(held, whole, ws)
    copy.start()
    line.end_pieces()
    copy.wait()


def norm_and_gather(tokens, gains, cid, pieces, count, plane):
    rows, width = tokens.shape
    vm = pl.BlockSpec(memory_space=pltpu.VMEM)
    sem = pltpu.SemaphoreType.DMA
    normed, gains = pl.pallas_call(
        functools.partial(norm_kernel, count, plane, pieces),
        out_shape=(jax.ShapeDtypeStruct((count, rows, width), BF), jax.ShapeDtypeStruct((8, width), F32)),
        in_specs=[vm, vm],
        out_specs=(pl.BlockSpec(memory_space=pl.ANY), vm),
        scratch_shapes=[
            pltpu.VMEM((count, rows, width), BF),
            pltpu.VMEM((plane, 8, width // plane), F32),
            sem((2, count, pieces)),
            sem((2, count, pieces)),
            sem,
            sem((plane,)),
            sem((plane,)),
        ],
        cost_estimate=pl.CostEstimate(flops=0, bytes_accessed=270_000_000, transcendentals=0),
        compiler_params=pltpu.CompilerParams(
            collective_id=cid, has_side_effects=True, vmem_limit_bytes=40 * 1024 * 1024
        ),
    )(tokens, gains)
    return normed.reshape(count * rows, width), gains


def finish_attention(span, total, ins, outs):
    tokens, gain = ins
    residual = total[...] + tokens[span, :].astype(F32)
    outs[0][span, :] = residual
    scale = lax.rsqrt(jnp.mean(residual * residual, -1, keepdims=True) + EPSILON)
    return (residual * scale * gain[...]).astype(BF)


def finish_residual(span, total, ins, outs):
    residual_ref, grad_out, gain = ins
    residual = residual_ref[span, :]
    scale = lax.rsqrt(jnp.mean(residual * residual, -1, keepdims=True) + EPSILON)
    unit = residual * scale
    grads = total[...]
    scaled = grads * gain[...]
    grad_residual = grad_out[span, :].astype(F32) + scale * (
        scaled - unit * jnp.mean(scaled * unit, -1, keepdims=True)
    )
    outs[0][span, :] = grad_residual
    return grad_residual.astype(BF)


def finish_tokens(span, total, ins, outs):
    tokens, grad_residual, gain, _ = ins
    stream = tokens[span, :].astype(F32)
    scale = lax.rsqrt(jnp.mean(stream * stream, -1, keepdims=True) + EPSILON)
    unit = stream * scale
    grads = total[...]
    scaled = grads * gain[...]
    outs[0][span, :] = grad_residual[span, :] + scale * (
        scaled - unit * jnp.mean(scaled * unit, -1, keepdims=True)
    )


def ways(count):
    return [(k, (k + 1) % count) for k in range(count)], [(k, (k - 1) % count) for k in range(count)]


def both_ways(one, two, count):
    right, left = ways(count)
    return lax.ppermute(one, AXIS, right), lax.ppermute(two, AXIS, left)


def body(
    count,
    plane,
    tokens,
    segments,
    positions,
    attn_gain,
    w_query,
    w_key,
    w_value,
    w_out,
    mlp_gain,
    w_gate,
    w_up,
    w_down,
    grad_out,
):
    rows, width = tokens.shape
    half = rows // 2
    here = lax.axis_index(AXIS)
    heads = w_query.shape[1] // HD
    groups = w_key.shape[1] // HD
    after = lax.optimization_barrier
    mix = lax.all_gather(jnp.concatenate([w_query, w_key, w_value], 1), DP, axis=0, tiled=True)
    full_out = lax.all_gather(w_out, DP, axis=1, tiled=True)
    full_gate = lax.all_gather(w_gate, DP, axis=0, tiled=True)
    full_up = lax.all_gather(w_up, DP, axis=0, tiled=True)
    full_down = lax.all_gather(w_down, DP, axis=1, tiled=True)
    gains = jnp.concatenate([jnp.stack([attn_gain, mlp_gain]).astype(F32), jnp.zeros((6, attn_gain.shape[0]), F32)])

    normed_one, gains = norm_and_gather(tokens, gains, 1, 4, count, plane)
    gain_one, gain_two = gains[0:1], gains[1:2]
    angles = frequencies(HD)[:, None] * positions.astype(F32)[None, :]
    cosine, sine = jnp.cos(angles), jnp.sin(angles)

    grad_rows = jnp.zeros((count, rows, width), BF)
    grad_rows = lax.dynamic_update_slice(grad_rows, grad_out[None], (here, 0, 0))

    def place(whole, one, two, step):
        whole = lax.dynamic_update_slice(whole, one[None], ((here - step) % count, 0, 0))
        return lax.dynamic_update_slice(whole, two[None], ((here + step) % count, half, 0))

    one, two, normed_one = after((grad_out[:half], grad_out[half:], normed_one))
    one, two = both_ways(one, two, count)
    lin = dot(mix, normed_one, 0, 1)
    mixed, lse, q, kt, k, vt, v = attend(lin, cosine, sine, segments, heads, groups)
    one, two, mixed = after((one, two, mixed))
    part = dot(mixed, full_out, 0, 0).astype(BF)
    residual, _, normed_two = sum_and_finish(
        part, part, (tokens, gain_two), (jax.ShapeDtypeStruct((rows, width), F32),),
        finish_attention, True, False, 2, 16, count, plane,
    )
    normed_two = normed_two.reshape(count * rows, width)
    for step in range(1, count - 1):
        grad_rows = place(grad_rows, one, two, step)
        one, two, normed_two = after((one, two, normed_two))
        one, two = both_ways(one, two, count)
        if step == 1:
            gate_values = dot(normed_two, full_gate, 1, 0)
            up_values = dot(normed_two, full_up, 1, 0)
            one, two, gate_values, up_values = after((one, two, gate_values, up_values))
    sigmoid_gate = jax.nn.sigmoid(gate_values)
    activated = gate_values * sigmoid_gate
    product = (activated * up_values).astype(BF)
    down = dot(product, full_down, 1, 0).astype(BF)
    one, two, down = after((one, two, down))
    grad_rows = place(grad_rows, one, two, count - 1).reshape(count * rows, width)

    cut = down.reshape(count, 2, half, width)

    def term(owner, side):
        return lax.dynamic_slice(cut, (owner % count, side, 0, 0), (1, 1, half, width))[0, 0].astype(F32)

    def add_terms(one, two, step):
        return one.astype(F32) + term(here - step - 1, 0), two.astype(F32) + term(here + step + 1, 1)

    one, two = both_ways(term(here - 1, 0).astype(BF), term(here + 1, 1).astype(BF), count)
    grad_product = dot(grad_rows, full_down, 1, 1)
    grad_gated = (
        grad_product * up_values * sigmoid_gate * (1.0 + gate_values * (1.0 - sigmoid_gate))
    ).astype(BF)
    grad_lifted = (grad_product * activated).astype(BF)
    one, two, grad_gated, grad_lifted = after((one, two, grad_gated, grad_lifted))
    one, two = add_terms(one, two, 1)
    one, two = both_ways(one.astype(BF), two.astype(BF), count)
    grad_down = dot(product, grad_rows, 0, 0).astype(BF)
    grad_down, grad_gated, grad_lifted = after((grad_down, grad_gated, grad_lifted))
    grad_down = lax.psum_scatter(grad_down, DP, scatter_dimension=1, tiled=True)
    grad_gate = dot(normed_two, grad_gated, 0, 0).astype(BF)
    grad_up = dot(normed_two, grad_lifted, 0, 0).astype(BF)
    grad_gate, grad_up, grad_gated, grad_lifted = after((grad_gate, grad_up, grad_gated, grad_lifted))
    grad_gate = lax.psum_scatter(grad_gate, DP, scatter_dimension=0, tiled=True)
    grad_up = lax.psum_scatter(grad_up, DP, scatter_dimension=0, tiled=True)
    part = (dot(grad_gated, full_gate, 1, 1) + dot(grad_lifted, full_up, 1, 1)).astype(BF)
    one, two, part = after((one, two, part))
    one, two = add_terms(one, two, 2)
    wide = jax.ShapeDtypeStruct((rows, width), F32)
    grad_residual, terms_two, grad_low = sum_and_finish(
        part, normed_two, (residual, grad_out, gain_two), (wide,), finish_residual, True, False, 3, 16, count, plane
    )
    for step in range(3, count - 1):
        one, two = both_ways(one.astype(BF), two.astype(BF), count)
        one, two = add_terms(one, two, step)
    grad_low = grad_low.reshape(count * rows, width)
    one, two, grad_low, grad_down, grad_gate = after((one.astype(BF), two.astype(BF), grad_low, grad_down, grad_gate))
    one, two = both_ways(one, two, count)
    grad_mixed = dot(full_out, grad_low, 1, 1).astype(BF)
    grad_out_proj = lax.psum_scatter(dot(mixed, grad_low, 1, 0).astype(BF), DP, scatter_dimension=1, tiled=True)
    turned = attend_back(q, kt, k, v, lse, grad_mixed, cosine, sine, segments, heads, groups)
    grad_mix = dot(normed_one, turned, 0, 1).astype(BF)
    one, two, turned, grad_mix = after((one, two, turned, grad_mix))
    grad_mix = lax.psum_scatter(grad_mix, DP, scatter_dimension=0, tiled=True)
    one, two = add_terms(one, two, count - 1)
    block_out = (residual + jnp.concatenate([one, two], 0)).astype(BF)
    part = dot(turned, mix, 0, 1).astype(BF)
    part, grad_up = after((part, grad_up))
    grad_tokens, sums = sum_and_finish(
        part, normed_one, (tokens, grad_residual, gain_one, terms_two), (wide,), finish_tokens, False, True, 4, 4, count, plane
    )
    sums = jnp.sum(sums.reshape(2, 8, -1), 1)
    edges = (heads * HD, (heads + groups) * HD)
    grad_query, grad_key, grad_value = jnp.split(grad_mix.astype(F32), edges, 1)
    return (
        block_out,
        grad_tokens,
        sums[0] / attn_gain.astype(F32),
        grad_query,
        grad_key,
        grad_value,
        grad_out_proj.astype(F32),
        sums[1] / mlp_gain.astype(F32),
        grad_gate.astype(F32),
        grad_up.astype(F32),
        grad_down.astype(F32),
    )


def solution(mesh):
    placed = (
        P(("dp", "tensor"), None),
        P("dp"),
        P("dp"),
        P("dp"),
        P("dp", "tensor"),
        P("dp", "tensor"),
        P("dp", "tensor"),
        P("tensor", "dp"),
        P("dp"),
        P("dp", "tensor"),
        P("dp", "tensor"),
        P("tensor", "dp"),
        P(("dp", "tensor"), None),
    )
    return jax.shard_map(
        functools.partial(body, mesh.shape["tensor"], mesh.shape["dp"]),
        mesh=mesh,
        in_specs=placed,
        out_specs=(
            P(("dp", "tensor"), None),
            P(("dp", "tensor"), None),
            P("dp"),
            P("dp", "tensor"),
            P("dp", "tensor"),
            P("dp", "tensor"),
            P("tensor", "dp"),
            P("dp"),
            P("dp", "tensor"),
            P("dp", "tensor"),
            P("tensor", "dp"),
        ),
        check_vma=False,
    )
```

```python
import functools
import math

import jax
import jax.numpy as jnp
from jax import lax
from jax.experimental import pallas as pl
from jax.experimental.pallas import tpu as pltpu
from jax.sharding import PartitionSpec as P

HD = 64
EPSILON = 1e-05
MASKED = -1e30
F32 = jnp.float32
BF = jnp.bfloat16

def turn_t(values, cosine, sine, sign):
    half=values.shape[0]//2
    first, second = values[:half], values[half:]
    return jnp.concatenate([first*cosine - sign*second*sine, second*cosine + sign*first*sine],0)

def block_bias(segs_col, segs_row, start, block):
    keys=start+block
    key_places=lax.broadcasted_iota(jnp.int32,(keys,block),0)
    query_places=start+lax.broadcasted_iota(jnp.int32,(keys,block),1)
    allowed=(key_places<=query_places)&(segs_col[0:keys,:]==segs_row[0:1,start:start+block])
    return jnp.where(allowed,0.0,MASKED).astype(F32)

def attend_kernel(heads, groups, block, count, pieces, mix_ref, normed_ref, cos_ref, sin_ref, segc_ref, segr_ref, wo_ref, grad_ref,
                  mixed_ref, lse_ref, q_ref, kt_ref, k_ref, vt_ref, v_ref, part_ref, rows_hbm,
                  lin_ref, bias_ref, held, hs, hr, cs):
    length=normed_ref.shape[0]
    per=heads//groups
    rows=grad_ref.shape[0]
    line=Line(count,pieces,rows,held=held,held_sems=(hs,hr),sub=rows//(2*pieces))
    greet(line.here,count)
    for u in range(pieces):
        line.send_own(u,grad_ref.at[line.span(u),:])
    lines=mix_ref.shape[0]
    cut=256 if lines%256==0 else lines
    def project(c,_):
        some=pl.ds(pl.multiple_of(c*cut,cut),cut)
        lin_ref[some,:]=lax.dot_general(mix_ref[some,:],normed_ref[...],(((1,),(1,)),((),())),preferred_element_type=F32)
        return 0
    lax.fori_loop(0,lines//cut,project,0)
    cosine, sine = cos_ref[...], sin_ref[...]
    def rope(h,_):
        rows=pl.ds(pl.multiple_of(h*HD,HD),HD)
        q_ref[rows,:]=(turn_t(lin_ref[rows,:],cosine,sine,1.0).astype(BF)*jnp.asarray(0.125,BF))
        return 0
    lax.fori_loop(0,heads,rope,0)
    turned=[turn_t(lin_ref[(heads+g)*HD:(heads+g+1)*HD,:],cosine,sine,1.0) for g in range(groups)]
    keys_t=jnp.concatenate(turned,0)
    kt_ref[...]=keys_t.astype(BF)
    vals_t=lin_ref[(heads+groups)*HD:(heads+2*groups)*HD,:]
    vt_ref[...]=vals_t.astype(BF)
    keys_n=keys_t.T.astype(BF)
    vals_n=vals_t.T.astype(BF)
    for g in range(groups):
        k_ref[g]=keys_n[:,g*HD:(g+1)*HD]
        v_ref[g]=vals_n[:,g*HD:(g+1)*HD]
    done=0
    steps=pieces+count-1
    for start in range(0,length,block):
        keys=start+block
        if done<steps-2:
            done+=1
            line.pass_pieces(done)
        bias_ref[0:keys,:]=block_bias(segc_ref,segr_ref,start,block)
        def head(h,_):
            g=h//per
            rows=pl.ds(pl.multiple_of(h*HD,HD),HD)
            grows=pl.ds(pl.multiple_of(g*HD,HD),HD)
            scores=jnp.dot(k_ref[g,0:keys,:],q_ref[rows,start:start+block],preferred_element_type=F32)
            scores=scores+bias_ref[0:keys,:]
            top=jnp.max(scores,0,keepdims=True)
            weights=jnp.exp(scores-top)
            total=jnp.sum(weights,0,keepdims=True)
            out=jnp.dot(vt_ref[grows,0:keys],weights.astype(BF),preferred_element_type=F32)
            mixed_ref[rows,start:start+block]=(out/total).astype(BF)
            lse_ref[h,:,start:start+block]=top+jnp.log(total)
            return 0
        lax.fori_loop(0,heads,head,0)
    width=wo_ref.shape[1]
    wide=min(512,width)
    def out(c,_):
        cols=pl.ds(pl.multiple_of(c*wide,wide),wide)
        part_ref[:,cols]=lax.dot_general(mixed_ref[...],wo_ref[:,cols],(((0,),(0,)),((),())),preferred_element_type=F32).astype(BF)
        return 0
    lax.fori_loop(0,width//wide,out,0)
    for t in range(done+1,steps):
        line.pass_pieces(t)
    half=rows//2
    held[line.here,0:half]=grad_ref[0:half,:]
    copy=pltpu.make_async_copy(held,rows_hbm,cs)
    copy.start()
    line.end_pieces()
    copy.wait()

def attend(mix, normed, cosine, sine, segments, w_out, grad_out, heads, groups, cid, pieces, count):
    length,width=normed.shape
    rows=grad_out.shape[0]
    block=min(256,length)
    sds=jax.ShapeDtypeStruct
    vm=pl.BlockSpec(memory_space=pltpu.VMEM)
    sem=pltpu.SemaphoreType.DMA
    return pl.pallas_call(functools.partial(attend_kernel,heads,groups,block,count,pieces),
        out_shape=(sds((heads*HD,length),BF),sds((heads,1,length),F32),sds((heads*HD,length),BF),
            sds((groups*HD,length),BF),sds((groups,length,HD),BF),sds((groups*HD,length),BF),sds((groups,length,HD),BF),
            sds((length,width),BF),sds((count,rows//2,width),BF)),
        in_specs=[vm]*8,out_specs=(vm,)*8+(pl.BlockSpec(memory_space=pl.ANY),),
        scratch_shapes=[pltpu.VMEM((mix.shape[0],length),F32),pltpu.VMEM((length,block),F32),pltpu.VMEM((count,rows//2,width),BF),
            sem((2,count,pieces)),sem((2,count,pieces)),sem],
        cost_estimate=pl.CostEstimate(flops=30_000_000_000,bytes_accessed=130_000_000,transcendentals=8_000_000),
        compiler_params=pltpu.CompilerParams(collective_id=cid,has_side_effects=True,vmem_limit_bytes=56*1024*1024),
    )(mix,normed,cosine,sine,segments.reshape(length,1),segments.reshape(1,length),w_out,grad_out)

def attend_back_kernel(heads, groups, block, q_ref, kt_ref, k_ref, v_ref, lse_ref, gm_ref, cos_ref, sin_ref, segc_ref, segr_ref,
                  out_ref, bias_ref, qn_ref, gn_ref, dq_ref, dk_ref, dv_ref):
    length=q_ref.shape[1]
    per=heads//groups
    cosine, sine = cos_ref[...], sin_ref[...]
    def flip(p,_):
        rows=pl.ds(pl.multiple_of(p*2*HD,2*HD),2*HD)
        qn=q_ref[rows,:].astype(F32).T.astype(BF)
        gn=gm_ref[rows,:].astype(F32).T.astype(BF)
        qn_ref[2*p]=qn[:,:HD]
        qn_ref[2*p+1]=qn[:,HD:]
        gn_ref[2*p]=gn[:,:HD]
        gn_ref[2*p+1]=gn[:,HD:]
        return 0
    lax.fori_loop(0,heads//2,flip,0)
    dk_ref[...]=jnp.zeros_like(dk_ref)
    dv_ref[...]=jnp.zeros_like(dv_ref)
    for start in range(0,length,block):
        keys=start+block
        cols=slice(start,start+block)
        bias_ref[0:keys,:]=block_bias(segc_ref,segr_ref,start,block)
        def head(h,_):
            g=h//per
            rows=pl.ds(pl.multiple_of(h*HD,HD),HD)
            grows=pl.ds(pl.multiple_of(g*HD,HD),HD)
            scores=jnp.dot(k_ref[g,0:keys,:],q_ref[rows,cols],preferred_element_type=F32)
            probs=jnp.exp(scores+bias_ref[0:keys,:]-lse_ref[h,:,cols])
            dv_ref[g,0:keys,:]+=jnp.dot(probs.astype(BF),gn_ref[h,cols,:],preferred_element_type=F32)
            gp=jnp.dot(v_ref[g,0:keys,:],gm_ref[rows,cols],preferred_element_type=F32)
            weighted=probs*gp
            centre=jnp.sum(weighted,0,keepdims=True)
            gs=(weighted-probs*centre).astype(BF)
            dk_ref[g,0:keys,:]+=jnp.dot(gs,qn_ref[h,cols,:],preferred_element_type=F32)
            dq_ref[rows,cols]=0.125*jnp.dot(kt_ref[grows,0:keys],gs,preferred_element_type=F32)
            return 0
        lax.fori_loop(0,heads,head,0)
    def back(h,_):
        rows=pl.ds(pl.multiple_of(h*HD,HD),HD)
        out_ref[rows,:]=turn_t(dq_ref[rows,:],cosine,sine,-1.0).astype(BF)
        return 0
    lax.fori_loop(0,heads,back,0)
    dk=jnp.concatenate([dk_ref[g] for g in range(groups)],1).T
    dv=jnp.concatenate([dv_ref[g] for g in range(groups)],1).T
    for g in range(groups):
        out_ref[(heads+g)*HD:(heads+g+1)*HD,:]=turn_t(dk[g*HD:(g+1)*HD],cosine,sine,-1.0).astype(BF)
    out_ref[(heads+groups)*HD:,:]=dv.astype(BF)

def attend_back(q,kt,k,v,lse,gm,cosine,sine,segments,heads,groups):
    length=q.shape[1]
    block=min(256,length)
    vm=pl.BlockSpec(memory_space=pltpu.VMEM)
    return pl.pallas_call(functools.partial(attend_back_kernel,heads,groups,block),
        out_shape=jax.ShapeDtypeStruct(((heads+2*groups)*HD,length),BF),
        in_specs=[vm]*10,out_specs=vm,
        scratch_shapes=[pltpu.VMEM((length,block),F32),pltpu.VMEM((heads,length,HD),BF),pltpu.VMEM((heads,length,HD),BF),
            pltpu.VMEM((heads*HD,length),F32),pltpu.VMEM((groups,length,HD),F32),pltpu.VMEM((groups,length,HD),F32)],
        cost_estimate=pl.CostEstimate(flops=60_000_000_000,bytes_accessed=10_000_000,transcendentals=8_000_000),
        compiler_params=pltpu.CompilerParams(vmem_limit_bytes=48*1024*1024),
    )(q,kt,k,v,lse,gm,cosine,sine,segments.reshape(length,1),segments.reshape(1,length))


AXIS="tensor"
DP="dp"
MESH=pl.DeviceIdType.MESH

def greet(here, count, plane=0):
    barrier=pltpu.get_barrier_semaphore()
    if plane:
        def call(k,_):
            pl.semaphore_signal(barrier,inc=1,device_id={DP:lax.rem(lax.axis_index(DP)+k,plane)},device_id_type=MESH)
            return 0
        lax.fori_loop(1,plane,call,0)
        for k in range(1,count):
            pl.semaphore_signal(barrier,inc=1,device_id={AXIS:lax.rem(here+k,count)},device_id_type=MESH)
        pl.semaphore_wait(barrier,plane+count-2)
    else:
        @pl.when(here>0)
        def _(): pl.semaphore_signal(barrier,inc=1,device_id={AXIS:here-1},device_id_type=MESH)
        @pl.when(here<count-1)
        def _(): pl.semaphore_signal(barrier,inc=1,device_id={AXIS:here+1},device_id_type=MESH)
        pl.semaphore_wait(barrier,jnp.where((here>0)&(here<count-1),2,1))

def swap(axis, count, source, landing, sends, recvs):
    me=lax.axis_index(axis)
    def copy(peer, slot, k):
        return pltpu.make_async_remote_copy(src_ref=source(peer),dst_ref=landing.at[slot],send_sem=sends.at[k],
            recv_sem=recvs.at[slot],device_id={axis:peer},device_id_type=MESH)
    def begin(k,_):
        copy(lax.rem(me+k,count),me,k).start()
        return 0
    def end(k,_):
        peer=lax.rem(me+k,count)
        copy(peer,peer,k).wait_recv()
        copy(peer,me,k).wait_send()
        return 0
    return (lambda: lax.fori_loop(1,count,begin,0)),(lambda: lax.fori_loop(1,count,end,0))

def remote(src,dst,send,recv,target):
    return pltpu.make_async_remote_copy(src_ref=src,dst_ref=dst,send_sem=send,recv_sem=recv,
        device_id={AXIS:target},device_id_type=MESH)

class Line:
    def __init__(self,count,pieces,rows,part=None,sums=None,sum_sems=None,held=None,held_sems=None,base=0,sub=None):
        self.n,self.pieces,self.rows=count,pieces,rows
        self.sub=rows//pieces if sub is None else sub
        self.base=base
        self.here=lax.axis_index(AXIS)
        self.part,self.sums,self.sum_sems=part,sums,sum_sems
        self.held,self.held_sems=held,held_sems
    def span(self,u): return pl.ds(pl.multiple_of(self.base+u*self.sub,self.sub),self.sub)
    def fits(self,u): return (u>=0)&(u<self.pieces)
    def _target(self,way):
        return lax.min(self.here+1,self.n-1) if way==0 else lax.max(self.here-1,0)
    def slot(self,way,j,device):
        return j if way==0 else jnp.where(j==device,self.n,j)
    def sum_copy(self,way,j,u,first):
        sends,recvs=self.sum_sems
        dst=self.sums.at[self.slot(way,j,self._target(way)),self.span(u)]
        src=self.part.at[j,self.span(u)] if first else self.sums.at[self.slot(way,j,self.here),self.span(u)]
        return remote(src,dst,sends.at[way,j,u],recvs.at[way,j,u],self._target(way))
    def sum_arrival(self,way,j,u):
        sends,recvs=self.sum_sems
        ref=self.sums.at[self.slot(way,j,self.here),self.span(u)]
        return remote(ref,ref,sends.at[way,j,u],recvs.at[way,j,u],self._target(way))
    def relay(self,way,j,u,begins,passes):
        @pl.when(begins)
        def _(): self.sum_copy(way,j,u,True).start()
        @pl.when(passes)
        def _():
            self.sum_arrival(way,j,u).wait_recv()
            ref=self.sums.at[j,self.span(u)]
            ref[...]=(ref[...].astype(F32)+self.part[j,self.span(u)].astype(F32)).astype(BF)
            self.sum_copy(way,j,u,False).start()
    def far_steps(self): return (self.n-1)*self.pieces+1
    def far_step(self,t,total,finish):
        here,n,S=self.here,self.n,self.pieces
        for way in (0,1):
            q=t-here if way==0 else t-(n-1-here)
            ok=(q>=0)&(q<S*(n-1-here if way==0 else here))
            q=jnp.clip(q,0,S*(n-1)-1)
            j=n-1-q//S if way==0 else q//S
            end=(here==0) if way==0 else (here==n-1)
            self.relay(way,j,q%S,ok&end,ok&jnp.logical_not(end))
        u=t-(n-2)*S-1
        @pl.when(self.fits(u))
        def _():
            self.own_sum(u,total)
            finish(self.span(u),total)
    def send_sums(self,t):
        here,n=self.here,self.n
        for k in range(n-1):
            for way,j in ((0,n-1-k),(1,k)):
                u=t-here if way==0 else t-(n-1-here)
                ok=self.fits(u)
                u=jnp.clip(u,0,self.pieces-1)
                begins=(here==0) if way==0 else (here==n-1)
                passes=((here>0)&(here<j)) if way==0 else ((here<n-1)&(here>j))
                self.relay(way,j,u,ok&begins,ok&passes)
    def own_sum(self,u,total):
        here,n=self.here,self.n
        total[...]=self.part[here,self.span(u)].astype(F32)
        for way in (0,1):
            @pl.when(here>0 if way==0 else here<n-1)
            def _():
                self.sum_arrival(way,here,u).wait_recv()
                total[...]+=self.sums[self.slot(way,here,here),self.span(u)].astype(F32)
    def end_sums(self):
        here,n=self.here,self.n
        def one(u,_):
            for k in range(n-1):
                for way,j in ((0,n-1-k),(1,k)):
                    @pl.when((here<j) if way==0 else (here>j))
                    def _(): self.sum_copy(way,j,u,False).wait_send()
            return 0
        lax.fori_loop(0,self.pieces,one,0)
    def piece_copy(self,way,c,u,src=None):
        sends,recvs=self.held_sems
        dst=self.held.at[c,self.span(u)]
        return remote(dst if src is None else src,dst,sends.at[way,c,u],recvs.at[way,c,u],self._target(way))
    def send_own(self,u,src=None):
        here,n=self.here,self.n
        for way in (0,1):
            @pl.when(here<n-1 if way==0 else here>0)
            def _(): self.piece_copy(way,here,u,src).start()
    def pass_pieces(self,t,use=None):
        here,n=self.here,self.n
        for k in range(1,n):
            u=t-k
            ok=self.fits(u)
            u=jnp.clip(u,0,self.pieces-1)
            for way in (0,1):
                c=here-k if way==0 else here+k
                there=ok&((c>=0) if way==0 else (c<n))
                c=jnp.clip(c,0,n-1)
                @pl.when(there)
                def _(): self.piece_copy(way,c,u).wait_recv()
                @pl.when(there&(here<n-1 if way==0 else here>0))
                def _(): self.piece_copy(way,c,u).start()
                if use is not None:
                    @pl.when(there)
                    def _(): use(c,u)
    def end_pieces(self):
        here,n=self.here,self.n
        def one(u,_):
            for k in range(n):
                for way in (0,1):
                    c=here-k if way==0 else here+k
                    there=(c>=0) if way==0 else (c<n)
                    c=jnp.clip(c,0,n-1)
                    @pl.when(there&(here<n-1 if way==0 else here>0))
                    def _(): self.piece_copy(way,c,u).wait_send()
            return 0
        lax.fori_loop(0,self.pieces,one,0)

def turn_over(finish, count, plane, pieces, n_in, n_out, gather, share, *refs):
    part,other=refs[:2]; ins=refs[2:2+n_in]; outs=refs[2+n_in:2+n_in+n_out]
    rest=list(refs[2+n_in+n_out:])
    acc_out=rest.pop(0)
    whole=rest.pop(0) if gather else None
    sums,total,ss,sr,acc=rest[:5]; rest=rest[5:]
    held=hs=hr=None
    if gather: held,hs,hr,ws=rest[:4]; rest=rest[4:]
    if share: cut,landed,level,stacked,ds,dr,zs,zr=rest
    rows=part.shape[1]
    line=Line(count,pieces,rows,part,sums,(ss,sr),held,(hs,hr))
    greet(line.here,count,plane if share else 0)
    far=count-1
    acc[...]=jnp.zeros_like(acc)
    width=part.shape[2]
    def terms(t):
        def some(k,_):
            span=pl.ds(pl.multiple_of(k*16,16),16)
            both=part[t,span].astype(F32)*other[t,span].astype(F32)
            acc[...]+=both[:8]+both[8:]
            return 0
        lax.fori_loop(0,rows//16,some,0)
    if share:
        me=lax.axis_index(DP)
        piece=width//plane
        begin_dp,end_dp=swap(DP,plane,lambda p: cut.at[p],landed,ds,dr)
        begin_z,end_z=swap(AXIS,count,lambda p: level,stacked,zs,zr)
    def step(t,_):
        if gather:
            line.send_sums(t)
            line.pass_pieces(t-far)
            u=t-far
            @pl.when(line.fits(u))
            def _():
                line.own_sum(u,total)
                held[line.here,line.span(u)]=finish(line.span(u),total,ins,outs)
                line.send_own(u)
        else:
            line.far_step(t,total,lambda span,total: finish(span,total,ins,outs))
        @pl.when(t<count)
        def _(): terms(jnp.clip(t,0,count-1))
        if share:
            @pl.when(t==count-1)
            def _():
                for p in range(plane):
                    cut[p,0:8,:]=acc[:,p*piece:(p+1)*piece]
                    cut[p,8:16,:]=ins[-1][:,p*piece:(p+1)*piece]
                landed[me]=cut[me]
                begin_dp()
            @pl.when(t==count)
            def _():
                end_dp()
                level[...]=jnp.sum(landed[...],0)
                stacked[line.here]=level[...]
                begin_z()
        return 0
    steps=pieces+2*far if gather else line.far_steps()
    lax.fori_loop(0,steps,step,0)
    if gather:
        copy=pltpu.make_async_copy(held,whole,ws); copy.start()
    if share:
        end_z()
        acc_out[...]=jnp.sum(stacked[...],0)
    else:
        acc_out[...]=acc[...]
    line.end_sums()
    if gather:
        line.end_pieces()
        copy.wait()

def sum_and_finish(part,other,ins,out_shapes,finish,gather,share,cid,pieces,tensor,plane):
    n=tensor; rows=part.shape[0]//n; D=part.shape[1]
    assert pieces>=2
    vm=pl.BlockSpec(memory_space=pltpu.VMEM)
    outs=list(out_shapes); out_specs=[vm]*len(outs)
    sds=jax.ShapeDtypeStruct
    outs.append(sds((16,D//plane) if share else (8,D),F32)); out_specs.append(vm)
    sem=pltpu.SemaphoreType.DMA
    scratch=[pltpu.VMEM((n+1,rows,D),BF),pltpu.VMEM((rows//pieces,D),F32),sem((2,n,pieces)),sem((2,n,pieces)),pltpu.VMEM((8,D),F32)]
    if gather:
        outs.append(sds((n,rows,D),BF)); out_specs.append(pl.BlockSpec(memory_space=pl.ANY))
        scratch+=[pltpu.VMEM((n,rows,D),BF),sem((2,n,pieces)),sem((2,n,pieces)),sem]
    if share:
        w=D//plane
        scratch+=[pltpu.VMEM((plane,16,w),F32),pltpu.VMEM((plane,16,w),F32),pltpu.VMEM((16,w),F32),pltpu.VMEM((n,16,w),F32),
            sem((plane,)),sem((plane,)),sem((n,)),sem((n,))]
    res=pl.pallas_call(functools.partial(turn_over,finish,n,plane,pieces,len(ins),len(out_shapes),gather,share),
        out_shape=tuple(outs),in_specs=[vm]*(2+len(ins)),out_specs=tuple(out_specs),scratch_shapes=scratch,
        cost_estimate=pl.CostEstimate(flops=0,bytes_accessed=270_000_000,transcendentals=0),
        compiler_params=pltpu.CompilerParams(collective_id=cid,has_side_effects=True,vmem_limit_bytes=56*1024*1024),
    )(part.reshape(n,rows,D),other.reshape(n,rows,D),*ins)
    return res


def mlp_kernel(count,pieces,tile,x_ref,grad_ref,res_ref,early_hbm,wg_hbm,wu_hbm,wd_hbm,
        part_ref,wide_ref,out_ref,gr,product,gated,lifted,down,ring,tall,sums,total,hs,hr,ss,sr,ws,ts,ls):
    s=pl.program_id(0)
    length,hidden=product.shape
    width=x_ref.shape[1]
    rows=grad_ref.shape[0]
    half=rows//2
    first,second=hidden//tile,width//tile
    slots=ring.shape[0]
    at_down=first; at_grad=first+second; at_part=2*first+second; at_weight=2*first+2*second
    spread=pieces//2
    get=Line(count,spread,rows,held=gr,held_sems=(hs,hr),base=half,sub=half//spread)
    line=Line(count,pieces,rows,down,sums,(ss,sr))
    def strip(k,size): return pl.ds(pl.multiple_of(jnp.clip(k,0,size-1)*tile,tile),tile)
    def tall_load(k):
        slot=lax.rem(k,slots)
        @pl.when((k<2*first)&(lax.rem(k,2)==0))
        def _(): pltpu.make_async_copy(wg_hbm.at[:,strip(k//2,first)],tall.at[slot],ts.at[slot]).start()
        @pl.when((k<2*first)&(lax.rem(k,2)==1))
        def _(): pltpu.make_async_copy(wu_hbm.at[:,strip(k//2,first)],tall.at[slot],ts.at[slot]).start()
        @pl.when((k>=2*first)&(k<2*first+second))
        def _(): pltpu.make_async_copy(wd_hbm.at[:,strip(k-2*first,second)],tall.at[slot],ts.at[slot]).start()
    def tall_loaded(k):
        slot=lax.rem(k,slots)
        pltpu.make_async_copy(wg_hbm.at[:,pl.ds(0,tile)],tall.at[slot],ts.at[slot]).wait()
        return slot
    def load(k):
        slot=lax.rem(k,slots)
        late=strip((k-first)//2,second)
        @pl.when(k<first)
        def _(): pltpu.make_async_copy(wd_hbm.at[strip(k,first),:],ring.at[slot],ws.at[slot]).start()
        @pl.when((k>=first)&(lax.rem(k-first,2)==0)&(k<first+2*second))
        def _(): pltpu.make_async_copy(wg_hbm.at[late,:],ring.at[slot],ws.at[slot]).start()
        @pl.when((k>=first)&(lax.rem(k-first,2)==1)&(k<first+2*second))
        def _(): pltpu.make_async_copy(wu_hbm.at[late,:],ring.at[slot],ws.at[slot]).start()
    def loaded(k):
        slot=lax.rem(k,slots)
        pltpu.make_async_copy(wd_hbm.at[pl.ds(0,tile),:],ring.at[slot],ws.at[slot]).wait()
        return slot
    def own(): return pltpu.make_async_copy(grad_ref,gr.at[get.here],ls.at[0])
    def early(c): return pltpu.make_async_copy(early_hbm.at[c],gr.at[c,pl.ds(0,half)],ls.at[1+c])
    @pl.when(s==0)
    def _():
        for k in range(slots): tall_load(k)
        greet(get.here,count)
        for u in range(spread):
            get.send_own(u,grad_ref.at[get.span(u),:])
        own().start()
        for c in range(count):
            @pl.when(c!=get.here)
            def _(): early(c).start()
    @pl.when(s==at_down-1)
    def _():
        for k in range(slots): load(k)
    hops=spread+count-2
    gap=max(1,at_grad//hops)
    @pl.when((s>0)&(lax.rem(s,gap)==0)&(s<=gap*hops))
    def _(): get.pass_pieces(s//gap)
    @pl.when(s==at_grad)
    def _():
        own().wait()
        for c in range(count):
            @pl.when(c!=get.here)
            def _(): early(c).wait()
    def finish(span,total):
        out_ref[span,:]=(res_ref[span,:]+total[...]).astype(BF)
    r=s-at_grad
    if first==4 and second==4 and line.far_steps()==13:
        ok=(r>=0)&(r!=2)&((r<8)|(lax.rem(r,4)==0))
        t=jnp.where(r<2,r,jnp.where(r<8,r-1,5+r//4))
    else:
        ok=(r>=0)&(r<line.far_steps())
        t=r
    @pl.when(ok)
    def _(): line.far_step(t,total,finish)
    @pl.when(s<at_down)
    def _():
        one=tall_loaded(2*s)
        two=tall_loaded(2*s+1)
        cols=strip(s,first)
        for c in range(count):
            span=slice(c*rows,(c+1)*rows)
            gate=jnp.dot(x_ref[span,:],tall[one],preferred_element_type=F32)
            up=jnp.dot(x_ref[span,:],tall[two],preferred_element_type=F32)
            sigmoid=1.0/(1.0+jnp.exp(-gate))
            active=gate*sigmoid
            product[span,cols]=(active*up).astype(BF)
            lifted[span,cols]=active.astype(BF)
            gated[span,cols]=(up*(sigmoid+active*(1.0-sigmoid))).astype(BF)
        tall_load(2*s+slots)
        tall_load(2*s+1+slots)
    @pl.when((s>=at_down)&(s<at_grad))
    def _():
        k=2*first+s-at_down
        slot=tall_loaded(k)
        sums_here=jnp.dot(product[...],tall[slot],preferred_element_type=F32).astype(BF)
        cols=strip(s-at_down,second)
        for c in range(count): down[c,:,cols]=sums_here[c*rows:(c+1)*rows]
        tall_load(k+slots)
    @pl.when((s>=at_grad)&(s<at_part))
    def _():
        k=s-at_grad
        slot=loaded(k)
        cols=strip(k,first)
        for c in range(count):
            span=slice(c*rows,(c+1)*rows)
            grads=lax.dot_general(gr[c],ring[slot],(((1,),(1,)),((),())),preferred_element_type=F32)
            gated[span,cols]=(grads*gated[span,cols].astype(F32)).astype(BF)
            lifted[span,cols]=(grads*lifted[span,cols].astype(F32)).astype(BF)
        load(k+slots)
    @pl.when((s>=at_part)&(s<at_weight))
    def _():
        k=first+2*(s-at_part)
        one=loaded(k)
        both=lax.dot_general(gated[...],ring[one],(((1,),(1,)),((),())),preferred_element_type=F32)
        load(k+slots)
        two=loaded(k+1)
        both=both+lax.dot_general(lifted[...],ring[two],(((1,),(1,)),((),())),preferred_element_type=F32)
        part_ref[...]=both.astype(BF)
        load(k+1+slots)
    last=s-at_weight
    cols=strip(last//6,second)
    kind=lax.rem(last,6)
    cut=hidden//2
    def weight(left,right):
        wide_ref[...]=lax.dot_general(left,right,(((0,),(0,)),((),())),preferred_element_type=F32).astype(BF)
    for side in (0,1):
        these=slice(side*cut,(side+1)*cut)
        @pl.when((last>=0)&(kind==side))
        def _(): weight(x_ref[:,cols],gated[:,these])
        @pl.when((last>=0)&(kind==2+side))
        def _(): weight(x_ref[:,cols],lifted[:,these])
        @pl.when((last>=0)&(kind==4+side))
        def _(): weight(gr[:,:,cols].reshape(length,tile),product[:,these])
    @pl.when(s==at_weight+6*second-1)
    def _():
        get.end_pieces()
        line.end_sums()

def mlp(x,grad_out,residual,early,w_gate,w_up,w_down,cid,pieces,count):
    length,width=x.shape
    hidden=w_gate.shape[1]
    rows=length//count
    tile=min(512,hidden,width)
    first,second=hidden//tile,width//tile
    steps=2*first+8*second
    assert first+7*second>=(count-1)*pieces+1
    whole=lambda shape: pl.BlockSpec(shape,lambda s: (0,)*len(shape),pipeline_mode=pl.Buffered(1))
    hbm=pl.BlockSpec(memory_space=pl.ANY)
    sds=jax.ShapeDtypeStruct
    sem=pltpu.SemaphoreType.DMA
    at_part=2*first+second
    def wide_map(s):
        k=jnp.maximum(s-at_part-second,0)
        return (k//6,k%6)
    vmem=pltpu.VMEM
    spread=pieces//2
    return pl.pallas_call(functools.partial(mlp_kernel,count,pieces,tile),
        grid=(steps,),
        out_shape=(sds((length,width),BF),sds((width,3*hidden),BF),sds((rows,width),BF)),
        in_specs=[whole((length,width)),whole((rows,width)),whole((rows,width)),hbm,hbm,hbm,hbm],
        out_specs=(pl.BlockSpec((length,tile),lambda s: (0,jnp.clip(s-at_part,0,second-1))),
            pl.BlockSpec((tile,hidden//2),wide_map),whole((rows,width))),
        scratch_shapes=[vmem((count,rows,width),BF),vmem((length,hidden),BF),vmem((length,hidden),BF),vmem((length,hidden),BF),
            vmem((count,rows,width),BF),vmem((4,tile,width),BF),vmem((4,width,tile),BF),vmem((count+1,rows,width),BF),vmem((rows//pieces,width),F32),
            sem((2,count,spread)),sem((2,count,spread)),sem((2,count,pieces)),sem((2,count,pieces)),sem((4,)),sem((4,)),sem((count+1,))],
        cost_estimate=pl.CostEstimate(flops=78_000_000_000,bytes_accessed=380_000_000,transcendentals=0),
        compiler_params=pltpu.CompilerParams(collective_id=cid,has_side_effects=True,vmem_limit_bytes=60*1024*1024,
            dimension_semantics=("arbitrary",)),
    )(x,grad_out,residual,early,w_gate,w_up,w_down)


def frequencies(head_size):
    inverse = 1.0 / 500000.0 ** (jnp.arange(head_size // 2, dtype=jnp.float32) * 2.0 / head_size)
    wavelength = 2.0 * math.pi / inverse
    smooth = (8192.0 / wavelength - 1.0) / 3.0
    blended = (1.0 - smooth) * inverse / 32.0 + smooth * inverse
    return jnp.where(
        wavelength > 8192.0, inverse / 32.0, jnp.where(wavelength < 2048.0, inverse, blended)
    )


def dot(left_side, right_side, left_dim, right_dim):
    return lax.dot_general(
        left_side, right_side, (((left_dim,), (right_dim,)), ((), ())), preferred_element_type=F32
    )


def norm_kernel(count, plane, pieces, tokens_ref, gains_ref, normed, gains_out, held, landed, hs, hr, ds, dr):
    line = Line(count, pieces, tokens_ref.shape[0], held=held, held_sems=(hs, hr))
    greet(line.here, count, plane)
    me = lax.axis_index(DP)
    begin, end = swap(DP, plane, lambda p: gains_ref, landed, ds, dr)
    for u in range(pieces):
        line.send_own(u, tokens_ref.at[line.span(u), :])
    begin()
    landed[me] = gains_ref[...]
    end()
    piece = gains_ref.shape[1]
    for p in range(plane):
        gains_out[:, p * piece : (p + 1) * piece] = landed[p]

    def norm(rows, c, u):
        stream = rows.astype(F32)
        scale = lax.rsqrt(jnp.mean(stream * stream, -1, keepdims=True) + EPSILON)
        normed[c, line.span(u)] = (stream * scale * gains_out[0:1, :]).astype(BF)

    def step(t, _):
        line.pass_pieces(t, lambda c, u: norm(held[c, line.span(u)], c, u))

        @pl.when(t < pieces)
        def _():
            u = jnp.clip(t, 0, pieces - 1)
            norm(tokens_ref[line.span(u), :], line.here, u)

        return 0

    lax.fori_loop(0, pieces + count - 1, step, 0)
    line.end_pieces()


def norm_and_gather(tokens, gains, cid, pieces, count, plane):
    rows, width = tokens.shape
    vm = pl.BlockSpec(memory_space=pltpu.VMEM)
    sem = pltpu.SemaphoreType.DMA
    normed, gains = pl.pallas_call(
        functools.partial(norm_kernel, count, plane, pieces),
        out_shape=(jax.ShapeDtypeStruct((count, rows, width), BF), jax.ShapeDtypeStruct((8, width), F32)),
        in_specs=[vm, vm],
        out_specs=(vm, vm),
        scratch_shapes=[
            pltpu.VMEM((count, rows, width), BF),
            pltpu.VMEM((plane, 8, width // plane), F32),
            sem((2, count, pieces)),
            sem((2, count, pieces)),
            sem((plane,)),
            sem((plane,)),
        ],
        cost_estimate=pl.CostEstimate(flops=0, bytes_accessed=270_000_000, transcendentals=0),
        compiler_params=pltpu.CompilerParams(
            collective_id=cid, has_side_effects=True, vmem_limit_bytes=40 * 1024 * 1024
        ),
    )(tokens, gains)
    return normed.reshape(count * rows, width), gains


def finish_attention(span, total, ins, outs):
    tokens, gain = ins
    residual = total[...] + tokens[span, :].astype(F32)
    outs[0][span, :] = residual
    scale = lax.rsqrt(jnp.mean(residual * residual, -1, keepdims=True) + EPSILON)
    return (residual * scale * gain[...]).astype(BF)


def finish_residual(span, total, ins, outs):
    residual_ref, grad_out, gain = ins
    residual = residual_ref[span, :]
    scale = lax.rsqrt(jnp.mean(residual * residual, -1, keepdims=True) + EPSILON)
    unit = residual * scale
    grads = total[...]
    scaled = grads * gain[...]
    grad_residual = grad_out[span, :].astype(F32) + scale * (
        scaled - unit * jnp.mean(scaled * unit, -1, keepdims=True)
    )
    outs[0][span, :] = grad_residual
    return grad_residual.astype(BF)


def finish_tokens(span, total, ins, outs):
    tokens, grad_residual, gain, _ = ins
    stream = tokens[span, :].astype(F32)
    scale = lax.rsqrt(jnp.mean(stream * stream, -1, keepdims=True) + EPSILON)
    unit = stream * scale
    grads = total[...]
    scaled = grads * gain[...]
    outs[0][span, :] = grad_residual[span, :] + scale * (
        scaled - unit * jnp.mean(scaled * unit, -1, keepdims=True)
    )


def body(
    count,
    plane,
    tokens,
    segments,
    positions,
    attn_gain,
    w_query,
    w_key,
    w_value,
    w_out,
    mlp_gain,
    w_gate,
    w_up,
    w_down,
    grad_out,
):
    rows, width = tokens.shape
    heads = w_query.shape[1] // HD
    groups = w_key.shape[1] // HD
    after = lax.optimization_barrier
    mix = lax.all_gather(jnp.concatenate([w_query, w_key, w_value], 1).T, DP, axis=1, tiled=True)
    full_out = lax.all_gather(w_out, DP, axis=1, tiled=True)
    full_gate = lax.all_gather(w_gate, DP, axis=0, tiled=True)
    full_up = lax.all_gather(w_up, DP, axis=0, tiled=True)
    full_down = lax.all_gather(w_down, DP, axis=1, tiled=True)
    gains = jnp.concatenate([jnp.stack([attn_gain, mlp_gain]).astype(F32), jnp.zeros((6, attn_gain.shape[0]), F32)])

    normed_one, gains = norm_and_gather(tokens, gains, 1, 4, count, plane)
    gain_one, gain_two = gains[0:1], gains[1:2]
    angles = frequencies(HD)[:, None] * positions.astype(F32)[None, :]
    cosine, sine = jnp.cos(angles), jnp.sin(angles)

    mixed, lse, q, kt, k, vt, v, part, early = attend(
        mix, normed_one, cosine, sine, segments, full_out, grad_out, heads, groups, 6, 2, count
    )
    residual, _, normed_two = sum_and_finish(
        part, part, (tokens, gain_two), (jax.ShapeDtypeStruct((rows, width), F32),),
        finish_attention, True, False, 2, 16, count, plane,
    )
    normed_two = normed_two.reshape(count * rows, width)
    part, grad_wide, block_out = mlp(normed_two, grad_out, residual, early, full_gate, full_up, full_down, 5, 4, count)
    grad_wide = lax.psum_scatter(grad_wide, DP, scatter_dimension=0, tiled=True)
    wide = jax.ShapeDtypeStruct((rows, width), F32)
    grad_residual, terms_two, grad_low = sum_and_finish(
        part, normed_two, (residual, grad_out, gain_two), (wide,), finish_residual, True, False, 3, 16, count, plane
    )
    grad_low = grad_low.reshape(count * rows, width)
    grad_mixed = dot(full_out, grad_low, 1, 1).astype(BF)
    grad_out_proj = dot(grad_low, mixed, 0, 1).astype(BF)
    turned = attend_back(q, kt, k, v, lse, grad_mixed, cosine, sine, segments, heads, groups)
    grad_mix = jnp.concatenate([dot(normed_one, turned, 0, 1).astype(BF), grad_out_proj], 1)
    turned, grad_mix, grad_wide = after((turned, grad_mix, grad_wide))
    grad_mix = lax.psum_scatter(grad_mix, DP, scatter_dimension=0, tiled=True)
    part = dot(turned, mix, 0, 0).astype(BF)
    grad_tokens, sums = sum_and_finish(
        part, normed_one, (tokens, grad_residual, gain_one, terms_two), (wide,), finish_tokens, False, True, 4, 4, count, plane
    )
    sums = jnp.sum(sums.reshape(2, 8, -1), 1)
    edges = (heads * HD, (heads + groups) * HD, (heads + 2 * groups) * HD)
    grad_query, grad_key, grad_value, grad_out_proj = jnp.split(grad_mix.astype(F32), edges, 1)
    grad_gate, grad_up, grad_down = jnp.split(grad_wide.astype(F32), 3, 1)
    return (
        block_out,
        grad_tokens,
        sums[0] / attn_gain.astype(F32),
        grad_query,
        grad_key,
        grad_value,
        grad_out_proj.T,
        sums[1] / mlp_gain.astype(F32),
        grad_gate,
        grad_up,
        grad_down.T,
    )


def solution(mesh):
    placed = (
        P(("dp", "tensor"), None),
        P("dp"),
        P("dp"),
        P("dp"),
        P("dp", "tensor"),
        P("dp", "tensor"),
        P("dp", "tensor"),
        P("tensor", "dp"),
        P("dp"),
        P("dp", "tensor"),
        P("dp", "tensor"),
        P("tensor", "dp"),
        P(("dp", "tensor"), None),
    )
    return jax.shard_map(
        functools.partial(body, mesh.shape["tensor"], mesh.shape["dp"]),
        mesh=mesh,
        in_specs=placed,
        out_specs=(
            P(("dp", "tensor"), None),
            P(("dp", "tensor"), None),
            P("dp"),
            P("dp", "tensor"),
            P("dp", "tensor"),
            P("dp", "tensor"),
            P("tensor", "dp"),
            P("dp"),
            P("dp", "tensor"),
            P("dp", "tensor"),
            P("tensor", "dp"),
        ),
        check_vma=False,
    )
```

```python
import functools
import math

import jax
import jax.numpy as jnp
from jax import lax
from jax.experimental import pallas as pl
from jax.experimental.pallas import tpu as pltpu
from jax.sharding import PartitionSpec as P

HD = 64
EPSILON = 1e-05
MASKED = -1e30
F32 = jnp.float32
BF = jnp.bfloat16

def turn_t(values, cosine, sine, sign):
    half=values.shape[0]//2
    first, second = values[:half], values[half:]
    return jnp.concatenate([first*cosine - sign*second*sine, second*cosine + sign*first*sine],0)

def block_bias(segs_col, segs_row, start, block):
    keys=start+block
    key_places=lax.broadcasted_iota(jnp.int32,(keys,block),0)
    query_places=start+lax.broadcasted_iota(jnp.int32,(keys,block),1)
    allowed=(key_places<=query_places)&(segs_col[0:keys,:]==segs_row[0:1,start:start+block])
    return jnp.where(allowed,0.0,MASKED).astype(F32)

def attend_kernel(heads, groups, block, count, pieces, fine, mix_ref, normed_ref, cos_ref, sin_ref, segc_ref, segr_ref, wo_hbm, grad_ref, tokens_hbm, gain_ref,
                  mixed_ref, lse_ref, q_ref, kt_ref, k_ref, v_ref, residual_ref, rows_hbm, whole_hbm,
                  lin_ref, bias_ref, vt_ref, wo_ref, tokens_ref, part_ref, held, hs, hr, sums, total, ss, sr, moved, ms, mr, cs):
    length=normed_ref.shape[0]
    per=heads//groups
    rows=grad_ref.shape[0]
    line=Line(count,pieces,rows,held=held,held_sems=(hs,hr),sub=rows//(2*pieces))
    greet(line.here,count)
    for u in range(pieces):
        line.send_own(u,grad_ref.at[line.span(u),:])
    weights=pltpu.make_async_copy(wo_hbm,wo_ref,cs.at[0])
    weights.start()
    stream=pltpu.make_async_copy(tokens_hbm,tokens_ref,cs.at[1])
    stream.start()
    lines=mix_ref.shape[1]
    cut=256 if lines%256==0 else lines
    for c in range(0,lines,cut):
        lin_ref[c:c+cut,:]=lax.dot_general(mix_ref[:,c:c+cut],normed_ref[...],(((0,),(1,)),((),())),preferred_element_type=F32)
    steps=pieces+count-1
    line.pass_pieces(1)
    done=1
    cosine, sine = cos_ref[...], sin_ref[...]
    def rope(h,_):
        rows=pl.ds(pl.multiple_of(h*HD,HD),HD)
        q_ref[rows,:]=(turn_t(lin_ref[rows,:],cosine,sine,1.0).astype(BF)*jnp.asarray(0.125,BF))
        return 0
    lax.fori_loop(0,heads,rope,0)
    turned=[turn_t(lin_ref[(heads+g)*HD:(heads+g+1)*HD,:],cosine,sine,1.0) for g in range(groups)]
    keys_t=jnp.concatenate(turned,0)
    kt_ref[...]=keys_t.astype(BF)
    vals_t=lin_ref[(heads+groups)*HD:(heads+2*groups)*HD,:]
    vt_ref[...]=vals_t.astype(BF)
    keys_n=keys_t.T.astype(BF)
    vals_n=vals_t.T.astype(BF)
    for g in range(groups):
        k_ref[g]=keys_n[:,g*HD:(g+1)*HD]
        v_ref[g]=vals_n[:,g*HD:(g+1)*HD]
    for start in range(0,length,block):
        keys=start+block
        if start==3*block and done<steps-1:
            done+=1
            line.pass_pieces(done)
        bias_ref[0:keys,:]=block_bias(segc_ref,segr_ref,start,block)
        def head(h,_):
            g=h//per
            rows=pl.ds(pl.multiple_of(h*HD,HD),HD)
            grows=pl.ds(pl.multiple_of(g*HD,HD),HD)
            scores=jnp.dot(k_ref[g,0:keys,:],q_ref[rows,start:start+block],preferred_element_type=F32)
            scores=scores+bias_ref[0:keys,:]
            top=jnp.max(scores,0,keepdims=True)
            weights=jnp.exp(scores-top)
            total=jnp.sum(weights,0,keepdims=True)
            out=jnp.dot(vt_ref[grows,0:keys],weights.astype(BF),preferred_element_type=F32)
            mixed_ref[rows,start:start+block]=(out/total).astype(BF)
            lse_ref[h,:,start:start+block]=top+jnp.log(total)
            return 0
        lax.fori_loop(0,heads,head,0)
    width=wo_ref.shape[1]
    wide=min(512,width)
    weights.wait()
    if done<steps-1:
        done+=1
        line.pass_pieces(done)
    def out(c,_):
        cols=pl.ds(pl.multiple_of(c*wide,wide),wide)
        product=lax.dot_general(mixed_ref[...],wo_ref[:,cols],(((0,),(0,)),((),())),preferred_element_type=F32).astype(BF)
        for j in range(count): part_ref[j,:,cols]=product[j*rows:(j+1)*rows]
        return 0
    lax.fori_loop(0,width//wide,out,0)
    half=rows//2
    held[line.here,0:half]=grad_ref[0:half,:]
    copy=pltpu.make_async_copy(held,rows_hbm,cs.at[2])
    stream.wait()
    sweep=Line(count,fine,rows,part_ref,sums,(ss,sr),moved,(ms,mr))
    def finish(span,total):
        residual=total[...]+tokens_ref[span,:].astype(F32)
        residual_ref[span,:]=residual
        scale=lax.rsqrt(jnp.mean(residual*residual,-1,keepdims=True)+EPSILON)
        return (residual*scale*gain_ref[...]).astype(BF)
    def step(t,_):
        sweep.sweep(t,total,finish)
        for k in range(done+1,steps):
            @pl.when(t==2*(k-done-1))
            def _(): line.pass_pieces(k)
        return 0
    lax.fori_loop(0,sweep.sweep_steps(),step,0)
    copy.start()
    last=pltpu.make_async_copy(moved,whole_hbm,cs.at[3])
    last.start()
    line.end_pieces()
    sweep.end_sums()
    sweep.end_pieces()
    copy.wait()
    last.wait()

def attend(mix, normed, cosine, sine, segments, w_out, grad_out, tokens, gain, heads, groups, cid, pieces, fine, count):
    length,width=normed.shape
    rows=grad_out.shape[0]
    block=min(256,length)
    sds=jax.ShapeDtypeStruct
    vm=pl.BlockSpec(memory_space=pltpu.VMEM)
    hbm=pl.BlockSpec(memory_space=pl.ANY)
    sem=pltpu.SemaphoreType.DMA
    vmem=pltpu.VMEM
    return pl.pallas_call(functools.partial(attend_kernel,heads,groups,block,count,pieces,fine),
        out_shape=(sds((heads*HD,length),BF),sds((heads,1,length),F32),sds((heads*HD,length),BF),
            sds((groups*HD,length),BF),sds((groups,length,HD),BF),sds((groups,length,HD),BF),
            sds((rows,width),F32),sds((count,rows//2,width),BF),sds((count,rows,width),BF)),
        in_specs=[vm]*6+[hbm,vm,hbm,vm],out_specs=(vm,)*7+(hbm,hbm),
        scratch_shapes=[vmem((mix.shape[1],length),F32),vmem((length,block),F32),vmem((groups*HD,length),BF),vmem(w_out.shape,BF),
            vmem(tokens.shape,BF),vmem((count,rows,width),BF),vmem((count,rows//2,width),BF),sem((2,count,pieces)),sem((2,count,pieces)),
            vmem((count+1,rows,width),BF),vmem((rows//fine,width),F32),sem((2,count,fine)),sem((2,count,fine)),
            vmem((count,rows,width),BF),sem((2,count,fine)),sem((2,count,fine)),sem((4,))],
        cost_estimate=pl.CostEstimate(flops=30_000_000_000,bytes_accessed=500_000_000,transcendentals=8_000_000),
        compiler_params=pltpu.CompilerParams(collective_id=cid,has_side_effects=True,vmem_limit_bytes=58*1024*1024),
    )(mix,normed,cosine,sine,segments.reshape(length,1),segments.reshape(1,length),w_out,grad_out,tokens,gain)

def attend_back_kernel(heads, groups, block, count, pieces, fine, grads_hbm, two_hbm, go_ref, gain_ref, wo_hbm, q_ref, kt_ref, k_ref, v_ref, lse_ref, cos_ref, sin_ref, segc_ref, segr_ref,
                  down_ref, res_ref, early_ref, mixed_hbm, normed_hbm, mix_hbm,
                  gres_ref, acc, part_hbm, grad_hbm, out_ref,
                  part_ref, normed_ref, low_ref, wide_sums, wide_total, ws, wr, hs, hr,
                  wo_ref, mixed_ref, mix_ref, turn_ref, gm_ref, bias_ref, qn_ref, gn_ref, dq_ref, dk_ref, dv_ref, sums, total, ss, sr, grad_ref, cs, gs_sem):
    length=q_ref.shape[1]
    per=heads//groups
    width=wo_ref.shape[1]
    rows=res_ref.shape[0]
    half=rows//2
    line=Line(count,pieces,half,down_ref,sums,(ss,sr))
    sweep=Line(count,fine,rows,part_ref,wide_sums,(ws,wr),low_ref,(hs,hr))
    first=pltpu.make_async_copy(grads_hbm,part_ref,cs.at[0])
    first.start()
    second=pltpu.make_async_copy(two_hbm,normed_ref,cs.at[1])
    second.start()
    late=[pltpu.make_async_copy(s,d,cs.at[2+k]) for k,(s,d) in enumerate(((mixed_hbm,mixed_ref),(mix_hbm,mix_ref),(wo_hbm,wo_ref)))]
    for copy in late: copy.start()
    greet(line.here,count)
    acc[...]=jnp.zeros_like(acc)
    out_ref[0:half,:]=early_ref[...]
    first.wait()
    def turn(span,total):
        residual=res_ref[span,:]
        scale=lax.rsqrt(jnp.mean(residual*residual,-1,keepdims=True)+EPSILON)
        unit=residual*scale
        scaled=total[...]*gain_ref[...]
        grads=go_ref[span,:].astype(F32)+scale*(scaled-unit*jnp.mean(scaled*unit,-1,keepdims=True))
        gres_ref[span,:]=grads
        return grads.astype(BF)
    def finish(span,total):
        places=pl.ds(pl.multiple_of(half+span.start,line.sub),line.sub)
        out_ref[places,:]=(res_ref[places,:]+total[...]).astype(BF)
    steps=sweep.sweep_steps()
    begun=2
    def step(t,_):
        sweep.sweep(t,wide_total,turn)
        @pl.when(t==2)
        def _(): second.wait()
        @pl.when((t>=2)&(t<count+2))
        def _(): gain_terms(part_ref,normed_ref,acc,jnp.clip(t-2,0,count-1))
        for k in range(begun):
            @pl.when(t==steps-2*(begun-k))
            def _(): line.far_step(jnp.int32(k),total,finish)
        return 0
    lax.fori_loop(0,steps,step,0)
    third=pltpu.make_async_copy(normed_hbm,normed_ref,cs.at[1])
    third.start()
    ticks=[begun]
    def tick(amount=1):
        for _ in range(amount):
            if ticks[0]<line.far_steps():
                line.far_step(jnp.int32(ticks[0]),total,finish)
                ticks[0]+=1
    late[2].wait()
    whole=lambda: low_ref[...].reshape(length,width)
    cosine, sine = cos_ref[...], sin_ref[...]
    deep=heads*HD
    cut=256 if deep%256==0 else deep
    for c in range(0,deep,cut):
        gm_ref[c:c+cut,:]=lax.dot_general(wo_ref[c:c+cut,:],whole(),(((1,),(1,)),((),())),preferred_element_type=F32).astype(BF)
    def flip(p,_):
        rows=pl.ds(pl.multiple_of(p*2*HD,2*HD),2*HD)
        qn=q_ref[rows,:].astype(F32).T.astype(BF)
        gn=gm_ref[rows,:].astype(F32).T.astype(BF)
        qn_ref[2*p]=qn[:,:HD]
        qn_ref[2*p+1]=qn[:,HD:]
        gn_ref[2*p]=gn[:,:HD]
        gn_ref[2*p+1]=gn[:,HD:]
        return 0
    lax.fori_loop(0,heads//2,flip,0)
    dk_ref[...]=jnp.zeros_like(dk_ref)
    dv_ref[...]=jnp.zeros_like(dv_ref)
    lines=(heads+2*groups)*HD
    strip=min(512,width)
    late[0].wait()
    tick()
    for c in range(0,width,strip):
        grad_ref[c:c+strip,lines:]=lax.dot_general(low_ref[:,:,c:c+strip].reshape(length,strip),mixed_ref[...],(((0,),(1,)),((),())),preferred_element_type=F32).astype(BF)
    for start in range(0,length,block):
        keys=start+block
        cols=slice(start,start+block)
        bias_ref[0:keys,:]=block_bias(segc_ref,segr_ref,start,block)
        def head(h,_):
            g=h//per
            rows=pl.ds(pl.multiple_of(h*HD,HD),HD)
            grows=pl.ds(pl.multiple_of(g*HD,HD),HD)
            scores=jnp.dot(k_ref[g,0:keys,:],q_ref[rows,cols],preferred_element_type=F32)
            probs=jnp.exp(scores+bias_ref[0:keys,:]-lse_ref[h,:,cols])
            dv_ref[g,0:keys,:]+=jnp.dot(probs.astype(BF),gn_ref[h,cols,:],preferred_element_type=F32)
            gp=jnp.dot(v_ref[g,0:keys,:],gm_ref[rows,cols],preferred_element_type=F32)
            weighted=probs*gp
            centre=jnp.sum(weighted,0,keepdims=True)
            gs=(weighted-probs*centre).astype(BF)
            dk_ref[g,0:keys,:]+=jnp.dot(gs,qn_ref[h,cols,:],preferred_element_type=F32)
            dq_ref[rows,cols]=0.125*jnp.dot(kt_ref[grows,0:keys],gs,preferred_element_type=F32)
            return 0
        lax.fori_loop(0,heads,head,0)
        if start>0: tick()
    def back(h,_):
        rows=pl.ds(pl.multiple_of(h*HD,HD),HD)
        turn_ref[rows,:]=turn_t(dq_ref[rows,:],cosine,sine,-1.0).astype(BF)
        return 0
    lax.fori_loop(0,heads,back,0)
    dk=jnp.concatenate([dk_ref[g] for g in range(groups)],1).T
    dv=jnp.concatenate([dv_ref[g] for g in range(groups)],1).T
    for g in range(groups):
        turn_ref[(heads+g)*HD:(heads+g+1)*HD,:]=turn_t(dk[g*HD:(g+1)*HD],cosine,sine,-1.0).astype(BF)
    turn_ref[(heads+groups)*HD:,:]=dv.astype(BF)
    late[1].wait()
    sweep.end_sums()
    for c in range(0,width,strip):
        product=lax.dot_general(turn_ref[...],mix_ref[c:c+strip,:],(((0,),(1,)),((),())),preferred_element_type=F32).astype(BF)
        for j in range(count): part_ref[j,:,c:c+strip]=product[j*rows:(j+1)*rows]
    give=pltpu.make_async_copy(part_ref,part_hbm,cs.at[0])
    give.start()
    tick()
    third.wait()
    for k,c in enumerate(range(0,width,strip)):
        grad_ref[c:c+strip,0:lines]=lax.dot_general(normed_ref[:,:,c:c+strip].reshape(length,strip),turn_ref[...],(((0,),(1,)),((),())),preferred_element_type=F32).astype(BF)
        pltpu.make_async_copy(grad_ref.at[c:c+strip],grad_hbm.at[c:c+strip],gs_sem.at[k]).start()
    tick(line.far_steps())
    line.end_sums()
    sweep.end_pieces()
    give.wait()
    for k,c in enumerate(range(0,width,strip)):
        pltpu.make_async_copy(grad_ref.at[c:c+strip],grad_hbm.at[c:c+strip],gs_sem.at[k]).wait()

def attend_back(grads,two,grad_out,gain,w_out,q,kt,k,v,lse,cosine,sine,segments,down,residual,early,mixed,normed,mix,heads,groups,cid,pieces,fine,count):
    rows,width=residual.shape
    length=rows*count
    lines=mix.shape[1]
    block=min(256,length)
    vm=pl.BlockSpec(memory_space=pltpu.VMEM)
    hbm=pl.BlockSpec(memory_space=pl.ANY)
    vmem=pltpu.VMEM
    sds=jax.ShapeDtypeStruct
    sem=pltpu.SemaphoreType.DMA
    cut=lambda x: x.reshape(count,rows,width)
    return pl.pallas_call(functools.partial(attend_back_kernel,heads,groups,block,count,pieces,fine),
        out_shape=(sds((rows,width),F32),sds((8,width),F32),sds((count,rows,width),BF),sds((width,lines+heads*HD),BF),sds((rows,width),BF)),
        in_specs=[hbm,hbm,vm,vm,hbm]+[vm]*12+[hbm]*3,out_specs=(vm,vm,hbm,hbm,vm),
        scratch_shapes=[vmem((count,rows,width),BF),vmem((count,rows,width),BF),vmem((count,rows,width),BF),vmem((count+1,rows,width),BF),
            vmem((rows//fine,width),F32),sem((2,count,fine)),sem((2,count,fine)),sem((2,count,fine)),sem((2,count,fine)),
            vmem(w_out.shape,BF),vmem(mixed.shape,BF),vmem(mix.shape,BF),vmem((lines,length),BF),vmem((heads*HD,length),BF),
            vmem((length,block),F32),vmem((heads,length,HD),BF),vmem((heads,length,HD),BF),
            vmem((heads*HD,length),F32),vmem((groups,length,HD),F32),vmem((groups,length,HD),F32),
            vmem((count+1,rows//2,width),BF),vmem((rows//2//pieces,width),F32),sem((2,count,pieces)),sem((2,count,pieces)),
            vmem((width,lines+heads*HD),BF),sem((5,)),sem((max(1,width//min(512,width)),))],
        cost_estimate=pl.CostEstimate(flops=60_000_000_000,bytes_accessed=550_000_000,transcendentals=8_000_000),
        compiler_params=pltpu.CompilerParams(collective_id=cid,has_side_effects=True,vmem_limit_bytes=60*1024*1024),
    )(cut(grads),cut(two),grad_out,gain,w_out,q,kt,k,v,lse,cosine,sine,segments.reshape(length,1),segments.reshape(1,length),down,residual,early,mixed,cut(normed),mix)


AXIS="tensor"
DP="dp"
MESH=pl.DeviceIdType.MESH

def greet(here, count, plane=0):
    barrier=pltpu.get_barrier_semaphore()
    if plane:
        def call(k,_):
            pl.semaphore_signal(barrier,inc=1,device_id={DP:lax.rem(lax.axis_index(DP)+k,plane)},device_id_type=MESH)
            return 0
        lax.fori_loop(1,plane,call,0)
        for k in range(1,count):
            pl.semaphore_signal(barrier,inc=1,device_id={AXIS:lax.rem(here+k,count)},device_id_type=MESH)
        pl.semaphore_wait(barrier,plane+count-2)
    else:
        @pl.when(here>0)
        def _(): pl.semaphore_signal(barrier,inc=1,device_id={AXIS:here-1},device_id_type=MESH)
        @pl.when(here<count-1)
        def _(): pl.semaphore_signal(barrier,inc=1,device_id={AXIS:here+1},device_id_type=MESH)
        pl.semaphore_wait(barrier,jnp.where((here>0)&(here<count-1),2,1))

def swap(axis, count, source, landing, sends, recvs):
    me=lax.axis_index(axis)
    def copy(peer, slot, k):
        return pltpu.make_async_remote_copy(src_ref=source(peer),dst_ref=landing.at[slot],send_sem=sends.at[k],
            recv_sem=recvs.at[slot],device_id={axis:peer},device_id_type=MESH)
    def begin(k,_):
        copy(lax.rem(me+k,count),me,k).start()
        return 0
    def end(k,_):
        peer=lax.rem(me+k,count)
        copy(peer,peer,k).wait_recv()
        copy(peer,me,k).wait_send()
        return 0
    return (lambda: lax.fori_loop(1,count,begin,0)),(lambda: lax.fori_loop(1,count,end,0))

def remote(src,dst,send,recv,target):
    return pltpu.make_async_remote_copy(src_ref=src,dst_ref=dst,send_sem=send,recv_sem=recv,
        device_id={AXIS:target},device_id_type=MESH)

class Line:
    def __init__(self,count,pieces,rows,part=None,sums=None,sum_sems=None,held=None,held_sems=None,base=0,sub=None):
        self.n,self.pieces,self.rows=count,pieces,rows
        self.sub=rows//pieces if sub is None else sub
        self.base=base
        self.here=lax.axis_index(AXIS)
        self.part,self.sums,self.sum_sems=part,sums,sum_sems
        self.held,self.held_sems=held,held_sems
    def span(self,u): return pl.ds(pl.multiple_of(self.base+u*self.sub,self.sub),self.sub)
    def fits(self,u): return (u>=0)&(u<self.pieces)
    def _target(self,way):
        return lax.min(self.here+1,self.n-1) if way==0 else lax.max(self.here-1,0)
    def slot(self,way,j,device):
        return j if way==0 else jnp.where(j==device,self.n,j)
    def sum_copy(self,way,j,u,first):
        sends,recvs=self.sum_sems
        dst=self.sums.at[self.slot(way,j,self._target(way)),self.span(u)]
        src=self.part.at[j,self.span(u)] if first else self.sums.at[self.slot(way,j,self.here),self.span(u)]
        return remote(src,dst,sends.at[way,j,u],recvs.at[way,j,u],self._target(way))
    def sum_arrival(self,way,j,u):
        sends,recvs=self.sum_sems
        ref=self.sums.at[self.slot(way,j,self.here),self.span(u)]
        return remote(ref,ref,sends.at[way,j,u],recvs.at[way,j,u],self._target(way))
    def relay(self,way,j,u,begins,passes):
        @pl.when(begins)
        def _(): self.sum_copy(way,j,u,True).start()
        @pl.when(passes)
        def _():
            self.sum_arrival(way,j,u).wait_recv()
            ref=self.sums.at[j,self.span(u)]
            ref[...]=(ref[...].astype(F32)+self.part[j,self.span(u)].astype(F32)).astype(BF)
            self.sum_copy(way,j,u,False).start()
    def far_steps(self): return (self.n-1)*self.pieces+1
    def far_step(self,t,total,finish):
        here,n,S=self.here,self.n,self.pieces
        for way in (0,1):
            q=t-here if way==0 else t-(n-1-here)
            ok=(q>=0)&(q<S*(n-1-here if way==0 else here))
            q=jnp.clip(q,0,S*(n-1)-1)
            j=n-1-q//S if way==0 else q//S
            end=(here==0) if way==0 else (here==n-1)
            self.relay(way,j,q%S,ok&end,ok&jnp.logical_not(end))
        u=t-(n-2)*S-1
        @pl.when(self.fits(u))
        def _():
            self.own_sum(u,total)
            finish(self.span(u),total)
    def send_sums(self,t):
        here,n=self.here,self.n
        for k in range(n-1):
            for way,j in ((0,n-1-k),(1,k)):
                u=t-here-(n-1-j) if way==0 else t-(n-1-here)-j
                ok=self.fits(u)
                u=jnp.clip(u,0,self.pieces-1)
                begins=(here==0) if way==0 else (here==n-1)
                passes=((here>0)&(here<j)) if way==0 else ((here<n-1)&(here>j))
                self.relay(way,j,u,ok&begins,ok&passes)
    def sweep_steps(self): return self.pieces+2*(self.n-1)
    def sweep(self,t,total,finish):
        far=self.n-1
        self.send_sums(t)
        self.pass_pieces(t-far)
        u=t-far
        @pl.when(self.fits(u))
        def _():
            self.own_sum(u,total)
            self.held[self.here,self.span(u)]=finish(self.span(u),total)
            self.send_own(u)
    def own_sum(self,u,total):
        here,n=self.here,self.n
        total[...]=self.part[here,self.span(u)].astype(F32)
        for way in (0,1):
            @pl.when(here>0 if way==0 else here<n-1)
            def _():
                self.sum_arrival(way,here,u).wait_recv()
                total[...]+=self.sums[self.slot(way,here,here),self.span(u)].astype(F32)
    def end_sums(self):
        here,n=self.here,self.n
        def one(u,_):
            for k in range(n-1):
                for way,j in ((0,n-1-k),(1,k)):
                    @pl.when((here<j) if way==0 else (here>j))
                    def _(): self.sum_copy(way,j,u,False).wait_send()
            return 0
        lax.fori_loop(0,self.pieces,one,0)
    def piece_copy(self,way,c,u,src=None):
        sends,recvs=self.held_sems
        dst=self.held.at[c,self.span(u)]
        return remote(dst if src is None else src,dst,sends.at[way,c,u],recvs.at[way,c,u],self._target(way))
    def send_own(self,u,src=None):
        here,n=self.here,self.n
        for way in (0,1):
            @pl.when(here<n-1 if way==0 else here>0)
            def _(): self.piece_copy(way,here,u,src).start()
    def pass_pieces(self,t,use=None):
        here,n=self.here,self.n
        for k in range(1,n):
            u=t-k
            ok=self.fits(u)
            u=jnp.clip(u,0,self.pieces-1)
            for way in (0,1):
                c=here-k if way==0 else here+k
                there=ok&((c>=0) if way==0 else (c<n))
                c=jnp.clip(c,0,n-1)
                @pl.when(there)
                def _(): self.piece_copy(way,c,u).wait_recv()
                @pl.when(there&(here<n-1 if way==0 else here>0))
                def _(): self.piece_copy(way,c,u).start()
                if use is not None:
                    @pl.when(there)
                    def _(): use(c,u)
    def end_pieces(self):
        here,n=self.here,self.n
        def one(u,_):
            for k in range(n):
                for way in (0,1):
                    c=here-k if way==0 else here+k
                    there=(c>=0) if way==0 else (c<n)
                    c=jnp.clip(c,0,n-1)
                    @pl.when(there&(here<n-1 if way==0 else here>0))
                    def _(): self.piece_copy(way,c,u).wait_send()
            return 0
        lax.fori_loop(0,self.pieces,one,0)

def gain_terms(part,other,acc,c):
    rows=part.shape[1]
    def some(k,_):
        span=pl.ds(pl.multiple_of(k*16,16),16)
        both=part[c,span].astype(F32)*other[c,span].astype(F32)
        acc[...]+=both[:8]+both[8:]
        return 0
    lax.fori_loop(0,rows//16,some,0)

def last_kernel(count, plane, pieces, part, other, tokens, grads, gain, terms, out, shared, sums, total, ss, sr, acc, cut, landed, level, stacked, ds, dr, zs, zr):
    width=part.shape[2]
    line=Line(count,pieces,part.shape[1],part,sums,(ss,sr))
    greet(line.here,count,plane)
    acc[...]=jnp.zeros_like(acc)
    me=lax.axis_index(DP)
    piece=width//plane
    begin_dp,end_dp=swap(DP,plane,lambda p: cut.at[p],landed,ds,dr)
    begin_z,end_z=swap(AXIS,count,lambda p: level,stacked,zs,zr)
    def finish(span,total):
        stream=tokens[span,:].astype(F32)
        scale=lax.rsqrt(jnp.mean(stream*stream,-1,keepdims=True)+EPSILON)
        unit=stream*scale
        scaled=total[...]*gain[...]
        out[span,:]=grads[span,:]+scale*(scaled-unit*jnp.mean(scaled*unit,-1,keepdims=True))
    def step(t,_):
        line.far_step(t,total,finish)
        @pl.when(t<count)
        def _(): gain_terms(part,other,acc,jnp.clip(t,0,count-1))
        @pl.when(t==count-1)
        def _():
            for p in range(plane):
                cut[p,0:8,:]=acc[:,p*piece:(p+1)*piece]
                cut[p,8:16,:]=terms[:,p*piece:(p+1)*piece]
            landed[me]=cut[me]
            begin_dp()
        @pl.when(t==count+1)
        def _():
            end_dp()
            level[...]=jnp.sum(landed[...],0)
            stacked[line.here]=level[...]
            begin_z()
        return 0
    assert line.far_steps()>count+1
    lax.fori_loop(0,line.far_steps(),step,0)
    end_z()
    shared[...]=jnp.sum(stacked[...],0)
    line.end_sums()

def last_sums(part,other,tokens,grads,gain,terms,cid,pieces,n,plane):
    rows,D=tokens.shape
    vm=pl.BlockSpec(memory_space=pltpu.VMEM)
    sds=jax.ShapeDtypeStruct
    sem=pltpu.SemaphoreType.DMA
    w=D//plane
    return pl.pallas_call(functools.partial(last_kernel,n,plane,pieces),
        out_shape=(sds((rows,D),F32),sds((16,w),F32)),in_specs=[vm]*6,out_specs=(vm,vm),
        scratch_shapes=[pltpu.VMEM((n+1,rows,D),BF),pltpu.VMEM((rows//pieces,D),F32),sem((2,n,pieces)),sem((2,n,pieces)),pltpu.VMEM((8,D),F32),
            pltpu.VMEM((plane,16,w),F32),pltpu.VMEM((plane,16,w),F32),pltpu.VMEM((16,w),F32),pltpu.VMEM((n,16,w),F32),
            sem((plane,)),sem((plane,)),sem((n,)),sem((n,))],
        cost_estimate=pl.CostEstimate(flops=0,bytes_accessed=270_000_000,transcendentals=0),
        compiler_params=pltpu.CompilerParams(collective_id=cid,has_side_effects=True,vmem_limit_bytes=56*1024*1024),
    )(part.reshape(n,rows,D),other.reshape(n,rows,D),tokens,grads,gain,terms)


def mlp_kernel(count,pieces,tile,x_ref,grad_ref,res_ref,early_hbm,wg_hbm,wu_hbm,wd_hbm,
        part_ref,wide_ref,out_ref,rest_hbm,gr,product,gated,lifted,down,ring,tall,sums,total,hs,hr,ss,sr,ws,ts,ls,rs):
    s=pl.program_id(0)
    length,hidden=product.shape
    width=x_ref.shape[1]
    rows=grad_ref.shape[0]
    half=rows//2
    first,second=hidden//tile,width//tile
    slots=ring.shape[0]
    at_down=first; at_grad=first+second; at_part=2*first+second; at_weight=2*first+2*second
    spread=pieces
    get=Line(count,spread,rows,held=gr,held_sems=(hs,hr),base=half,sub=half//spread)
    line=Line(count,pieces,rows,down,sums,(ss,sr),sub=half//pieces)
    def rest(c): return pltpu.make_async_copy(down.at[c,pl.ds(half,half)],rest_hbm.at[c],rs.at[c])
    def strip(k,size): return pl.ds(pl.multiple_of(jnp.clip(k,0,size-1)*tile,tile),tile)
    def tall_load(k):
        slot=lax.rem(k,slots)
        @pl.when((k<2*first)&(lax.rem(k,2)==0))
        def _(): pltpu.make_async_copy(wg_hbm.at[:,strip(k//2,first)],tall.at[slot],ts.at[slot]).start()
        @pl.when((k<2*first)&(lax.rem(k,2)==1))
        def _(): pltpu.make_async_copy(wu_hbm.at[:,strip(k//2,first)],tall.at[slot],ts.at[slot]).start()
        @pl.when((k>=2*first)&(k<2*first+second))
        def _(): pltpu.make_async_copy(wd_hbm.at[:,strip(k-2*first,second)],tall.at[slot],ts.at[slot]).start()
    def tall_loaded(k):
        slot=lax.rem(k,slots)
        pltpu.make_async_copy(wg_hbm.at[:,pl.ds(0,tile)],tall.at[slot],ts.at[slot]).wait()
        return slot
    def load(k):
        slot=lax.rem(k,slots)
        late=strip((k-first)//2,second)
        @pl.when(k<first)
        def _(): pltpu.make_async_copy(wd_hbm.at[strip(k,first),:],ring.at[slot],ws.at[slot]).start()
        @pl.when((k>=first)&(lax.rem(k-first,2)==0)&(k<first+2*second))
        def _(): pltpu.make_async_copy(wg_hbm.at[late,:],ring.at[slot],ws.at[slot]).start()
        @pl.when((k>=first)&(lax.rem(k-first,2)==1)&(k<first+2*second))
        def _(): pltpu.make_async_copy(wu_hbm.at[late,:],ring.at[slot],ws.at[slot]).start()
    def loaded(k):
        slot=lax.rem(k,slots)
        pltpu.make_async_copy(wd_hbm.at[pl.ds(0,tile),:],ring.at[slot],ws.at[slot]).wait()
        return slot
    def own(): return pltpu.make_async_copy(grad_ref,gr.at[get.here],ls.at[0])
    def early(c): return pltpu.make_async_copy(early_hbm.at[c],gr.at[c,pl.ds(0,half)],ls.at[1+c])
    @pl.when(s==0)
    def _():
        for k in range(slots): tall_load(k)
        greet(get.here,count)
        for u in range(spread):
            get.send_own(u,grad_ref.at[get.span(u),:])
        own().start()
        for c in range(count):
            @pl.when(c!=get.here)
            def _(): early(c).start()
    @pl.when(s==at_down-1)
    def _():
        for k in range(slots): load(k)
    hops=spread+count-2
    gap=max(1,at_grad//hops)
    @pl.when((s>0)&(lax.rem(s,gap)==0)&(s<=gap*hops))
    def _(): get.pass_pieces(s//gap)
    @pl.when(s==at_grad)
    def _():
        own().wait()
        for c in range(count):
            @pl.when(c!=get.here)
            def _(): early(c).wait()
    def finish(span,total):
        out_ref[span,:]=(res_ref[span,:]+total[...]).astype(BF)
    r=s-at_grad
    t=jnp.int32(-1)
    marks=(0,2,4,5,6,7,12) if first==4 and second==4 else tuple(range(line.far_steps()))
    for k,mark in enumerate(marks): t=jnp.where(r==mark,k,t)
    @pl.when(t>=0)
    def _(): line.far_step(t,total,finish)
    @pl.when(r==0)
    def _():
        for c in range(count): rest(c).start()
    @pl.when(s<at_down)
    def _():
        one=tall_loaded(2*s)
        two=tall_loaded(2*s+1)
        cols=strip(s,first)
        for c in range(count):
            span=slice(c*rows,(c+1)*rows)
            gate=jnp.dot(x_ref[span,:],tall[one],preferred_element_type=F32)
            up=jnp.dot(x_ref[span,:],tall[two],preferred_element_type=F32)
            sigmoid=1.0/(1.0+jnp.exp(-gate))
            active=gate*sigmoid
            product[span,cols]=(active*up).astype(BF)
            lifted[span,cols]=active.astype(BF)
            gated[span,cols]=(up*(sigmoid+active*(1.0-sigmoid))).astype(BF)
        tall_load(2*s+slots)
        tall_load(2*s+1+slots)
    @pl.when((s>=at_down)&(s<at_grad))
    def _():
        k=2*first+s-at_down
        slot=tall_loaded(k)
        sums_here=jnp.dot(product[...],tall[slot],preferred_element_type=F32).astype(BF)
        cols=strip(s-at_down,second)
        for c in range(count): down[c,:,cols]=sums_here[c*rows:(c+1)*rows]
        tall_load(k+slots)
    @pl.when((s>=at_grad)&(s<at_part))
    def _():
        k=s-at_grad
        slot=loaded(k)
        cols=strip(k,first)
        for c in range(count):
            span=slice(c*rows,(c+1)*rows)
            grads=lax.dot_general(gr[c],ring[slot],(((1,),(1,)),((),())),preferred_element_type=F32)
            gated[span,cols]=(grads*gated[span,cols].astype(F32)).astype(BF)
            lifted[span,cols]=(grads*lifted[span,cols].astype(F32)).astype(BF)
        load(k+slots)
    @pl.when((s>=at_part)&(s<at_weight))
    def _():
        k=first+2*(s-at_part)
        one=loaded(k)
        both=lax.dot_general(gated[...],ring[one],(((1,),(1,)),((),())),preferred_element_type=F32)
        load(k+slots)
        two=loaded(k+1)
        both=both+lax.dot_general(lifted[...],ring[two],(((1,),(1,)),((),())),preferred_element_type=F32)
        part_ref[...]=both.astype(BF)
        load(k+1+slots)
    last=s-at_weight
    cols=strip(last//6,second)
    kind=lax.rem(last,6)
    cut=hidden//2
    def weight(left,right):
        wide_ref[...]=lax.dot_general(left,right,(((0,),(0,)),((),())),preferred_element_type=F32).astype(BF)
    for side in (0,1):
        these=slice(side*cut,(side+1)*cut)
        @pl.when((last>=0)&(kind==side))
        def _(): weight(x_ref[:,cols],gated[:,these])
        @pl.when((last>=0)&(kind==2+side))
        def _(): weight(x_ref[:,cols],lifted[:,these])
        @pl.when((last>=0)&(kind==4+side))
        def _(): weight(gr[:,:,cols].reshape(length,tile),product[:,these])
    @pl.when(s==at_weight+6*second-1)
    def _():
        get.end_pieces()
        line.end_sums()
        for c in range(count): rest(c).wait()

def mlp(x,grad_out,residual,early,w_gate,w_up,w_down,cid,pieces,count):
    length,width=x.shape
    hidden=w_gate.shape[1]
    rows=length//count
    tile=min(512,hidden,width)
    first,second=hidden//tile,width//tile
    steps=2*first+8*second
    assert first!=4 or second!=4 or (count-1)*pieces+1==7
    assert first+7*second>=(count-1)*pieces+1
    whole=lambda shape: pl.BlockSpec(shape,lambda s: (0,)*len(shape),pipeline_mode=pl.Buffered(1))
    hbm=pl.BlockSpec(memory_space=pl.ANY)
    sds=jax.ShapeDtypeStruct
    sem=pltpu.SemaphoreType.DMA
    at_part=2*first+second
    def wide_map(s):
        k=jnp.maximum(s-at_part-second,0)
        return (k//6,k%6)
    vmem=pltpu.VMEM
    spread=pieces
    return pl.pallas_call(functools.partial(mlp_kernel,count,pieces,tile),
        grid=(steps,),
        out_shape=(sds((length,width),BF),sds((width,3*hidden),BF),sds((rows//2,width),BF),sds((count,rows//2,width),BF)),
        in_specs=[whole((length,width)),whole((rows,width)),pl.BlockSpec((rows//2,width),lambda s: (0,0),pipeline_mode=pl.Buffered(1)),hbm,hbm,hbm,hbm],
        out_specs=(pl.BlockSpec((length,tile),lambda s: (0,jnp.clip(s-at_part,0,second-1))),
            pl.BlockSpec((tile,hidden//2),wide_map),whole((rows//2,width)),hbm),
        scratch_shapes=[vmem((count,rows,width),BF),vmem((length,hidden),BF),vmem((length,hidden),BF),vmem((length,hidden),BF),
            vmem((count,rows,width),BF),vmem((4,tile,width),BF),vmem((4,width,tile),BF),vmem((count+1,rows//2,width),BF),vmem((rows//2//pieces,width),F32),
            sem((2,count,spread)),sem((2,count,spread)),sem((2,count,pieces)),sem((2,count,pieces)),sem((4,)),sem((4,)),sem((count+1,)),sem((count,))],
        cost_estimate=pl.CostEstimate(flops=78_000_000_000,bytes_accessed=380_000_000,transcendentals=0),
        compiler_params=pltpu.CompilerParams(collective_id=cid,has_side_effects=True,vmem_limit_bytes=60*1024*1024,
            dimension_semantics=("arbitrary",)),
    )(x,grad_out,residual,early,w_gate,w_up,w_down)


def frequencies(head_size):
    inverse = 1.0 / 500000.0 ** (jnp.arange(head_size // 2, dtype=jnp.float32) * 2.0 / head_size)
    wavelength = 2.0 * math.pi / inverse
    smooth = (8192.0 / wavelength - 1.0) / 3.0
    blended = (1.0 - smooth) * inverse / 32.0 + smooth * inverse
    return jnp.where(
        wavelength > 8192.0, inverse / 32.0, jnp.where(wavelength < 2048.0, inverse, blended)
    )


def dot(left_side, right_side, left_dim, right_dim):
    return lax.dot_general(
        left_side, right_side, (((left_dim,), (right_dim,)), ((), ())), preferred_element_type=F32
    )


def norm_kernel(count, plane, pieces, tokens_ref, gains_ref, normed, gains_out, held, landed, hs, hr, ds, dr):
    line = Line(count, pieces, tokens_ref.shape[0], held=held, held_sems=(hs, hr))
    greet(line.here, count, plane)
    me = lax.axis_index(DP)
    begin, end = swap(DP, plane, lambda p: gains_ref, landed, ds, dr)
    for u in range(pieces):
        line.send_own(u, tokens_ref.at[line.span(u), :])
    begin()
    landed[me] = gains_ref[...]
    end()
    piece = gains_ref.shape[1]
    for p in range(plane):
        gains_out[:, p * piece : (p + 1) * piece] = landed[p]

    def norm(rows, c, u):
        stream = rows.astype(F32)
        scale = lax.rsqrt(jnp.mean(stream * stream, -1, keepdims=True) + EPSILON)
        normed[c, line.span(u)] = (stream * scale * gains_out[0:1, :]).astype(BF)

    def step(t, _):
        line.pass_pieces(t, lambda c, u: norm(held[c, line.span(u)], c, u))

        @pl.when(t < pieces)
        def _():
            u = jnp.clip(t, 0, pieces - 1)
            norm(tokens_ref[line.span(u), :], line.here, u)

        return 0

    lax.fori_loop(0, pieces + count - 1, step, 0)
    line.end_pieces()


def norm_and_gather(tokens, gains, cid, pieces, count, plane):
    rows, width = tokens.shape
    vm = pl.BlockSpec(memory_space=pltpu.VMEM)
    sem = pltpu.SemaphoreType.DMA
    normed, gains = pl.pallas_call(
        functools.partial(norm_kernel, count, plane, pieces),
        out_shape=(jax.ShapeDtypeStruct((count, rows, width), BF), jax.ShapeDtypeStruct((8, width), F32)),
        in_specs=[vm, vm],
        out_specs=(vm, vm),
        scratch_shapes=[
            pltpu.VMEM((count, rows, width), BF),
            pltpu.VMEM((plane, 8, width // plane), F32),
            sem((2, count, pieces)),
            sem((2, count, pieces)),
            sem((plane,)),
            sem((plane,)),
        ],
        cost_estimate=pl.CostEstimate(flops=0, bytes_accessed=270_000_000, transcendentals=0),
        compiler_params=pltpu.CompilerParams(
            collective_id=cid, has_side_effects=True, vmem_limit_bytes=40 * 1024 * 1024
        ),
    )(tokens, gains)
    return normed.reshape(count * rows, width), gains


def results_kernel(gate_in, up_in, down_in, mix_ref, gate, up, down, query, key, value, out):
    gate[...] = gate_in[...].astype(F32)
    up[...] = up_in[...].astype(F32)
    down[...] = down_in[...].astype(F32).T
    query[...] = mix_ref[:, : query.shape[1]].astype(F32)
    edge = query.shape[1]
    key[...] = mix_ref[:, edge : edge + key.shape[1]].astype(F32)
    edge += key.shape[1]
    value[...] = mix_ref[:, edge : edge + value.shape[1]].astype(F32)
    edge += value.shape[1]
    out[...] = mix_ref[:, edge:].astype(F32).T


def results(wide, mix, hidden, deep, narrow):
    shard = wide.shape[0]
    tile = min(512, hidden)
    steps = hidden // tile
    sds = jax.ShapeDtypeStruct
    still = lambda shape: pl.BlockSpec(shape, lambda s: (0, 0))
    return pl.pallas_call(
        results_kernel,
        grid=(steps,),
        out_shape=(
            sds((shard, hidden), F32),
            sds((shard, hidden), F32),
            sds((hidden, shard), F32),
            sds((shard, deep), F32),
            sds((shard, narrow), F32),
            sds((shard, narrow), F32),
            sds((deep, shard), F32),
        ),
        in_specs=[pl.BlockSpec((shard, tile), lambda s, k=k: (0, k * steps + s)) for k in range(3)] + [still(mix.shape)],
        out_specs=(
            pl.BlockSpec((shard, tile), lambda s: (0, s)),
            pl.BlockSpec((shard, tile), lambda s: (0, s)),
            pl.BlockSpec((tile, shard), lambda s: (s, 0)),
            still((shard, deep)),
            still((shard, narrow)),
            still((shard, narrow)),
            still((deep, shard)),
        ),
        compiler_params=pltpu.CompilerParams(vmem_limit_bytes=32 * 1024 * 1024),
    )(wide, wide, wide, mix)


def body(
    count,
    plane,
    tokens,
    segments,
    positions,
    attn_gain,
    w_query,
    w_key,
    w_value,
    w_out,
    mlp_gain,
    w_gate,
    w_up,
    w_down,
    grad_out,
):
    rows, width = tokens.shape
    heads = w_query.shape[1] // HD
    groups = w_key.shape[1] // HD
    after = lax.optimization_barrier
    mix = lax.all_gather(jnp.concatenate([w_query, w_key, w_value], 1), DP, axis=0, tiled=True)
    full_out = lax.all_gather(w_out, DP, axis=1, tiled=True)
    full_gate = lax.all_gather(w_gate, DP, axis=0, tiled=True)
    full_up = lax.all_gather(w_up, DP, axis=0, tiled=True)
    full_down = lax.all_gather(w_down, DP, axis=1, tiled=True)
    gains = jnp.concatenate([jnp.stack([attn_gain, mlp_gain]).astype(F32), jnp.zeros((6, attn_gain.shape[0]), F32)])

    normed_one, gains = norm_and_gather(tokens, gains, 1, 4, count, plane)
    gain_one, gain_two = gains[0:1], gains[1:2]
    angles = frequencies(HD)[:, None] * positions.astype(F32)[None, :]
    cosine, sine = jnp.cos(angles), jnp.sin(angles)

    mixed, lse, q, kt, k, v, residual, early, normed_two = attend(
        mix, normed_one, cosine, sine, segments, full_out, grad_out, tokens, gain_two, heads, groups, 6, 2, 16, count
    )
    normed_two = normed_two.reshape(count * rows, width)
    part, grad_wide, block_early, down = mlp(normed_two, grad_out, residual, early, full_gate, full_up, full_down, 5, 2, count)
    grad_wide = lax.psum_scatter(grad_wide, DP, scatter_dimension=0, tiled=True)
    grad_residual, terms_two, part, grad_mix, block_out = attend_back(
        part, normed_two, grad_out, gain_two, full_out, q, kt, k, v, lse, cosine, sine, segments, down, residual, block_early,
        mixed, normed_one, mix, heads, groups, 7, 2, 16, count,
    )
    part, grad_mix, grad_wide = after((part, grad_mix, grad_wide))
    grad_mix = lax.psum_scatter(grad_mix, DP, scatter_dimension=0, tiled=True)
    grad_tokens, sums = last_sums(part, normed_one, tokens, grad_residual, gain_one, terms_two, 4, 4, count, plane)
    sums = jnp.sum(sums.reshape(2, 8, -1), 1)
    grad_gate, grad_up, grad_down, grad_query, grad_key, grad_value, grad_out_proj = results(
        grad_wide, grad_mix, full_gate.shape[1], heads * HD, groups * HD
    )
    return (
        block_out,
        grad_tokens,
        sums[0] / attn_gain.astype(F32),
        grad_query,
        grad_key,
        grad_value,
        grad_out_proj,
        sums[1] / mlp_gain.astype(F32),
        grad_gate,
        grad_up,
        grad_down,
    )


def solution(mesh):
    placed = (
        P(("dp", "tensor"), None),
        P("dp"),
        P("dp"),
        P("dp"),
        P("dp", "tensor"),
        P("dp", "tensor"),
        P("dp", "tensor"),
        P("tensor", "dp"),
        P("dp"),
        P("dp", "tensor"),
        P("dp", "tensor"),
        P("tensor", "dp"),
        P(("dp", "tensor"), None),
    )
    return jax.shard_map(
        functools.partial(body, mesh.shape["tensor"], mesh.shape["dp"]),
        mesh=mesh,
        in_specs=placed,
        out_specs=(
            P(("dp", "tensor"), None),
            P(("dp", "tensor"), None),
            P("dp"),
            P("dp", "tensor"),
            P("dp", "tensor"),
            P("dp", "tensor"),
            P("tensor", "dp"),
            P("dp"),
            P("dp", "tensor"),
            P("dp", "tensor"),
            P("tensor", "dp"),
        ),
        check_vma=False,
    )
```

```python
import functools
import math

import jax
import jax.numpy as jnp
from jax import lax
from jax.experimental import pallas as pl
from jax.experimental.pallas import tpu as pltpu
from jax.sharding import PartitionSpec as P

HD = 64
EPSILON = 1e-05
MASKED = -1e30
F32 = jnp.float32
BF = jnp.bfloat16

def turn_t(values, cosine, sine, sign):
    half=values.shape[0]//2
    first, second = values[:half], values[half:]
    return jnp.concatenate([first*cosine - sign*second*sine, second*cosine + sign*first*sine],0)

def column(row_ref):
    return jnp.broadcast_to(row_ref[...].astype(F32),(8,row_ref.shape[1])).T[:,0:1].astype(jnp.int32)

def block_bias(segs_col, segs_row, start, block):
    keys=start+block
    key_places=lax.broadcasted_iota(jnp.int32,(keys,block),0)
    query_places=start+lax.broadcasted_iota(jnp.int32,(keys,block),1)
    allowed=(key_places<=query_places)&(segs_col[0:keys,:]==segs_row[0:1,start:start+block])
    return jnp.where(allowed,0.0,MASKED).astype(F32)

def attend_kernel(heads, groups, block, count, pieces, fine, mix_hbm, normed_hbm, cos_ref, sin_ref, segr_ref, wo_hbm, grad_ref, tokens_hbm, gain_ref,
                  mixed_ref, lse_ref, q_ref, kt_ref, k_ref, v_ref, residual_ref, rows_hbm, whole_hbm,
                  mix_ref, normed_ref, lin_ref, bias_ref, vt_ref, wo_ref, tokens_ref, part_ref, held, hs, hr, sums, total, ss, sr, moved, ms, mr, cs):
    length=normed_ref.shape[0]
    per=heads//groups
    rows=grad_ref.shape[0]
    early=held.shape[1]
    line=Line(count,pieces,rows,held=held,held_sems=(hs,hr),sub=early//pieces)
    inputs=[pltpu.make_async_copy(s,d,cs.at[4+k]) for k,(s,d) in enumerate(((normed_hbm,normed_ref),(mix_hbm,mix_ref)))]
    for copy in inputs: copy.start()
    greet(line.here,count)
    line.gather_step(0,grad_ref)
    for copy in inputs: copy.wait()
    weights=pltpu.make_async_copy(wo_hbm,wo_ref,cs.at[0])
    weights.start()
    stream=pltpu.make_async_copy(tokens_hbm,tokens_ref,cs.at[1])
    stream.start()
    lines=mix_ref.shape[1]
    cut=256 if lines%256==0 else lines
    for c in range(0,lines,cut):
        lin_ref[c:c+cut,:]=lax.dot_general(mix_ref[:,c:c+cut],normed_ref[...],(((0,),(1,)),((),())),preferred_element_type=F32)
    steps=line.gather_steps()
    done=0
    def tick():
        nonlocal done
        if done+1<steps:
            done+=1
            line.gather_step(done,grad_ref)
    tick()
    cosine, sine = cos_ref[...], sin_ref[...]
    def rope(h,_):
        rows=pl.ds(pl.multiple_of(h*HD,HD),HD)
        q_ref[rows,:]=(turn_t(lin_ref[rows,:],cosine,sine,1.0).astype(BF)*jnp.asarray(0.125,BF))
        return 0
    lax.fori_loop(0,heads,rope,0)
    turned=[turn_t(lin_ref[(heads+g)*HD:(heads+g+1)*HD,:],cosine,sine,1.0) for g in range(groups)]
    keys_t=jnp.concatenate(turned,0)
    kt_ref[...]=keys_t.astype(BF)
    vals_t=lin_ref[(heads+groups)*HD:(heads+2*groups)*HD,:]
    vt_ref[...]=vals_t.astype(BF)
    keys_n=keys_t.T.astype(BF)
    vals_n=vals_t.T.astype(BF)
    for g in range(groups):
        k_ref[g]=keys_n[:,g*HD:(g+1)*HD]
        v_ref[g]=vals_n[:,g*HD:(g+1)*HD]
    segs_col=column(segr_ref)
    for start in range(0,length,block):
        keys=start+block
        if start in (block,3*block): tick()
        bias_ref[0:keys,:]=block_bias(segs_col,segr_ref,start,block)
        def head(h,_):
            g=h//per
            rows=pl.ds(pl.multiple_of(h*HD,HD),HD)
            grows=pl.ds(pl.multiple_of(g*HD,HD),HD)
            scores=jnp.dot(k_ref[g,0:keys,:],q_ref[rows,start:start+block],preferred_element_type=F32)
            scores=scores+bias_ref[0:keys,:]
            top=jnp.max(scores,0,keepdims=True)
            weights=jnp.exp(scores-top)
            total=jnp.sum(weights,0,keepdims=True)
            out=jnp.dot(vt_ref[grows,0:keys],weights.astype(BF),preferred_element_type=F32)
            mixed_ref[rows,start:start+block]=(out/total).astype(BF)
            lse_ref[h,:,start:start+block]=top+jnp.log(total)
            return 0
        lax.fori_loop(0,heads,head,0)
    width=wo_ref.shape[1]
    wide=min(512,width)
    weights.wait()
    tick()
    def out(c,_):
        cols=pl.ds(pl.multiple_of(c*wide,wide),wide)
        product=lax.dot_general(mixed_ref[...],wo_ref[:,cols],(((0,),(0,)),((),())),preferred_element_type=F32).astype(BF)
        for j in range(count): part_ref[j,:,cols]=product[j*rows:(j+1)*rows]
        return 0
    lax.fori_loop(0,width//wide,out,0)
    held[line.here]=grad_ref[0:early,:]
    copy=pltpu.make_async_copy(held,rows_hbm,cs.at[2])
    stream.wait()
    sweep=Line(count,fine,rows,part_ref,sums,(ss,sr),moved,(ms,mr))
    def finish(span,total):
        residual=total[...]+tokens_ref[span,:].astype(F32)
        residual_ref[span,:]=residual
        scale=lax.rsqrt(jnp.mean(residual*residual,-1,keepdims=True)+EPSILON)
        return (residual*scale*gain_ref[1:2,:]).astype(BF)
    def step(t,_):
        sweep.sweep(t,total,finish)
        for k in range(done+1,steps):
            @pl.when(t==2*(k-done-1))
            def _(): line.gather_step(k,grad_ref)
        return 0
    lax.fori_loop(0,sweep.sweep_steps(),step,0)
    copy.start()
    last=pltpu.make_async_copy(moved,whole_hbm,cs.at[3])
    last.start()
    line.end_pieces()
    sweep.end_sums()
    sweep.end_pieces()
    copy.wait()
    last.wait()

def attend(mix, normed, cosine, sine, segments, w_out, grad_out, tokens, gain, heads, groups, cid, early, pieces, fine, count):
    length,width=normed.shape
    rows=grad_out.shape[0]
    block=min(256,length)
    sds=jax.ShapeDtypeStruct
    vm=pl.BlockSpec(memory_space=pltpu.VMEM)
    hbm=pl.BlockSpec(memory_space=pl.ANY)
    sem=pltpu.SemaphoreType.DMA
    vmem=pltpu.VMEM
    return pl.pallas_call(functools.partial(attend_kernel,heads,groups,block,count,pieces,fine),
        out_shape=(sds((heads*HD,length),BF),sds((heads,1,length),F32),sds((heads*HD,length),BF),
            sds((groups*HD,length),BF),sds((groups,length,HD),BF),sds((groups,length,HD),BF),
            sds((rows,width),F32),sds((count,early,width),BF),sds((count,rows,width),BF)),
        in_specs=[hbm,hbm]+[vm]*3+[hbm,vm,hbm,vm],out_specs=(vm,)*7+(hbm,hbm),
        scratch_shapes=[vmem(mix.shape,BF),vmem(normed.shape,BF),vmem((mix.shape[1],length),F32),vmem((length,block),F32),vmem((groups*HD,length),BF),vmem(w_out.shape,BF),
            vmem(tokens.shape,BF),vmem((count,rows,width),BF),vmem((count,early,width),BF),sem((2,count,pieces)),sem((2,count,pieces)),
            vmem((count+1,rows,width),BF),vmem((rows//fine,width),F32),sem((2,count,fine)),sem((2,count,fine)),
            vmem((count,rows,width),BF),sem((2,count,fine)),sem((2,count,fine)),sem((6,))],
        cost_estimate=pl.CostEstimate(flops=30_000_000_000,bytes_accessed=500_000_000,transcendentals=8_000_000),
        compiler_params=pltpu.CompilerParams(collective_id=cid,has_side_effects=True,vmem_limit_bytes=58*1024*1024),
    )(mix,normed,cosine,sine,segments.reshape(1,length),w_out,grad_out,tokens,gain)

def attend_back_kernel(heads, groups, block, count, pieces, fine, grads_hbm, two_hbm, go_ref, gain_ref, wo_hbm, q_ref, kt_ref, k_ref, v_ref, lse_ref, cos_ref, sin_ref, segr_ref,
                  down_ref, res_ref, early_ref, mixed_hbm, normed_hbm, mix_hbm,
                  gres_ref, acc, part_hbm, grad_hbm, out_ref,
                  part_ref, normed_ref, low_ref, wide_sums, wide_total, ws, wr, hs, hr,
                  wo_ref, mixed_ref, mix_ref, turn_ref, gm_ref, bias_ref, qn_ref, gn_ref, dq_ref, dk_ref, dv_ref, sums, total, ss, sr, grad_ref, cs, gs_sem):
    length=q_ref.shape[1]
    per=heads//groups
    width=wo_ref.shape[1]
    rows=res_ref.shape[0]
    half=rows//2
    line=Line(count,pieces,half,down_ref,sums,(ss,sr))
    sweep=Line(count,fine,rows,part_ref,wide_sums,(ws,wr),low_ref,(hs,hr))
    first=pltpu.make_async_copy(grads_hbm,part_ref,cs.at[0])
    first.start()
    second=pltpu.make_async_copy(two_hbm,normed_ref,cs.at[1])
    second.start()
    late=[pltpu.make_async_copy(s,d,cs.at[2+k]) for k,(s,d) in enumerate(((mixed_hbm,mixed_ref),(mix_hbm,mix_ref),(wo_hbm,wo_ref)))]
    for copy in late: copy.start()
    greet(line.here,count)
    acc[...]=jnp.zeros_like(acc)
    out_ref[0:half,:]=early_ref[...]
    first.wait()
    def turn(span,total):
        residual=res_ref[span,:]
        scale=lax.rsqrt(jnp.mean(residual*residual,-1,keepdims=True)+EPSILON)
        unit=residual*scale
        scaled=total[...]*gain_ref[1:2,:]
        grads=go_ref[span,:].astype(F32)+scale*(scaled-unit*jnp.mean(scaled*unit,-1,keepdims=True))
        gres_ref[span,:]=grads
        return grads.astype(BF)
    def finish(span,total):
        places=pl.ds(pl.multiple_of(half+span.start,line.sub),line.sub)
        out_ref[places,:]=(res_ref[places,:]+total[...]).astype(BF)
    steps=sweep.sweep_steps()
    begun=2
    def step(t,_):
        sweep.sweep(t,wide_total,turn)
        @pl.when(t==2)
        def _(): second.wait()
        @pl.when((t>=2)&(t<count+2))
        def _(): gain_terms(part_ref,normed_ref,acc,jnp.clip(t-2,0,count-1))
        for k in range(begun):
            @pl.when(t==steps-2*(begun-k))
            def _(): line.far_step(jnp.int32(k),total,finish)
        return 0
    lax.fori_loop(0,steps,step,0)
    third=pltpu.make_async_copy(normed_hbm,normed_ref,cs.at[1])
    third.start()
    ticks=[begun]
    def tick(amount=1):
        for _ in range(amount):
            if ticks[0]<line.far_steps():
                line.far_step(jnp.int32(ticks[0]),total,finish)
                ticks[0]+=1
    late[2].wait()
    whole=lambda: low_ref[...].reshape(length,width)
    cosine, sine = cos_ref[...], sin_ref[...]
    deep=heads*HD
    cut=256 if deep%256==0 else deep
    for c in range(0,deep,cut):
        gm_ref[c:c+cut,:]=lax.dot_general(wo_ref[c:c+cut,:],whole(),(((1,),(1,)),((),())),preferred_element_type=F32).astype(BF)
    def flip(p,_):
        rows=pl.ds(pl.multiple_of(p*2*HD,2*HD),2*HD)
        qn=q_ref[rows,:].astype(F32).T.astype(BF)
        gn=gm_ref[rows,:].astype(F32).T.astype(BF)
        qn_ref[2*p]=qn[:,:HD]
        qn_ref[2*p+1]=qn[:,HD:]
        gn_ref[2*p]=gn[:,:HD]
        gn_ref[2*p+1]=gn[:,HD:]
        return 0
    lax.fori_loop(0,heads//2,flip,0)
    dk_ref[...]=jnp.zeros_like(dk_ref)
    dv_ref[...]=jnp.zeros_like(dv_ref)
    lines=(heads+2*groups)*HD
    strip=min(512,width)
    late[0].wait()
    tick()
    for c in range(0,width,strip):
        grad_ref[c:c+strip,lines:]=lax.dot_general(low_ref[:,:,c:c+strip].reshape(length,strip),mixed_ref[...],(((0,),(1,)),((),())),preferred_element_type=F32).astype(BF)
    segs_col=column(segr_ref)
    for start in range(0,length,block):
        keys=start+block
        cols=slice(start,start+block)
        bias_ref[0:keys,:]=block_bias(segs_col,segr_ref,start,block)
        def head(h,_):
            g=h//per
            rows=pl.ds(pl.multiple_of(h*HD,HD),HD)
            grows=pl.ds(pl.multiple_of(g*HD,HD),HD)
            scores=jnp.dot(k_ref[g,0:keys,:],q_ref[rows,cols],preferred_element_type=F32)
            probs=jnp.exp(scores+bias_ref[0:keys,:]-lse_ref[h,:,cols])
            dv_ref[g,0:keys,:]+=jnp.dot(probs.astype(BF),gn_ref[h,cols,:],preferred_element_type=F32)
            gp=jnp.dot(v_ref[g,0:keys,:],gm_ref[rows,cols],preferred_element_type=F32)
            weighted=probs*gp
            centre=jnp.sum(weighted,0,keepdims=True)
            gs=(weighted-probs*centre).astype(BF)
            dk_ref[g,0:keys,:]+=jnp.dot(gs,qn_ref[h,cols,:],preferred_element_type=F32)
            dq_ref[rows,cols]=0.125*jnp.dot(kt_ref[grows,0:keys],gs,preferred_element_type=F32)
            return 0
        lax.fori_loop(0,heads,head,0)
        if start>0: tick()
    def back(h,_):
        rows=pl.ds(pl.multiple_of(h*HD,HD),HD)
        turn_ref[rows,:]=turn_t(dq_ref[rows,:],cosine,sine,-1.0).astype(BF)
        return 0
    lax.fori_loop(0,heads,back,0)
    dk=jnp.concatenate([dk_ref[g] for g in range(groups)],1).T
    dv=jnp.concatenate([dv_ref[g] for g in range(groups)],1).T
    for g in range(groups):
        turn_ref[(heads+g)*HD:(heads+g+1)*HD,:]=turn_t(dk[g*HD:(g+1)*HD],cosine,sine,-1.0).astype(BF)
    turn_ref[(heads+groups)*HD:,:]=dv.astype(BF)
    late[1].wait()
    sweep.end_sums()
    for c in range(0,width,strip):
        product=lax.dot_general(turn_ref[...],mix_ref[c:c+strip,:],(((0,),(1,)),((),())),preferred_element_type=F32).astype(BF)
        for j in range(count): part_ref[j,:,c:c+strip]=product[j*rows:(j+1)*rows]
    give=pltpu.make_async_copy(part_ref,part_hbm,cs.at[0])
    give.start()
    tick()
    third.wait()
    for k,c in enumerate(range(0,width,strip)):
        grad_ref[c:c+strip,0:lines]=lax.dot_general(normed_ref[:,:,c:c+strip].reshape(length,strip),turn_ref[...],(((0,),(1,)),((),())),preferred_element_type=F32).astype(BF)
        pltpu.make_async_copy(grad_ref.at[c:c+strip],grad_hbm.at[c:c+strip],gs_sem.at[k]).start()
    tick(line.far_steps())
    line.end_sums()
    sweep.end_pieces()
    give.wait()
    for k,c in enumerate(range(0,width,strip)):
        pltpu.make_async_copy(grad_ref.at[c:c+strip],grad_hbm.at[c:c+strip],gs_sem.at[k]).wait()

def attend_back(grads,two,grad_out,gain,w_out,q,kt,k,v,lse,cosine,sine,segments,down,residual,early,mixed,normed,mix,heads,groups,cid,pieces,fine,count):
    rows,width=residual.shape
    length=rows*count
    lines=mix.shape[1]
    block=min(256,length)
    vm=pl.BlockSpec(memory_space=pltpu.VMEM)
    hbm=pl.BlockSpec(memory_space=pl.ANY)
    vmem=pltpu.VMEM
    sds=jax.ShapeDtypeStruct
    sem=pltpu.SemaphoreType.DMA
    cut=lambda x: x.reshape(count,rows,width)
    return pl.pallas_call(functools.partial(attend_back_kernel,heads,groups,block,count,pieces,fine),
        out_shape=(sds((rows,width),F32),sds((8,width),F32),sds((count,rows,width),BF),sds((width,lines+heads*HD),BF),sds((rows,width),BF)),
        in_specs=[hbm,hbm,vm,vm,hbm]+[vm]*11+[hbm]*3,out_specs=(vm,vm,hbm,hbm,vm),
        scratch_shapes=[vmem((count,rows,width),BF),vmem((count,rows,width),BF),vmem((count,rows,width),BF),vmem((count+1,rows,width),BF),
            vmem((rows//fine,width),F32),sem((2,count,fine)),sem((2,count,fine)),sem((2,count,fine)),sem((2,count,fine)),
            vmem(w_out.shape,BF),vmem(mixed.shape,BF),vmem(mix.shape,BF),vmem((lines,length),BF),vmem((heads*HD,length),BF),
            vmem((length,block),F32),vmem((heads,length,HD),BF),vmem((heads,length,HD),BF),
            vmem((heads*HD,length),F32),vmem((groups,length,HD),F32),vmem((groups,length,HD),F32),
            vmem((count+1,rows//2,width),BF),vmem((rows//2//pieces,width),F32),sem((2,count,pieces)),sem((2,count,pieces)),
            vmem((width,lines+heads*HD),BF),sem((5,)),sem((max(1,width//min(512,width)),))],
        cost_estimate=pl.CostEstimate(flops=60_000_000_000,bytes_accessed=550_000_000,transcendentals=8_000_000),
        compiler_params=pltpu.CompilerParams(collective_id=cid,has_side_effects=True,vmem_limit_bytes=60*1024*1024),
    )(cut(grads),cut(two),grad_out,gain,w_out,q,kt,k,v,lse,cosine,sine,segments.reshape(1,length),down,residual,early,mixed,cut(normed),mix)


AXIS="tensor"
DP="dp"
MESH=pl.DeviceIdType.MESH

def greet(here, count, plane=0):
    barrier=pltpu.get_barrier_semaphore()
    if plane:
        def call(k,_):
            pl.semaphore_signal(barrier,inc=1,device_id={DP:lax.rem(lax.axis_index(DP)+k,plane)},device_id_type=MESH)
            return 0
        lax.fori_loop(1,plane,call,0)
        for k in range(1,count):
            pl.semaphore_signal(barrier,inc=1,device_id={AXIS:lax.rem(here+k,count)},device_id_type=MESH)
        pl.semaphore_wait(barrier,plane+count-2)
    else:
        @pl.when(here>0)
        def _(): pl.semaphore_signal(barrier,inc=1,device_id={AXIS:here-1},device_id_type=MESH)
        @pl.when(here<count-1)
        def _(): pl.semaphore_signal(barrier,inc=1,device_id={AXIS:here+1},device_id_type=MESH)
        pl.semaphore_wait(barrier,jnp.where((here>0)&(here<count-1),2,1))

def swap(axis, count, source, landing, sends, recvs):
    me=lax.axis_index(axis)
    def copy(peer, slot, k):
        return pltpu.make_async_remote_copy(src_ref=source(peer),dst_ref=landing.at[slot],send_sem=sends.at[k],
            recv_sem=recvs.at[slot],device_id={axis:peer},device_id_type=MESH)
    def begin(k,_):
        copy(lax.rem(me+k,count),me,k).start()
        return 0
    def end(k,_):
        peer=lax.rem(me+k,count)
        copy(peer,peer,k).wait_recv()
        copy(peer,me,k).wait_send()
        return 0
    return (lambda: lax.fori_loop(1,count,begin,0)),(lambda: lax.fori_loop(1,count,end,0))

def remote(src,dst,send,recv,target):
    return pltpu.make_async_remote_copy(src_ref=src,dst_ref=dst,send_sem=send,recv_sem=recv,
        device_id={AXIS:target},device_id_type=MESH)

class Line:
    def __init__(self,count,pieces,rows,part=None,sums=None,sum_sems=None,held=None,held_sems=None,base=0,sub=None):
        self.n,self.pieces,self.rows=count,pieces,rows
        self.sub=rows//pieces if sub is None else sub
        self.base=base
        self.here=lax.axis_index(AXIS)
        self.part,self.sums,self.sum_sems=part,sums,sum_sems
        self.held,self.held_sems=held,held_sems
    def span(self,u): return pl.ds(pl.multiple_of(self.base+u*self.sub,self.sub),self.sub)
    def fits(self,u): return (u>=0)&(u<self.pieces)
    def _target(self,way):
        return lax.min(self.here+1,self.n-1) if way==0 else lax.max(self.here-1,0)
    def slot(self,way,j,device):
        return j if way==0 else jnp.where(j==device,self.n,j)
    def sum_copy(self,way,j,u,first):
        sends,recvs=self.sum_sems
        dst=self.sums.at[self.slot(way,j,self._target(way)),self.span(u)]
        src=self.part.at[j,self.span(u)] if first else self.sums.at[self.slot(way,j,self.here),self.span(u)]
        return remote(src,dst,sends.at[way,j,u],recvs.at[way,j,u],self._target(way))
    def sum_arrival(self,way,j,u):
        sends,recvs=self.sum_sems
        ref=self.sums.at[self.slot(way,j,self.here),self.span(u)]
        return remote(ref,ref,sends.at[way,j,u],recvs.at[way,j,u],self._target(way))
    def relay(self,way,j,u,begins,passes):
        @pl.when(begins)
        def _(): self.sum_copy(way,j,u,True).start()
        @pl.when(passes)
        def _():
            self.sum_arrival(way,j,u).wait_recv()
            ref=self.sums.at[j,self.span(u)]
            ref[...]=(ref[...].astype(F32)+self.part[j,self.span(u)].astype(F32)).astype(BF)
            self.sum_copy(way,j,u,False).start()
    def far_steps(self): return (self.n-1)*self.pieces+1
    def far_step(self,t,total,finish):
        here,n,S=self.here,self.n,self.pieces
        for way in (0,1):
            q=t-here if way==0 else t-(n-1-here)
            ok=(q>=0)&(q<S*(n-1-here if way==0 else here))
            q=jnp.clip(q,0,S*(n-1)-1)
            j=n-1-q//S if way==0 else q//S
            end=(here==0) if way==0 else (here==n-1)
            self.relay(way,j,q%S,ok&end,ok&jnp.logical_not(end))
        u=t-(n-2)*S-1
        @pl.when(self.fits(u))
        def _():
            self.own_sum(u,total)
            finish(self.span(u),total)
    def send_sums(self,t):
        here,n=self.here,self.n
        for k in range(n-1):
            for way,j in ((0,n-1-k),(1,k)):
                u=t-here-(n-1-j) if way==0 else t-(n-1-here)-j
                ok=self.fits(u)
                u=jnp.clip(u,0,self.pieces-1)
                begins=(here==0) if way==0 else (here==n-1)
                passes=((here>0)&(here<j)) if way==0 else ((here<n-1)&(here>j))
                self.relay(way,j,u,ok&begins,ok&passes)
    def sweep_steps(self): return self.pieces+2*(self.n-1)
    def sweep(self,t,total,finish):
        far=self.n-1
        self.send_sums(t)
        u=t-far
        @pl.when(self.fits(u))
        def _():
            self.own_sum(u,total)
            self.held[self.here,self.span(u)]=finish(self.span(u),total)
            self.send_own(u)
        self.pass_pieces(t-far)
    def own_sum(self,u,total):
        here,n=self.here,self.n
        total[...]=self.part[here,self.span(u)].astype(F32)
        for way in (0,1):
            @pl.when(here>0 if way==0 else here<n-1)
            def _():
                self.sum_arrival(way,here,u).wait_recv()
                total[...]+=self.sums[self.slot(way,here,here),self.span(u)].astype(F32)
    def end_sums(self):
        here,n=self.here,self.n
        def one(u,_):
            for k in range(n-1):
                for way,j in ((0,n-1-k),(1,k)):
                    @pl.when((here<j) if way==0 else (here>j))
                    def _(): self.sum_copy(way,j,u,False).wait_send()
            return 0
        lax.fori_loop(0,self.pieces,one,0)
    def piece_copy(self,way,c,u,src=None):
        sends,recvs=self.held_sems
        dst=self.held.at[c,self.span(u)]
        return remote(dst if src is None else src,dst,sends.at[way,c,u],recvs.at[way,c,u],self._target(way))
    def send_own(self,u,src=None):
        here,n=self.here,self.n
        for way in (0,1):
            @pl.when(here<n-1 if way==0 else here>0)
            def _(): self.piece_copy(way,here,u,src).start()
    def gather_step(self,t,source):
        if t==0:
            for u in range(min(2,self.pieces)): self.send_own(u,source.at[self.span(u),:])
        else:
            self.pass_pieces(t)
            if t+1<self.pieces: self.send_own(t+1,source.at[self.span(t+1),:])
    def gather_steps(self): return self.pieces+self.n-1
    def pass_pieces(self,t,use=None):
        here,n=self.here,self.n
        for k in range(1,n):
            u=t-k
            ok=self.fits(u)
            u=jnp.clip(u,0,self.pieces-1)
            for way in (0,1):
                c=here-k if way==0 else here+k
                there=ok&((c>=0) if way==0 else (c<n))
                c=jnp.clip(c,0,n-1)
                @pl.when(there)
                def _(): self.piece_copy(way,c,u).wait_recv()
                @pl.when(there&(here<n-1 if way==0 else here>0))
                def _(): self.piece_copy(way,c,u).start()
                if use is not None:
                    @pl.when(there)
                    def _(): use(c,u)
    def end_pieces(self):
        here,n=self.here,self.n
        def one(u,_):
            for k in range(n):
                for way in (0,1):
                    c=here-k if way==0 else here+k
                    there=(c>=0) if way==0 else (c<n)
                    c=jnp.clip(c,0,n-1)
                    @pl.when(there&(here<n-1 if way==0 else here>0))
                    def _(): self.piece_copy(way,c,u).wait_send()
            return 0
        lax.fori_loop(0,self.pieces,one,0)

def gain_terms(part,other,acc,c):
    rows=part.shape[1]
    def some(k,_):
        span=pl.ds(pl.multiple_of(k*16,16),16)
        both=part[c,span].astype(F32)*other[c,span].astype(F32)
        acc[...]+=both[:8]+both[8:]
        return 0
    lax.fori_loop(0,rows//16,some,0)

def last_kernel(count, plane, pieces, part_hbm, other_hbm, tokens_hbm, grads_hbm, gain, terms, out, shared, part, other, tokens, grads, cs, sums, total, ss, sr, acc, cut, landed, level, stacked, ds, dr, zs, zr):
    width=part.shape[2]
    line=Line(count,pieces,part.shape[1],part,sums,(ss,sr))
    loads=[pltpu.make_async_copy(s,d,cs.at[k]) for k,(s,d) in enumerate(((part_hbm,part),(other_hbm,other),(tokens_hbm,tokens),(grads_hbm,grads)))]
    for load in loads: load.start()
    greet(line.here,count,plane)
    loads[0].wait()
    acc[...]=jnp.zeros_like(acc)
    me=lax.axis_index(DP)
    piece=width//plane
    begin_dp,end_dp=swap(DP,plane,lambda p: cut.at[p],landed,ds,dr)
    begin_z,end_z=swap(AXIS,count,lambda p: level,stacked,zs,zr)
    def finish(span,total):
        stream=tokens[span,:].astype(F32)
        scale=lax.rsqrt(jnp.mean(stream*stream,-1,keepdims=True)+EPSILON)
        unit=stream*scale
        scaled=total[...]*gain[0:1,:]
        out[span,:]=grads[span,:]+scale*(scaled-unit*jnp.mean(scaled*unit,-1,keepdims=True))
    def step(t,_):
        line.far_step(t,total,finish)
        @pl.when(t==0)
        def _():
            for load in loads[1:]: load.wait()
        @pl.when(t<count)
        def _(): gain_terms(part,other,acc,jnp.clip(t,0,count-1))
        @pl.when(t==count-1)
        def _():
            for p in range(plane):
                cut[p,0:8,:]=acc[:,p*piece:(p+1)*piece]
                cut[p,8:16,:]=terms[:,p*piece:(p+1)*piece]
            landed[me]=cut[me]
            begin_dp()
        @pl.when(t==count+1)
        def _():
            end_dp()
            level[...]=jnp.sum(landed[...],0)
            stacked[line.here]=level[...]
            begin_z()
        return 0
    assert line.far_steps()>count+1
    lax.fori_loop(0,line.far_steps(),step,0)
    end_z()
    shared[...]=jnp.sum(stacked[...],0)
    line.end_sums()

def last_sums(part,other,tokens,grads,gains,terms,cid,pieces,n,plane):
    rows,D=tokens.shape
    vm=pl.BlockSpec(memory_space=pltpu.VMEM)
    hbm=pl.BlockSpec(memory_space=pl.ANY)
    sds=jax.ShapeDtypeStruct
    sem=pltpu.SemaphoreType.DMA
    w=D//plane
    return pl.pallas_call(functools.partial(last_kernel,n,plane,pieces),
        out_shape=(sds((rows,D),F32),sds((16,w),F32)),in_specs=[hbm]*4+[vm]*2,out_specs=(vm,vm),
        scratch_shapes=[pltpu.VMEM((n,rows,D),BF),pltpu.VMEM((n,rows,D),BF),pltpu.VMEM((rows,D),BF),pltpu.VMEM((rows,D),F32),sem((4,)),pltpu.VMEM((n+1,rows,D),BF),pltpu.VMEM((rows//pieces,D),F32),sem((2,n,pieces)),sem((2,n,pieces)),pltpu.VMEM((8,D),F32),
            pltpu.VMEM((plane,16,w),F32),pltpu.VMEM((plane,16,w),F32),pltpu.VMEM((16,w),F32),pltpu.VMEM((n,16,w),F32),
            sem((plane,)),sem((plane,)),sem((n,)),sem((n,))],
        cost_estimate=pl.CostEstimate(flops=0,bytes_accessed=270_000_000,transcendentals=0),
        compiler_params=pltpu.CompilerParams(collective_id=cid,has_side_effects=True,vmem_limit_bytes=56*1024*1024),
    )(part.reshape(n,rows,D),other.reshape(n,rows,D),tokens,grads,gains,terms)


def mlp_kernel(count,pieces,tile,x_hbm,grad_ref,res_ref,early_hbm,wgu_hbm,wd_hbm,
        part_ref,wide_ref,out_ref,rest_hbm,x_ref,gr,product,gated,lifted,down,ring,tall,sums,total,hs,hr,ss,sr,ws,ts,ls,rs,xs):
    s=pl.program_id(0)
    length,hidden=product.shape
    width=x_ref.shape[1]
    rows=grad_ref.shape[0]
    half=rows//2
    first,second=hidden//tile,width//tile
    slots=ring.shape[0]
    at_down=first; at_grad=first+second; at_part=2*first+second; at_weight=2*first+2*second
    begun=early_hbm.shape[1]
    spread=hs.shape[2]
    get=Line(count,spread,rows,held=gr,held_sems=(hs,hr),base=begun,sub=(rows-begun)//spread)
    line=Line(count,pieces,rows,down,sums,(ss,sr),sub=half//pieces)
    def rest(c): return pltpu.make_async_copy(down.at[c,pl.ds(half,half)],rest_hbm.at[c],rs.at[c])
    def strip(k,size): return pl.ds(pl.multiple_of(jnp.clip(k,0,size-1)*tile,tile),tile)
    def tall_load(k):
        slot=lax.rem(k,slots)
        @pl.when((k<2*first)&(lax.rem(k,2)==0))
        def _(): pltpu.make_async_copy(wgu_hbm.at[:,strip(k//2,first)],tall.at[slot],ts.at[slot]).start()
        @pl.when((k<2*first)&(lax.rem(k,2)==1))
        def _(): pltpu.make_async_copy(wgu_hbm.at[:,strip(first+k//2,2*first)],tall.at[slot],ts.at[slot]).start()
        @pl.when((k>=2*first)&(k<2*first+second))
        def _(): pltpu.make_async_copy(wd_hbm.at[:,strip(k-2*first,second)],tall.at[slot],ts.at[slot]).start()
    def tall_loaded(k):
        slot=lax.rem(k,slots)
        pltpu.make_async_copy(wd_hbm.at[:,pl.ds(0,tile)],tall.at[slot],ts.at[slot]).wait()
        return slot
    def load(k):
        slot=lax.rem(k,slots)
        late=strip((k-first)//2,second)
        @pl.when(k<first)
        def _(): pltpu.make_async_copy(wd_hbm.at[strip(k,first),:],ring.at[slot],ws.at[slot]).start()
        @pl.when((k>=first)&(lax.rem(k-first,2)==0)&(k<first+2*second))
        def _(): pltpu.make_async_copy(wgu_hbm.at[late,pl.ds(0,hidden)],ring.at[slot],ws.at[slot]).start()
        @pl.when((k>=first)&(lax.rem(k-first,2)==1)&(k<first+2*second))
        def _(): pltpu.make_async_copy(wgu_hbm.at[late,pl.ds(hidden,hidden)],ring.at[slot],ws.at[slot]).start()
    def loaded(k):
        slot=lax.rem(k,slots)
        pltpu.make_async_copy(wd_hbm.at[pl.ds(0,tile),:],ring.at[slot],ws.at[slot]).wait()
        return slot
    def own(): return pltpu.make_async_copy(grad_ref,gr.at[get.here],ls.at[0])
    def early(c): return pltpu.make_async_copy(early_hbm.at[c],gr.at[c,pl.ds(0,begun)],ls.at[1+c])
    def whole_x(): return pltpu.make_async_copy(x_hbm,x_ref,xs)
    @pl.when(s==0)
    def _():
        whole_x().start()
        for k in range(slots): tall_load(k)
        greet(get.here,count)
        get.gather_step(0,grad_ref)
        own().start()
        for c in range(count):
            @pl.when(c!=get.here)
            def _(): early(c).start()
        whole_x().wait()
    @pl.when(s==at_down-1)
    def _():
        for k in range(slots): load(k)
    hops=get.gather_steps()-1
    marks=(1,2,3,5,7) if first==4 and second==4 and hops==5 else tuple(min(k+1,at_grad) for k in range(hops))
    for k,mark in enumerate(marks):
        @pl.when(s==mark)
        def _(): get.gather_step(k+1,grad_ref)
    @pl.when(s==at_grad)
    def _():
        own().wait()
        for c in range(count):
            @pl.when(c!=get.here)
            def _(): early(c).wait()
    def finish(span,total):
        out_ref[span,:]=(res_ref[span,:]+total[...]).astype(BF)
    r=s-at_grad
    t=jnp.int32(-1)
    marks=(0,2,4,5,6,10,16) if first==4 and second==4 else tuple(range(line.far_steps()))
    for k,mark in enumerate(marks): t=jnp.where(r==mark,k,t)
    @pl.when(t>=0)
    def _(): line.far_step(t,total,finish)
    @pl.when(r==0)
    def _():
        for c in range(count): rest(c).start()
    @pl.when(s<at_down)
    def _():
        one=tall_loaded(2*s)
        two=tall_loaded(2*s+1)
        cols=strip(s,first)
        for c in range(count):
            span=slice(c*rows,(c+1)*rows)
            gate=jnp.dot(x_ref[span,:],tall[one],preferred_element_type=F32)
            up=jnp.dot(x_ref[span,:],tall[two],preferred_element_type=F32)
            sigmoid=1.0/(1.0+jnp.exp(-gate))
            active=gate*sigmoid
            product[span,cols]=(active*up).astype(BF)
            lifted[span,cols]=active.astype(BF)
            gated[span,cols]=(up*(sigmoid+active*(1.0-sigmoid))).astype(BF)
        tall_load(2*s+slots)
        tall_load(2*s+1+slots)
    @pl.when((s>=at_down)&(s<at_grad))
    def _():
        k=2*first+s-at_down
        slot=tall_loaded(k)
        sums_here=jnp.dot(product[...],tall[slot],preferred_element_type=F32).astype(BF)
        cols=strip(s-at_down,second)
        for c in range(count): down[c,:,cols]=sums_here[c*rows:(c+1)*rows]
        tall_load(k+slots)
    @pl.when((s>=at_grad)&(s<at_part))
    def _():
        k=s-at_grad
        slot=loaded(k)
        cols=strip(k,first)
        for c in range(count):
            span=slice(c*rows,(c+1)*rows)
            grads=lax.dot_general(gr[c],ring[slot],(((1,),(1,)),((),())),preferred_element_type=F32)
            gated[span,cols]=(grads*gated[span,cols].astype(F32)).astype(BF)
            lifted[span,cols]=(grads*lifted[span,cols].astype(F32)).astype(BF)
        load(k+slots)
    @pl.when((s>=at_part)&(s<at_weight))
    def _():
        k=first+2*(s-at_part)
        one=loaded(k)
        both=lax.dot_general(gated[...],ring[one],(((1,),(1,)),((),())),preferred_element_type=F32)
        load(k+slots)
        two=loaded(k+1)
        both=both+lax.dot_general(lifted[...],ring[two],(((1,),(1,)),((),())),preferred_element_type=F32)
        part_ref[...]=both.astype(BF)
        load(k+1+slots)
    last=s-at_weight
    cols=strip(last//6,second)
    kind=lax.rem(last,6)
    cut=hidden//2
    def weight(left,right):
        wide_ref[...]=lax.dot_general(left,right,(((0,),(0,)),((),())),preferred_element_type=F32).astype(BF)
    for side in (0,1):
        these=slice(side*cut,(side+1)*cut)
        @pl.when((last>=0)&(kind==side))
        def _(): weight(x_ref[:,cols],gated[:,these])
        @pl.when((last>=0)&(kind==2+side))
        def _(): weight(x_ref[:,cols],lifted[:,these])
        @pl.when((last>=0)&(kind==4+side))
        def _(): weight(gr[:,:,cols].reshape(length,tile),product[:,these])
    @pl.when(s==at_weight+6*second-1)
    def _():
        get.end_pieces()
        line.end_sums()
        for c in range(count): rest(c).wait()

def mlp(x,grad_out,residual,early,w_both,w_down,cid,spread,pieces,count):
    length,width=x.shape
    hidden=w_down.shape[0]
    rows=length//count
    tile=min(512,hidden,width)
    first,second=hidden//tile,width//tile
    steps=2*first+8*second
    assert first!=4 or second!=4 or (count-1)*pieces+1==7
    assert first+7*second>=(count-1)*pieces+1
    whole=lambda shape: pl.BlockSpec(shape,lambda s: (0,)*len(shape),pipeline_mode=pl.Buffered(1))
    hbm=pl.BlockSpec(memory_space=pl.ANY)
    sds=jax.ShapeDtypeStruct
    sem=pltpu.SemaphoreType.DMA
    at_part=2*first+second
    def wide_map(s):
        k=jnp.maximum(s-at_part-second,0)
        return (k//6,k%6)
    vmem=pltpu.VMEM
    return pl.pallas_call(functools.partial(mlp_kernel,count,pieces,tile),
        grid=(steps,),
        out_shape=(sds((length,width),BF),sds((width,3*hidden),BF),sds((rows//2,width),BF),sds((count,rows//2,width),BF)),
        in_specs=[hbm,whole((rows,width)),pl.BlockSpec((rows//2,width),lambda s: (0,0),pipeline_mode=pl.Buffered(1)),hbm,hbm,hbm],
        out_specs=(pl.BlockSpec((length,tile),lambda s: (0,jnp.clip(s-at_part,0,second-1))),
            pl.BlockSpec((tile,hidden//2),wide_map),whole((rows//2,width)),hbm),
        scratch_shapes=[vmem((length,width),BF),vmem((count,rows,width),BF),vmem((length,hidden),BF),vmem((length,hidden),BF),vmem((length,hidden),BF),
            vmem((count,rows,width),BF),vmem((4,tile,width),BF),vmem((4,width,tile),BF),vmem((count+1,rows//2,width),BF),vmem((rows//2//pieces,width),F32),
            sem((2,count,spread)),sem((2,count,spread)),sem((2,count,pieces)),sem((2,count,pieces)),sem((4,)),sem((4,)),sem((count+1,)),sem((count,)),sem],
        cost_estimate=pl.CostEstimate(flops=78_000_000_000,bytes_accessed=380_000_000,transcendentals=0),
        compiler_params=pltpu.CompilerParams(collective_id=cid,has_side_effects=True,vmem_limit_bytes=60*1024*1024,
            dimension_semantics=("arbitrary",)),
    )(x,grad_out,residual,early,w_both,w_down)


def frequencies(head_size):
    inverse = 1.0 / 500000.0 ** (jnp.arange(head_size // 2, dtype=jnp.float32) * 2.0 / head_size)
    wavelength = 2.0 * math.pi / inverse
    smooth = (8192.0 / wavelength - 1.0) / 3.0
    blended = (1.0 - smooth) * inverse / 32.0 + smooth * inverse
    return jnp.where(
        wavelength > 8192.0, inverse / 32.0, jnp.where(wavelength < 2048.0, inverse, blended)
    )


def dot(left_side, right_side, left_dim, right_dim):
    return lax.dot_general(
        left_side, right_side, (((left_dim,), (right_dim,)), ((), ())), preferred_element_type=F32
    )


def norm_kernel(count, plane, pieces, tokens_ref, gains_ref, gate_hbm, up_hbm, angles_ref, normed_hbm, gains_out, both_hbm, cosine, sine, held, normed, landed, hs, hr, ds, dr, ws, bs):
    hidden = gate_hbm.shape[1]
    sides = [
        pltpu.make_async_copy(source, both_hbm.at[:, pl.ds(k * hidden, hidden)], bs.at[k])
        for k, source in enumerate((gate_hbm, up_hbm))
    ]
    line = Line(count, pieces, tokens_ref.shape[0], held=held, held_sems=(hs, hr))
    greet(line.here, count, plane)
    me = lax.axis_index(DP)
    begin, end = swap(DP, plane, lambda p: gains_ref, landed, ds, dr)
    for u in range(pieces):
        line.send_own(u, tokens_ref.at[line.span(u), :])
    begin()
    for side in sides:
        side.start()
    landed[me] = gains_ref[...]
    end()
    piece = gains_ref.shape[1]
    for p in range(plane):
        gains_out[:, p * piece : (p + 1) * piece] = landed[p]

    def give(c, u):
        return pltpu.make_async_copy(normed.at[c, line.span(u)], normed_hbm.at[c, line.span(u)], ws.at[c, u])

    def norm(rows, c, u):
        stream = rows.astype(F32)
        scale = lax.rsqrt(jnp.mean(stream * stream, -1, keepdims=True) + EPSILON)
        normed[c, line.span(u)] = (stream * scale * gains_out[0:1, :]).astype(BF)
        give(c, u).start()

    def step(t, _):
        line.pass_pieces(t, lambda c, u: norm(held[c, line.span(u)], c, u))

        @pl.when(t == 1)
        def _():
            cosine[...] = jnp.cos(angles_ref[...])
            sine[...] = jnp.sin(angles_ref[...])

        @pl.when(t < pieces)
        def _():
            u = jnp.clip(t, 0, pieces - 1)
            norm(tokens_ref[line.span(u), :], line.here, u)

        return 0

    lax.fori_loop(0, pieces + count - 1, step, 0)
    line.end_pieces()
    for side in sides:
        side.wait()
    for c in range(count):
        for u in range(pieces):
            give(c, u).wait()


def norm_and_gather(tokens, gains, w_gate, w_up, angles, cid, pieces, count, plane):
    rows, width = tokens.shape
    vm = pl.BlockSpec(memory_space=pltpu.VMEM)
    sem = pltpu.SemaphoreType.DMA
    hbm = pl.BlockSpec(memory_space=pl.ANY)
    sds = jax.ShapeDtypeStruct
    normed, *rest = pl.pallas_call(
        functools.partial(norm_kernel, count, plane, pieces),
        out_shape=(
            sds((count, rows, width), BF),
            sds((8, width), F32),
            sds((w_gate.shape[0], 2 * w_gate.shape[1]), BF),
            sds(angles.shape, F32),
            sds(angles.shape, F32),
        ),
        in_specs=[vm, vm, hbm, hbm, vm],
        out_specs=(hbm, vm, hbm, vm, vm),
        scratch_shapes=[
            pltpu.VMEM((count, rows, width), BF),
            pltpu.VMEM((count, rows, width), BF),
            pltpu.VMEM((plane, 8, width // plane), F32),
            sem((2, count, pieces)),
            sem((2, count, pieces)),
            sem((plane,)),
            sem((plane,)),
            sem((count, pieces)),
            sem((2,)),
        ],
        cost_estimate=pl.CostEstimate(flops=0, bytes_accessed=270_000_000, transcendentals=0),
        compiler_params=pltpu.CompilerParams(
            collective_id=cid, has_side_effects=True, vmem_limit_bytes=58 * 1024 * 1024
        ),
    )(tokens, gains, w_gate, w_up, angles)
    return normed.reshape(count * rows, width), *rest


def wide_results_kernel(gate_in, up_in, down_in, tokens_in, block_in, sums_ref, gains_ref, gate, up, down, tokens, block, terms):
    tokens[...] = tokens_in[...]
    block[...] = block_in[...]
    terms[0:1, :] = jnp.sum(sums_ref[0:8, :], 0, keepdims=True) / gains_ref[0:1, :]
    terms[1:2, :] = jnp.sum(sums_ref[8:16, :], 0, keepdims=True) / gains_ref[1:2, :]
    gate[...] = gate_in[...].astype(F32)
    up[...] = up_in[...].astype(F32)
    down[...] = down_in[...].astype(F32).T


def wide_results(wide, grad_tokens, block_out, sums, gains, hidden):
    shard = wide.shape[0]
    tile = min(512, hidden)
    steps = hidden // tile
    sds = jax.ShapeDtypeStruct
    still = lambda shape: pl.BlockSpec(shape, lambda s: (0, 0))
    strip = pl.BlockSpec((grad_tokens.shape[0], grad_tokens.shape[1] // steps), lambda s: (0, s))
    return pl.pallas_call(
        wide_results_kernel,
        grid=(steps,),
        out_shape=(
            sds((shard, hidden), F32),
            sds((shard, hidden), F32),
            sds((hidden, shard), F32),
            sds(grad_tokens.shape, F32),
            sds(block_out.shape, BF),
            sds((2, shard), F32),
        ),
        in_specs=[pl.BlockSpec((shard, tile), lambda s, k=k: (0, k * steps + s)) for k in range(3)]
        + [strip, strip, still(sums.shape), still(gains.shape)],
        out_specs=(
            pl.BlockSpec((shard, tile), lambda s: (0, s)),
            pl.BlockSpec((shard, tile), lambda s: (0, s)),
            pl.BlockSpec((tile, shard), lambda s: (s, 0)),
            strip,
            strip,
            still((2, shard)),
        ),
        compiler_params=pltpu.CompilerParams(vmem_limit_bytes=60 * 1024 * 1024),
    )(wide, wide, wide, grad_tokens, block_out, sums, gains)


def mix_results_kernel(mix_ref, terms_ref, query, key, value, out, first, second):
    edge = query.shape[1]
    query[...] = mix_ref[:, :edge].astype(F32)
    key[...] = mix_ref[:, edge : edge + key.shape[1]].astype(F32)
    edge += key.shape[1]
    value[...] = mix_ref[:, edge : edge + value.shape[1]].astype(F32)
    edge += value.shape[1]
    out[...] = mix_ref[:, edge:].astype(F32).T
    first[...] = terms_ref[0:1, :]
    second[...] = terms_ref[1:2, :]


def mix_results(mix, terms, deep, narrow):
    shard = mix.shape[0]
    sds = jax.ShapeDtypeStruct
    vm = pl.BlockSpec(memory_space=pltpu.VMEM)
    return pl.pallas_call(
        mix_results_kernel,
        out_shape=(
            sds((shard, deep), F32),
            sds((shard, narrow), F32),
            sds((shard, narrow), F32),
            sds((deep, shard), F32),
            sds((1, shard), F32),
            sds((1, shard), F32),
        ),
        in_specs=[vm, vm],
        out_specs=(vm,) * 6,
        compiler_params=pltpu.CompilerParams(vmem_limit_bytes=60 * 1024 * 1024),
    )(mix, terms)


def body(
    count,
    plane,
    tokens,
    segments,
    positions,
    attn_gain,
    w_query,
    w_key,
    w_value,
    w_out,
    mlp_gain,
    w_gate,
    w_up,
    w_down,
    grad_out,
):
    rows, width = tokens.shape
    heads = w_query.shape[1] // HD
    groups = w_key.shape[1] // HD
    after = lax.optimization_barrier
    mix = lax.all_gather(jnp.concatenate([w_query, w_key, w_value], 1), DP, axis=0, tiled=True)
    full_out = lax.all_gather(w_out, DP, axis=1, tiled=True)
    full_down = lax.all_gather(w_down, DP, axis=1, tiled=True)
    own_gains = jnp.concatenate([jnp.stack([attn_gain, mlp_gain]).astype(F32), jnp.zeros((6, attn_gain.shape[0]), F32)])

    angles = frequencies(HD)[:, None] * positions.astype(F32)[None, :]
    normed_one, gains, both, cosine, sine = norm_and_gather(tokens, own_gains, w_gate, w_up, angles, 1, 4, count, plane)
    full_both = lax.all_gather(both, DP, axis=0, tiled=True)

    mixed, lse, q, kt, k, v, residual, early, normed_two = attend(
        mix, normed_one, cosine, sine, segments, full_out, grad_out, tokens, gains, heads, groups, 6, rows * 5 // 8, 5, 16, count
    )
    normed_two = normed_two.reshape(count * rows, width)
    part, grad_wide, block_early, down = mlp(normed_two, grad_out, residual, early, full_both, full_down, 5, 3, 2, count)
    grad_wide = lax.psum_scatter(grad_wide, DP, scatter_dimension=0, tiled=True)
    grad_residual, terms_two, part, grad_mix, block_out = attend_back(
        part, normed_two, grad_out, gains, full_out, q, kt, k, v, lse, cosine, sine, segments, down, residual, block_early,
        mixed, normed_one, mix, heads, groups, 7, 2, 16, count,
    )
    grad_mix = lax.psum_scatter(grad_mix, DP, scatter_dimension=0, tiled=True)
    grad_tokens, sums = last_sums(part, normed_one, tokens, grad_residual, gains, terms_two, 4, 4, count, plane)
    grad_gate, grad_up, grad_down, grad_tokens, block_out, terms = wide_results(
        grad_wide, grad_tokens, block_out, sums, own_gains, full_down.shape[0]
    )
    grad_query, grad_key, grad_value, grad_out_proj, grad_attn_gain, grad_mlp_gain = mix_results(
        grad_mix, terms, heads * HD, groups * HD
    )
    return (
        block_out,
        grad_tokens,
        grad_attn_gain.reshape(-1),
        grad_query,
        grad_key,
        grad_value,
        grad_out_proj,
        grad_mlp_gain.reshape(-1),
        grad_gate,
        grad_up,
        grad_down,
    )


def solution(mesh):
    placed = (
        P(("dp", "tensor"), None),
        P("dp"),
        P("dp"),
        P("dp"),
        P("dp", "tensor"),
        P("dp", "tensor"),
        P("dp", "tensor"),
        P("tensor", "dp"),
        P("dp"),
        P("dp", "tensor"),
        P("dp", "tensor"),
        P("tensor", "dp"),
        P(("dp", "tensor"), None),
    )
    return jax.shard_map(
        functools.partial(body, mesh.shape["tensor"], mesh.shape["dp"]),
        mesh=mesh,
        in_specs=placed,
        out_specs=(
            P(("dp", "tensor"), None),
            P(("dp", "tensor"), None),
            P("dp"),
            P("dp", "tensor"),
            P("dp", "tensor"),
            P("dp", "tensor"),
            P("tensor", "dp"),
            P("dp"),
            P("dp", "tensor"),
            P("dp", "tensor"),
            P("tensor", "dp"),
        ),
        check_vma=False,
    )
```

```python
import functools
import math

import jax
import jax.numpy as jnp
from jax import lax
from jax.experimental import pallas as pl
from jax.experimental.pallas import tpu as pltpu
from jax.sharding import PartitionSpec as P

HD = 64
EPSILON = 1e-05
MASKED = -1e30
F32 = jnp.float32
BF = jnp.bfloat16

def turn_t(values, cosine, sine, sign):
    half=values.shape[0]//2
    first, second = values[:half], values[half:]
    return jnp.concatenate([first*cosine - sign*second*sine, second*cosine + sign*first*sine],0)

AUG=80

def thirds(x):
    one=x.astype(BF)
    rest=x-one.astype(F32)
    two=rest.astype(BF)
    three=(rest-two.astype(F32)).astype(BF)
    return [part.astype(F32) for part in (one,two,three)]

def tail_rows(rows,width):
    return jnp.concatenate(rows+[jnp.zeros((AUG-HD-len(rows),width),F32)],0)

def triangle(block):
    keys=lax.broadcasted_iota(jnp.int32,(block,block),0)
    queries=lax.broadcasted_iota(jnp.int32,(block,block),1)
    return jnp.where(keys<=queries,0.0,MASKED).astype(F32)

def attend_kernel(heads, groups, block, count, pieces, fine, mix_hbm, normed_hbm, cos_ref, sin_ref, segr_ref, wo_hbm, grad_ref, tokens_hbm, gain_ref,
                  mixed_ref, q_ref, kt_ref, k_ref, v_ref, residual_ref, rows_hbm, whole_hbm,
                  mix_ref, normed_ref, lin_ref, tri_ref, vt_ref, wo_ref, tokens_ref, part_ref, held, hs, hr, sums, total, ss, sr, moved, ms, mr, cs):
    length=normed_ref.shape[0]
    per=heads//groups
    rows=grad_ref.shape[0]
    early=held.shape[1]
    line=Line(count,pieces,rows,held=held,held_sems=(hs,hr),sub=early//pieces)
    inputs=[pltpu.make_async_copy(s,d,cs.at[4+k]) for k,(s,d) in enumerate(((normed_hbm,normed_ref),(mix_hbm,mix_ref)))]
    for copy in inputs: copy.start()
    greet(line.here,count)
    line.gather_step(0,grad_ref)
    for copy in inputs: copy.wait()
    weights=pltpu.make_async_copy(wo_hbm,wo_ref,cs.at[0])
    weights.start()
    stream=pltpu.make_async_copy(tokens_hbm,tokens_ref,cs.at[1])
    stream.start()
    lines=mix_ref.shape[1]
    cut=256 if lines%256==0 else lines
    for c in range(0,lines,cut):
        lin_ref[c:c+cut,:]=lax.dot_general(mix_ref[:,c:c+cut],normed_ref[...],(((0,),(1,)),((),())),preferred_element_type=F32)
    steps=line.gather_steps()
    done=0
    def tick():
        nonlocal done
        if done+1<steps:
            done+=1
            line.gather_step(done,grad_ref)
    tick()
    cosine, sine = cos_ref[...], sin_ref[...]
    segs=segr_ref[...]
    apart=[jnp.where(segs==s,MASKED,0.0).astype(F32) for s in range(3)]
    others=[jnp.where(segs==s,0.0,1.0).astype(F32) for s in range(3)]
    ones=jnp.ones((1,length),F32)
    plain=tail_rows(apart,length).astype(BF)
    def rope(h,_):
        rows=pl.ds(pl.multiple_of(h*HD,HD),HD)
        q_ref[h,0:HD,:]=(turn_t(lin_ref[rows,:],cosine,sine,1.0).astype(BF)*jnp.asarray(0.125,BF))
        q_ref[h,HD:,:]=plain
        return 0
    lax.fori_loop(0,heads,rope,0)
    beside=tail_rows(others+[ones]*3,length)
    below=tail_rows([ones]*3,length)
    for g in range(groups):
        keys_t=turn_t(lin_ref[(heads+g)*HD:(heads+g+1)*HD,:],cosine,sine,1.0)
        kt_ref[g*HD:(g+1)*HD,:]=keys_t.astype(BF)
        k_ref[g]=jnp.concatenate([keys_t,beside],0).T.astype(BF)
        vals_t=jnp.concatenate([lin_ref[(heads+groups+g)*HD:(heads+groups+g+1)*HD,:],below],0)
        vt_ref[g]=vals_t.astype(BF)
        v_ref[g]=vals_t.T.astype(BF)
    tri_ref[...]=triangle(block)
    for start in range(0,length,block):
        cols=slice(start,start+block)
        if start in (block,3*block): tick()
        def head(h,_):
            g=h//per
            rows=pl.ds(pl.multiple_of(h*HD,HD),HD)
            query=q_ref[h,:,cols]
            parts=[jnp.dot(k_ref[g,c:c+block,:],query,preferred_element_type=F32) for c in range(0,start+block,block)]
            parts[-1]=parts[-1]+tri_ref[...]
            top=functools.reduce(jnp.maximum,[jnp.max(part,0,keepdims=True) for part in parts])
            out=functools.reduce(jnp.add,[jnp.dot(vt_ref[g,:,k*block:(k+1)*block],jnp.exp(part-top).astype(BF),preferred_element_type=F32)
                for k,part in enumerate(parts)])
            total=out[HD:HD+1]
            mixed_ref[rows,cols]=(out[:HD]/total).astype(BF)
            logs=thirds(top+jnp.log(total))
            q_ref[h,HD:,cols]=tail_rows([row[:,cols] for row in apart]+[-x for x in logs],block).astype(BF)
            return 0
        lax.fori_loop(0,heads,head,0,unroll=2)
    width=wo_ref.shape[1]
    wide=min(512,width)
    weights.wait()
    tick()
    def out(c,_):
        cols=pl.ds(pl.multiple_of(c*wide,wide),wide)
        product=lax.dot_general(mixed_ref[...],wo_ref[:,cols],(((0,),(0,)),((),())),preferred_element_type=F32).astype(BF)
        for j in range(count): part_ref[j,:,cols]=product[j*rows:(j+1)*rows]
        return 0
    lax.fori_loop(0,width//wide,out,0)
    held[line.here]=grad_ref[0:early,:]
    copy=pltpu.make_async_copy(held,rows_hbm,cs.at[2])
    stream.wait()
    sweep=Line(count,fine,rows,part_ref,sums,(ss,sr),moved,(ms,mr))
    def finish(span,total):
        residual=total[...]+tokens_ref[span,:].astype(F32)
        residual_ref[span,:]=residual
        scale=lax.rsqrt(jnp.mean(residual*residual,-1,keepdims=True)+EPSILON)
        return (residual*scale*gain_ref[1:2,:]).astype(BF)
    def step(t,_):
        sweep.sweep(t,total,finish)
        for k in range(done+1,steps):
            @pl.when(t==2*(k-done-1))
            def _(): line.gather_step(k,grad_ref)
        return 0
    lax.fori_loop(0,sweep.sweep_steps(),step,0)
    copy.start()
    last=pltpu.make_async_copy(moved,whole_hbm,cs.at[3])
    last.start()
    line.end_pieces()
    sweep.end_sums()
    sweep.end_pieces()
    copy.wait()
    last.wait()

def attend(mix, normed, cosine, sine, segments, w_out, grad_out, tokens, gain, heads, groups, cid, early, pieces, fine, count):
    length,width=normed.shape
    rows=grad_out.shape[0]
    block=min(256,length)
    sds=jax.ShapeDtypeStruct
    vm=pl.BlockSpec(memory_space=pltpu.VMEM)
    hbm=pl.BlockSpec(memory_space=pl.ANY)
    sem=pltpu.SemaphoreType.DMA
    vmem=pltpu.VMEM
    return pl.pallas_call(functools.partial(attend_kernel,heads,groups,block,count,pieces,fine),
        out_shape=(sds((heads*HD,length),BF),sds((heads,AUG,length),BF),
            sds((groups*HD,length),BF),sds((groups,length,AUG),BF),sds((groups,length,AUG),BF),
            sds((rows,width),F32),sds((count,early,width),BF),sds((count,rows,width),BF)),
        in_specs=[hbm,hbm]+[vm]*3+[hbm,vm,hbm,vm],out_specs=(vm,)*6+(hbm,hbm),
        scratch_shapes=[vmem(mix.shape,BF),vmem(normed.shape,BF),vmem((mix.shape[1],length),F32),vmem((block,block),F32),vmem((groups,AUG,length),BF),vmem(w_out.shape,BF),
            vmem(tokens.shape,BF),vmem((count,rows,width),BF),vmem((count,early,width),BF),sem((2,count,pieces)),sem((2,count,pieces)),
            vmem((count+1,rows,width),BF),vmem((rows//fine,width),F32),sem((2,count,fine)),sem((2,count,fine)),
            vmem((count,rows,width),BF),sem((2,count,fine)),sem((2,count,fine)),sem((6,))],
        cost_estimate=pl.CostEstimate(flops=30_000_000_000,bytes_accessed=500_000_000,transcendentals=8_000_000),
        compiler_params=pltpu.CompilerParams(collective_id=cid,has_side_effects=True,vmem_limit_bytes=58*1024*1024),
    )(mix,normed,cosine,sine,segments.reshape(1,length),w_out,grad_out,tokens,gain)

def attend_back_kernel(heads, groups, block, count, pieces, fine, grads_hbm, two_hbm, go_ref, gain_ref, wo_hbm, q_ref, kt_ref, k_ref, v_ref, cos_ref, sin_ref,
                  down_ref, res_ref, early_ref, mixed_hbm, normed_hbm, mix_hbm,
                  gres_ref, acc, part_hbm, grad_hbm, out_ref,
                  part_ref, normed_ref, low_ref, wide_sums, wide_total, ws, wr, hs, hr,
                  wo_ref, mixed_ref, mix_ref, turn_ref, gm_ref, tri_ref, qn_ref, gn_ref, dq_ref, dk_ref, dv_ref, sums, total, ss, sr, grad_ref, cs, gs_sem):
    length=q_ref.shape[2]
    per=heads//groups
    width=wo_ref.shape[1]
    rows=res_ref.shape[0]
    half=rows//2
    line=Line(count,pieces,half,down_ref,sums,(ss,sr))
    sweep=Line(count,fine,rows,part_ref,wide_sums,(ws,wr),low_ref,(hs,hr))
    first=pltpu.make_async_copy(grads_hbm,part_ref,cs.at[0])
    first.start()
    second=pltpu.make_async_copy(two_hbm,normed_ref,cs.at[1])
    second.start()
    late=[pltpu.make_async_copy(s,d,cs.at[2+k]) for k,(s,d) in enumerate(((mixed_hbm,mixed_ref),(mix_hbm,mix_ref),(wo_hbm,wo_ref)))]
    for copy in late: copy.start()
    greet(line.here,count)
    acc[...]=jnp.zeros_like(acc)
    out_ref[0:half,:]=early_ref[...]
    first.wait()
    def turn(span,total):
        residual=res_ref[span,:]
        scale=lax.rsqrt(jnp.mean(residual*residual,-1,keepdims=True)+EPSILON)
        unit=residual*scale
        scaled=total[...]*gain_ref[1:2,:]
        grads=go_ref[span,:].astype(F32)+scale*(scaled-unit*jnp.mean(scaled*unit,-1,keepdims=True))
        gres_ref[span,:]=grads
        return grads.astype(BF)
    def finish(span,total):
        places=pl.ds(pl.multiple_of(half+span.start,line.sub),line.sub)
        out_ref[places,:]=(res_ref[places,:]+total[...]).astype(BF)
    steps=sweep.sweep_steps()
    begun=2
    dk_ref[...]=jnp.zeros_like(dk_ref)
    dv_ref[...]=jnp.zeros_like(dv_ref)
    tri_ref[...]=triangle(block)
    def flip_query(p):
        qn=jnp.concatenate([q_ref[2*p,0:HD,:],q_ref[2*p+1,0:HD,:]],0).astype(F32).T.astype(BF)
        qn_ref[2*p]=qn[:,:HD]
        qn_ref[2*p+1]=qn[:,HD:]
    def step(t,_):
        sweep.sweep(t,wide_total,turn)
        @pl.when((t>=8)&(t<8+heads//2))
        def _(): flip_query(jnp.clip(t-8,0,heads//2-1))
        @pl.when(t==2)
        def _(): second.wait()
        @pl.when((t>=2)&(t<count+2))
        def _(): gain_terms(part_ref,normed_ref,acc,jnp.clip(t-2,0,count-1))
        for k in range(begun):
            @pl.when(t==steps-2*(begun-k))
            def _(): line.far_step(jnp.int32(k),total,finish)
        return 0
    lax.fori_loop(0,steps,step,0)
    third=pltpu.make_async_copy(normed_hbm,normed_ref,cs.at[1])
    third.start()
    ticks=[begun]
    def tick(amount=1):
        for _ in range(amount):
            if ticks[0]<line.far_steps():
                line.far_step(jnp.int32(ticks[0]),total,finish)
                ticks[0]+=1
    late[2].wait()
    whole=lambda: low_ref[...].reshape(length,width)
    cosine, sine = cos_ref[...], sin_ref[...]
    deep=heads*HD
    cut=256 if deep%256==0 else deep
    late[0].wait()
    for c in range(0,deep,cut):
        product=lax.dot_general(wo_ref[c:c+cut,:],whole(),(((1,),(1,)),((),())),preferred_element_type=F32).astype(BF)
        for h in range(c//HD,(c+cut)//HD):
            grads=product[h*HD-c:(h+1)*HD-c]
            gm_ref[h,0:HD,:]=grads
            centre=jnp.sum(grads.astype(F32)*mixed_ref[h*HD:(h+1)*HD,:].astype(F32),0,keepdims=True)
            gm_ref[h,HD:,:]=tail_rows([-x for x in thirds(centre)],length).astype(BF)
    def flip(p,_):
        gn=jnp.concatenate([gm_ref[2*p,0:HD,:],gm_ref[2*p+1,0:HD,:]],0).astype(F32).T.astype(BF)
        gn_ref[2*p]=gn[:,:HD]
        gn_ref[2*p+1]=gn[:,HD:]
        return 0
    lax.fori_loop(0,heads//2,flip,0)
    lines=(heads+2*groups)*HD
    strip=min(512,width)
    tick()
    for c in range(0,width,strip):
        grad_ref[c:c+strip,lines:]=lax.dot_general(low_ref[:,:,c:c+strip].reshape(length,strip),mixed_ref[...],(((0,),(1,)),((),())),preferred_element_type=F32).astype(BF)
    for start in range(0,length,block):
        cols=slice(start,start+block)
        spans=[slice(start,start+block)]+([slice(0,start)] if start else [])
        def head(h,_):
            g=h//per
            rows=pl.ds(pl.multiple_of(h*HD,HD),HD)
            grows=pl.ds(pl.multiple_of(g*HD,HD),HD)
            query,grads=q_ref[h,:,cols],gm_ref[h,:,cols]
            query_n,grads_n=qn_ref[h,cols,:],gn_ref[h,cols,:]
            total_q=None
            for k,span in enumerate(spans):
                scores=jnp.dot(k_ref[g,span,:],query,preferred_element_type=F32)
                if k==0: scores=scores+tri_ref[...]
                probs=jnp.exp(scores)
                dv_ref[g,span,:]+=jnp.dot(probs.astype(BF),grads_n,preferred_element_type=F32)
                gs=(probs*jnp.dot(v_ref[g,span,:],grads,preferred_element_type=F32)).astype(BF)
                dk_ref[g,span,:]+=jnp.dot(gs,query_n,preferred_element_type=F32)
                one=jnp.dot(kt_ref[grows,span],gs,preferred_element_type=F32)
                total_q=one if total_q is None else total_q+one
            dq_ref[rows,cols]=0.125*total_q
            return 0
        lax.fori_loop(0,heads,head,0,unroll=2)
        if start>0: tick()
    def back(h,_):
        rows=pl.ds(pl.multiple_of(h*HD,HD),HD)
        turn_ref[rows,:]=turn_t(dq_ref[rows,:],cosine,sine,-1.0).astype(BF)
        return 0
    lax.fori_loop(0,heads,back,0)
    dk=jnp.concatenate([dk_ref[g] for g in range(groups)],1).T
    dv=jnp.concatenate([dv_ref[g] for g in range(groups)],1).T
    for g in range(groups):
        turn_ref[(heads+g)*HD:(heads+g+1)*HD,:]=turn_t(dk[g*HD:(g+1)*HD],cosine,sine,-1.0).astype(BF)
    turn_ref[(heads+groups)*HD:,:]=dv.astype(BF)
    late[1].wait()
    sweep.end_sums()
    for c in range(0,width,strip):
        product=lax.dot_general(turn_ref[...],mix_ref[c:c+strip,:],(((0,),(1,)),((),())),preferred_element_type=F32).astype(BF)
        for j in range(count): part_ref[j,:,c:c+strip]=product[j*rows:(j+1)*rows]
    give=pltpu.make_async_copy(part_ref,part_hbm,cs.at[0])
    give.start()
    tick()
    third.wait()
    for k,c in enumerate(range(0,width,strip)):
        grad_ref[c:c+strip,0:lines]=lax.dot_general(normed_ref[:,:,c:c+strip].reshape(length,strip),turn_ref[...],(((0,),(1,)),((),())),preferred_element_type=F32).astype(BF)
        pltpu.make_async_copy(grad_ref.at[c:c+strip],grad_hbm.at[c:c+strip],gs_sem.at[k]).start()
    tick(line.far_steps())
    line.end_sums()
    sweep.end_pieces()
    give.wait()
    for k,c in enumerate(range(0,width,strip)):
        pltpu.make_async_copy(grad_ref.at[c:c+strip],grad_hbm.at[c:c+strip],gs_sem.at[k]).wait()

def attend_back(grads,two,grad_out,gain,w_out,q,kt,k,v,cosine,sine,down,residual,early,mixed,normed,mix,heads,groups,cid,pieces,fine,count):
    rows,width=residual.shape
    length=rows*count
    lines=mix.shape[1]
    block=min(256,length)
    vm=pl.BlockSpec(memory_space=pltpu.VMEM)
    hbm=pl.BlockSpec(memory_space=pl.ANY)
    vmem=pltpu.VMEM
    sds=jax.ShapeDtypeStruct
    sem=pltpu.SemaphoreType.DMA
    cut=lambda x: x.reshape(count,rows,width)
    return pl.pallas_call(functools.partial(attend_back_kernel,heads,groups,block,count,pieces,fine),
        out_shape=(sds((rows,width),F32),sds((8,width),F32),sds((count,rows,width),BF),sds((width,lines+heads*HD),BF),sds((rows,width),BF)),
        in_specs=[hbm,hbm,vm,vm,hbm]+[vm]*9+[hbm]*3,out_specs=(vm,vm,hbm,hbm,vm),
        scratch_shapes=[vmem((count,rows,width),BF),vmem((count,rows,width),BF),vmem((count,rows,width),BF),vmem((count+1,rows,width),BF),
            vmem((rows//fine,width),F32),sem((2,count,fine)),sem((2,count,fine)),sem((2,count,fine)),sem((2,count,fine)),
            vmem(w_out.shape,BF),vmem(mixed.shape,BF),vmem(mix.shape,BF),vmem((lines,length),BF),vmem((heads,AUG,length),BF),
            vmem((block,block),F32),vmem((heads,length,HD),BF),vmem((heads,length,HD),BF),
            vmem((heads*HD,length),F32),vmem((groups,length,HD),F32),vmem((groups,length,HD),F32),
            vmem((count+1,rows//2,width),BF),vmem((rows//2//pieces,width),F32),sem((2,count,pieces)),sem((2,count,pieces)),
            vmem((width,lines+heads*HD),BF),sem((5,)),sem((max(1,width//min(512,width)),))],
        cost_estimate=pl.CostEstimate(flops=60_000_000_000,bytes_accessed=550_000_000,transcendentals=8_000_000),
        compiler_params=pltpu.CompilerParams(collective_id=cid,has_side_effects=True,vmem_limit_bytes=60*1024*1024),
    )(cut(grads),cut(two),grad_out,gain,w_out,q,kt,k,v,cosine,sine,down,residual,early,mixed,cut(normed),mix)


AXIS="tensor"
DP="dp"
MESH=pl.DeviceIdType.MESH

def greet(here, count, plane=0):
    barrier=pltpu.get_barrier_semaphore()
    if plane:
        def call(k,_):
            pl.semaphore_signal(barrier,inc=1,device_id={DP:lax.rem(lax.axis_index(DP)+k,plane)},device_id_type=MESH)
            return 0
        lax.fori_loop(1,plane,call,0)
        for k in range(1,count):
            pl.semaphore_signal(barrier,inc=1,device_id={AXIS:lax.rem(here+k,count)},device_id_type=MESH)
        pl.semaphore_wait(barrier,plane+count-2)
    else:
        @pl.when(here>0)
        def _(): pl.semaphore_signal(barrier,inc=1,device_id={AXIS:here-1},device_id_type=MESH)
        @pl.when(here<count-1)
        def _(): pl.semaphore_signal(barrier,inc=1,device_id={AXIS:here+1},device_id_type=MESH)
        pl.semaphore_wait(barrier,jnp.where((here>0)&(here<count-1),2,1))

def swap(axis, count, source, landing, sends, recvs):
    me=lax.axis_index(axis)
    def copy(peer, slot, k):
        return pltpu.make_async_remote_copy(src_ref=source(peer),dst_ref=landing.at[slot],send_sem=sends.at[k],
            recv_sem=recvs.at[slot],device_id={axis:peer},device_id_type=MESH)
    def begin(k,_):
        copy(lax.rem(me+k,count),me,k).start()
        return 0
    def end(k,_):
        peer=lax.rem(me+k,count)
        copy(peer,peer,k).wait_recv()
        copy(peer,me,k).wait_send()
        return 0
    return (lambda: lax.fori_loop(1,count,begin,0)),(lambda: lax.fori_loop(1,count,end,0))

def remote(src,dst,send,recv,target):
    return pltpu.make_async_remote_copy(src_ref=src,dst_ref=dst,send_sem=send,recv_sem=recv,
        device_id={AXIS:target},device_id_type=MESH)

class Line:
    def __init__(self,count,pieces,rows,part=None,sums=None,sum_sems=None,held=None,held_sems=None,base=0,sub=None):
        self.n,self.pieces,self.rows=count,pieces,rows
        self.sub=rows//pieces if sub is None else sub
        self.base=base
        self.here=lax.axis_index(AXIS)
        self.part,self.sums,self.sum_sems=part,sums,sum_sems
        self.held,self.held_sems=held,held_sems
    def span(self,u): return pl.ds(pl.multiple_of(self.base+u*self.sub,self.sub),self.sub)
    def fits(self,u): return (u>=0)&(u<self.pieces)
    def _target(self,way):
        return lax.min(self.here+1,self.n-1) if way==0 else lax.max(self.here-1,0)
    def slot(self,way,j,device):
        return j if way==0 else jnp.where(j==device,self.n,j)
    def sum_copy(self,way,j,u,first):
        sends,recvs=self.sum_sems
        dst=self.sums.at[self.slot(way,j,self._target(way)),self.span(u)]
        src=self.part.at[j,self.span(u)] if first else self.sums.at[self.slot(way,j,self.here),self.span(u)]
        return remote(src,dst,sends.at[way,j,u],recvs.at[way,j,u],self._target(way))
    def sum_arrival(self,way,j,u):
        sends,recvs=self.sum_sems
        ref=self.sums.at[self.slot(way,j,self.here),self.span(u)]
        return remote(ref,ref,sends.at[way,j,u],recvs.at[way,j,u],self._target(way))
    def relay(self,way,j,u,begins,passes):
        @pl.when(begins)
        def _(): self.sum_copy(way,j,u,True).start()
        @pl.when(passes)
        def _():
            self.sum_arrival(way,j,u).wait_recv()
            ref=self.sums.at[j,self.span(u)]
            ref[...]=(ref[...].astype(F32)+self.part[j,self.span(u)].astype(F32)).astype(BF)
            self.sum_copy(way,j,u,False).start()
    def far_steps(self): return (self.n-1)*self.pieces+1
    def far_step(self,t,total,finish):
        here,n,S=self.here,self.n,self.pieces
        for way in (0,1):
            q=t-here if way==0 else t-(n-1-here)
            ok=(q>=0)&(q<S*(n-1-here if way==0 else here))
            q=jnp.clip(q,0,S*(n-1)-1)
            j=n-1-q//S if way==0 else q//S
            end=(here==0) if way==0 else (here==n-1)
            self.relay(way,j,q%S,ok&end,ok&jnp.logical_not(end))
        u=t-(n-2)*S-1
        @pl.when(self.fits(u))
        def _():
            self.own_sum(u,total)
            finish(self.span(u),total)
    def send_sums(self,t):
        here,n=self.here,self.n
        for k in range(n-1):
            for way,j in ((0,n-1-k),(1,k)):
                u=t-here-(n-1-j) if way==0 else t-(n-1-here)-j
                ok=self.fits(u)
                u=jnp.clip(u,0,self.pieces-1)
                begins=(here==0) if way==0 else (here==n-1)
                passes=((here>0)&(here<j)) if way==0 else ((here<n-1)&(here>j))
                self.relay(way,j,u,ok&begins,ok&passes)
    def sweep_steps(self): return self.pieces+2*(self.n-1)
    def sweep(self,t,total,finish):
        far=self.n-1
        self.send_sums(t)
        u=t-far
        @pl.when(self.fits(u))
        def _():
            self.own_sum(u,total)
            self.held[self.here,self.span(u)]=finish(self.span(u),total)
            self.send_own(u)
        self.pass_pieces(t-far)
    def own_sum(self,u,total):
        here,n=self.here,self.n
        total[...]=self.part[here,self.span(u)].astype(F32)
        for way in (0,1):
            @pl.when(here>0 if way==0 else here<n-1)
            def _():
                self.sum_arrival(way,here,u).wait_recv()
                total[...]+=self.sums[self.slot(way,here,here),self.span(u)].astype(F32)
    def end_sums(self):
        here,n=self.here,self.n
        def one(u,_):
            for k in range(n-1):
                for way,j in ((0,n-1-k),(1,k)):
                    @pl.when((here<j) if way==0 else (here>j))
                    def _(): self.sum_copy(way,j,u,False).wait_send()
            return 0
        lax.fori_loop(0,self.pieces,one,0)
    def piece_copy(self,way,c,u,src=None):
        sends,recvs=self.held_sems
        dst=self.held.at[c,self.span(u)]
        return remote(dst if src is None else src,dst,sends.at[way,c,u],recvs.at[way,c,u],self._target(way))
    def send_own(self,u,src=None):
        here,n=self.here,self.n
        for way in (0,1):
            @pl.when(here<n-1 if way==0 else here>0)
            def _(): self.piece_copy(way,here,u,src).start()
    def gather_step(self,t,source):
        if t==0:
            for u in range(min(2,self.pieces)): self.send_own(u,source.at[self.span(u),:])
        else:
            self.pass_pieces(t)
            if t+1<self.pieces: self.send_own(t+1,source.at[self.span(t+1),:])
    def gather_steps(self): return self.pieces+self.n-1
    def pass_pieces(self,t,use=None):
        here,n=self.here,self.n
        for k in range(1,n):
            u=t-k
            ok=self.fits(u)
            u=jnp.clip(u,0,self.pieces-1)
            for way in (0,1):
                c=here-k if way==0 else here+k
                there=ok&((c>=0) if way==0 else (c<n))
                c=jnp.clip(c,0,n-1)
                @pl.when(there)
                def _(): self.piece_copy(way,c,u).wait_recv()
                @pl.when(there&(here<n-1 if way==0 else here>0))
                def _(): self.piece_copy(way,c,u).start()
                if use is not None:
                    @pl.when(there)
                    def _(): use(c,u)
    def end_pieces(self):
        here,n=self.here,self.n
        def one(u,_):
            for k in range(n):
                for way in (0,1):
                    c=here-k if way==0 else here+k
                    there=(c>=0) if way==0 else (c<n)
                    c=jnp.clip(c,0,n-1)
                    @pl.when(there&(here<n-1 if way==0 else here>0))
                    def _(): self.piece_copy(way,c,u).wait_send()
            return 0
        lax.fori_loop(0,self.pieces,one,0)

def gain_terms(part,other,acc,c):
    rows=part.shape[1]
    def some(k,_):
        span=pl.ds(pl.multiple_of(k*16,16),16)
        both=part[c,span].astype(F32)*other[c,span].astype(F32)
        acc[...]+=both[:8]+both[8:]
        return 0
    lax.fori_loop(0,rows//16,some,0)

def last_kernel(count, plane, pieces, part_hbm, other_hbm, tokens_hbm, grads_hbm, gain, terms, out, shared, part, other, tokens, grads, cs, sums, total, ss, sr, acc, cut, landed, level, stacked, ds, dr, zs, zr):
    width=part.shape[2]
    line=Line(count,pieces,part.shape[1],part,sums,(ss,sr))
    loads=[pltpu.make_async_copy(s,d,cs.at[k]) for k,(s,d) in enumerate(((part_hbm,part),(other_hbm,other),(tokens_hbm,tokens),(grads_hbm,grads)))]
    for load in loads: load.start()
    greet(line.here,count,plane)
    loads[0].wait()
    acc[...]=jnp.zeros_like(acc)
    me=lax.axis_index(DP)
    piece=width//plane
    begin_dp,end_dp=swap(DP,plane,lambda p: cut.at[p],landed,ds,dr)
    begin_z,end_z=swap(AXIS,count,lambda p: level,stacked,zs,zr)
    def finish(span,total):
        stream=tokens[span,:].astype(F32)
        scale=lax.rsqrt(jnp.mean(stream*stream,-1,keepdims=True)+EPSILON)
        unit=stream*scale
        scaled=total[...]*gain[0:1,:]
        out[span,:]=grads[span,:]+scale*(scaled-unit*jnp.mean(scaled*unit,-1,keepdims=True))
    def step(t,_):
        line.far_step(t,total,finish)
        @pl.when(t==0)
        def _():
            for load in loads[1:]: load.wait()
        @pl.when(t<count)
        def _(): gain_terms(part,other,acc,jnp.clip(t,0,count-1))
        @pl.when(t==count-1)
        def _():
            for p in range(plane):
                cut[p,0:8,:]=acc[:,p*piece:(p+1)*piece]
                cut[p,8:16,:]=terms[:,p*piece:(p+1)*piece]
            landed[me]=cut[me]
            begin_dp()
        @pl.when(t==count+1)
        def _():
            end_dp()
            level[...]=jnp.sum(landed[...],0)
            stacked[line.here]=level[...]
            begin_z()
        return 0
    assert line.far_steps()>count+1
    lax.fori_loop(0,line.far_steps(),step,0)
    end_z()
    shared[...]=jnp.sum(stacked[...],0)
    line.end_sums()

def last_sums(part,other,tokens,grads,gains,terms,cid,pieces,n,plane):
    rows,D=tokens.shape
    vm=pl.BlockSpec(memory_space=pltpu.VMEM)
    hbm=pl.BlockSpec(memory_space=pl.ANY)
    sds=jax.ShapeDtypeStruct
    sem=pltpu.SemaphoreType.DMA
    w=D//plane
    return pl.pallas_call(functools.partial(last_kernel,n,plane,pieces),
        out_shape=(sds((rows,D),F32),sds((16,w),F32)),in_specs=[hbm]*4+[vm]*2,out_specs=(vm,vm),
        scratch_shapes=[pltpu.VMEM((n,rows,D),BF),pltpu.VMEM((n,rows,D),BF),pltpu.VMEM((rows,D),BF),pltpu.VMEM((rows,D),F32),sem((4,)),pltpu.VMEM((n+1,rows,D),BF),pltpu.VMEM((rows//pieces,D),F32),sem((2,n,pieces)),sem((2,n,pieces)),pltpu.VMEM((8,D),F32),
            pltpu.VMEM((plane,16,w),F32),pltpu.VMEM((plane,16,w),F32),pltpu.VMEM((16,w),F32),pltpu.VMEM((n,16,w),F32),
            sem((plane,)),sem((plane,)),sem((n,)),sem((n,))],
        cost_estimate=pl.CostEstimate(flops=0,bytes_accessed=270_000_000,transcendentals=0),
        compiler_params=pltpu.CompilerParams(collective_id=cid,has_side_effects=True,vmem_limit_bytes=56*1024*1024),
    )(part.reshape(n,rows,D),other.reshape(n,rows,D),tokens,grads,gains,terms)


def mlp_kernel(count,pieces,tile,grad_ref,res_hbm,x_hbm,early_hbm,wgu_hbm,wd_hbm,
        out_ref,part_hbm,wide_hbm,rest_hbm,x_ref,gr,product,gated,lifted,down,ring,tall,part_stage,wide_stage,res_ref,sums,total,
        hs,hr,ss,sr,ws,ts,ls,rs,xs,ps,os):
    length,hidden=product.shape
    width=x_ref.shape[1]
    rows=grad_ref.shape[0]
    half=rows//2
    first,second=hidden//tile,width//tile
    slots=ring.shape[0]
    begun=early_hbm.shape[1]
    spread=hs.shape[2]
    get=Line(count,spread,rows,held=gr,held_sems=(hs,hr),base=begun,sub=(rows-begun)//spread)
    line=Line(count,pieces,rows,down,sums,(ss,sr),sub=half//pieces)
    def strip(k,size): return pl.ds(pl.multiple_of(jnp.clip(k,0,size-1)*tile,tile),tile)
    def tall_load(k):
        slot=lax.rem(k,slots)
        @pl.when(k<2*first)
        def _(): pltpu.make_async_copy(wgu_hbm.at[:,strip(lax.rem(k,2)*first+k//2,2*first)],tall.at[slot],ts.at[slot]).start()
        @pl.when((k>=2*first)&(k<2*first+second))
        def _(): pltpu.make_async_copy(wd_hbm.at[:,strip(k-2*first,second)],tall.at[slot],ts.at[slot]).start()
    def tall_loaded(k):
        slot=lax.rem(k,slots)
        pltpu.make_async_copy(wd_hbm.at[:,pl.ds(0,tile)],tall.at[slot],ts.at[slot]).wait()
        return slot
    def load(k):
        slot=lax.rem(k,slots)
        @pl.when(k<first)
        def _(): pltpu.make_async_copy(wd_hbm.at[strip(k,first),:],ring.at[slot],ws.at[slot]).start()
        @pl.when((k>=first)&(k<first+2*second))
        def _():
            side=pl.ds(pl.multiple_of(lax.rem(k-first,2)*hidden,hidden),hidden)
            pltpu.make_async_copy(wgu_hbm.at[strip((k-first)//2,second),side],ring.at[slot],ws.at[slot]).start()
    def loaded(k):
        slot=lax.rem(k,slots)
        pltpu.make_async_copy(wd_hbm.at[pl.ds(0,tile),:],ring.at[slot],ws.at[slot]).wait()
        return slot
    def own(): return pltpu.make_async_copy(grad_ref,gr.at[get.here],ls.at[0])
    def early(c): return pltpu.make_async_copy(early_hbm.at[c],gr.at[c,pl.ds(0,begun)],ls.at[1+c])
    def rest(c): return pltpu.make_async_copy(down.at[c,pl.ds(half,half)],rest_hbm.at[c],rs.at[c])
    whole_x=pltpu.make_async_copy(x_hbm,x_ref,xs)
    whole_x.start()
    base=pltpu.make_async_copy(res_hbm.at[pl.ds(0,half)],res_ref,ls.at[1+count])
    base.start()
    for k in range(slots): tall_load(jnp.int32(k))
    greet(get.here,count)
    get.gather_step(0,grad_ref)
    own().start()
    for c in range(count):
        @pl.when(c!=get.here)
        def _(): early(c).start()
    whole_x.wait()
    hops=get.gather_steps()
    gather_marks=(1,2,3,5,7) if first==4 and second==4 and hops==6 else tuple(min(k+1,first+second-1) for k in range(hops-1))
    sum_marks=(0,2,4,5,6,9,12) if first==4 and second==4 and line.far_steps()==7 else tuple(min(k,first+4*second-1) for k in range(line.far_steps()))
    def gather_at(n):
        for k,mark in enumerate(gather_marks):
            @pl.when(n==mark)
            def _(): get.gather_step(k+1,grad_ref)
    def finish(span,total):
        out_ref[span,:]=(res_ref[span,:]+total[...]).astype(BF)
    def sum_at(n):
        for k,mark in enumerate(sum_marks):
            @pl.when(n==mark)
            def _(): line.far_step(jnp.int32(k),total,finish)
    def forward(n,_):
        gather_at(n)
        one=tall_loaded(2*n)
        two=tall_loaded(2*n+1)
        cols=strip(n,first)
        for c in range(count):
            span=slice(c*rows,(c+1)*rows)
            gate=jnp.dot(x_ref[span,:],tall[one],preferred_element_type=F32)
            up=jnp.dot(x_ref[span,:],tall[two],preferred_element_type=F32)
            sigmoid=1.0/(1.0+jnp.exp(-gate))
            active=gate*sigmoid
            product[span,cols]=(active*up).astype(BF)
            lifted[span,cols]=active.astype(BF)
            gated[span,cols]=(up*(sigmoid+active*(1.0-sigmoid))).astype(BF)
        tall_load(2*n+slots)
        tall_load(2*n+1+slots)
        return 0
    lax.fori_loop(0,first,forward,0)
    for k in range(slots): load(jnp.int32(k))
    def lower(n,_):
        gather_at(first+n)
        slot=tall_loaded(2*first+n)
        sums_here=jnp.dot(product[...],tall[slot],preferred_element_type=F32).astype(BF)
        cols=strip(n,second)
        for c in range(count): down[c,:,cols]=sums_here[c*rows:(c+1)*rows]
        tall_load(2*first+n+slots)
        return 0
    lax.fori_loop(0,second,lower,0)
    for c in range(count): rest(c).start()
    base.wait()
    own().wait()
    for c in range(count):
        @pl.when(c!=get.here)
        def _(): early(c).wait()
    def back(n,_):
        sum_at(n)
        slot=loaded(n)
        cols=strip(n,first)
        for c in range(count):
            span=slice(c*rows,(c+1)*rows)
            grads=lax.dot_general(gr[c],ring[slot],(((1,),(1,)),((),())),preferred_element_type=F32)
            gated[span,cols]=(grads*gated[span,cols].astype(F32)).astype(BF)
            lifted[span,cols]=(grads*lifted[span,cols].astype(F32)).astype(BF)
        load(n+slots)
        return 0
    lax.fori_loop(0,first,back,0)
    def part_copy(n):
        slot=lax.rem(n,2)
        return pltpu.make_async_copy(part_stage.at[slot],part_hbm.at[:,strip(n,second)],ps.at[slot])
    def inner(n,_):
        sum_at(first+n)
        k=first+2*n
        one=loaded(k)
        both=lax.dot_general(gated[...],ring[one],(((1,),(1,)),((),())),preferred_element_type=F32)
        load(k+slots)
        two=loaded(k+1)
        both=both+lax.dot_general(lifted[...],ring[two],(((1,),(1,)),((),())),preferred_element_type=F32)
        @pl.when(n>=2)
        def _(): part_copy(n-2).wait()
        part_stage[lax.rem(n,2)]=both.astype(BF)
        part_copy(n).start()
        load(k+1+slots)
        return 0
    lax.fori_loop(0,second,inner,0)
    def wide_copy(n):
        slot=lax.rem(n,2)
        side=pl.ds(pl.multiple_of(lax.rem(n,3)*hidden,hidden),hidden)
        return pltpu.make_async_copy(wide_stage.at[slot],wide_hbm.at[strip(n//3,second),side],os.at[slot])
    cut=hidden//2
    def weights(m,_):
        cols=strip(m,second)
        for kind in range(3):
            n=3*m+kind
            sum_at(first+second+n)
            @pl.when(n>=2)
            def _(): wide_copy(n-2).wait()
            left=gr[:,:,cols].reshape(length,tile) if kind==2 else x_ref[:,cols]
            right=(gated,lifted,product)[kind]
            for side in (0,1):
                these=slice(side*cut,(side+1)*cut)
                wide_stage[lax.rem(n,2),:,these]=lax.dot_general(left,right[:,these],(((0,),(0,)),((),())),preferred_element_type=F32).astype(BF)
            wide_copy(n).start()
        return 0
    lax.fori_loop(0,second,weights,0)
    get.end_pieces()
    line.end_sums()
    for c in range(count): rest(c).wait()
    for n in range(max(0,second-2),second): part_copy(jnp.int32(n)).wait()
    for n in range(3*second-2,3*second): wide_copy(jnp.int32(n)).wait()

def mlp(x,grad_out,residual,early,w_both,w_down,cid,spread,pieces,count):
    length,width=x.shape
    hidden=w_down.shape[0]
    rows=length//count
    tile=min(512,hidden,width)
    vm=pl.BlockSpec(memory_space=pltpu.VMEM)
    hbm=pl.BlockSpec(memory_space=pl.ANY)
    sds=jax.ShapeDtypeStruct
    sem=pltpu.SemaphoreType.DMA
    vmem=pltpu.VMEM
    half=rows//2
    return pl.pallas_call(functools.partial(mlp_kernel,count,pieces,tile),
        out_shape=(sds((half,width),BF),sds((length,width),BF),sds((width,3*hidden),BF),sds((count,half,width),BF)),
        in_specs=[vm,hbm,hbm,hbm,hbm,hbm],
        out_specs=(vm,hbm,hbm,hbm),
        scratch_shapes=[vmem((length,width),BF),vmem((count,rows,width),BF),vmem((length,hidden),BF),vmem((length,hidden),BF),vmem((length,hidden),BF),
            vmem((count,rows,width),BF),vmem((4,tile,width),BF),vmem((4,width,tile),BF),vmem((2,length,tile),BF),vmem((2,tile,hidden),BF),vmem((half,width),F32),
            vmem((count+1,half,width),BF),vmem((half//pieces,width),F32),
            sem((2,count,spread)),sem((2,count,spread)),sem((2,count,pieces)),sem((2,count,pieces)),sem((4,)),sem((4,)),sem((count+2,)),sem((count,)),sem,
            sem((2,)),sem((2,))],
        cost_estimate=pl.CostEstimate(flops=78_000_000_000,bytes_accessed=380_000_000,transcendentals=0),
        compiler_params=pltpu.CompilerParams(collective_id=cid,has_side_effects=True,vmem_limit_bytes=60*1024*1024),
    )(grad_out,residual,x,early,w_both,w_down)


def frequencies(head_size):
    inverse = 1.0 / 500000.0 ** (jnp.arange(head_size // 2, dtype=jnp.float32) * 2.0 / head_size)
    wavelength = 2.0 * math.pi / inverse
    smooth = (8192.0 / wavelength - 1.0) / 3.0
    blended = (1.0 - smooth) * inverse / 32.0 + smooth * inverse
    return jnp.where(
        wavelength > 8192.0, inverse / 32.0, jnp.where(wavelength < 2048.0, inverse, blended)
    )


def dot(left_side, right_side, left_dim, right_dim):
    return lax.dot_general(
        left_side, right_side, (((left_dim,), (right_dim,)), ((), ())), preferred_element_type=F32
    )


def norm_kernel(count, plane, pieces, tokens_ref, gains_ref, gate_hbm, up_hbm, angles_ref, normed_hbm, gains_out, both_hbm, cosine, sine, held, normed, landed, hs, hr, ds, dr, ws, bs):
    hidden = gate_hbm.shape[1]
    sides = [
        pltpu.make_async_copy(source, both_hbm.at[:, pl.ds(k * hidden, hidden)], bs.at[k])
        for k, source in enumerate((gate_hbm, up_hbm))
    ]
    line = Line(count, pieces, tokens_ref.shape[0], held=held, held_sems=(hs, hr))
    greet(line.here, count, plane)
    me = lax.axis_index(DP)
    begin, end = swap(DP, plane, lambda p: gains_ref, landed, ds, dr)
    for u in range(pieces):
        line.send_own(u, tokens_ref.at[line.span(u), :])
    begin()
    for side in sides:
        side.start()
    landed[me] = gains_ref[...]
    end()
    piece = gains_ref.shape[1]
    for p in range(plane):
        gains_out[:, p * piece : (p + 1) * piece] = landed[p]

    def give(c, u):
        return pltpu.make_async_copy(normed.at[c, line.span(u)], normed_hbm.at[c, line.span(u)], ws.at[c, u])

    def norm(rows, c, u):
        stream = rows.astype(F32)
        scale = lax.rsqrt(jnp.mean(stream * stream, -1, keepdims=True) + EPSILON)
        normed[c, line.span(u)] = (stream * scale * gains_out[0:1, :]).astype(BF)
        give(c, u).start()

    def step(t, _):
        line.pass_pieces(t, lambda c, u: norm(held[c, line.span(u)], c, u))

        @pl.when(t == 1)
        def _():
            cosine[...] = jnp.cos(angles_ref[...])
            sine[...] = jnp.sin(angles_ref[...])

        @pl.when(t < pieces)
        def _():
            u = jnp.clip(t, 0, pieces - 1)
            norm(tokens_ref[line.span(u), :], line.here, u)

        return 0

    lax.fori_loop(0, pieces + count - 1, step, 0)
    line.end_pieces()
    for side in sides:
        side.wait()
    for c in range(count):
        for u in range(pieces):
            give(c, u).wait()


def norm_and_gather(tokens, gains, w_gate, w_up, angles, cid, pieces, count, plane):
    rows, width = tokens.shape
    vm = pl.BlockSpec(memory_space=pltpu.VMEM)
    sem = pltpu.SemaphoreType.DMA
    hbm = pl.BlockSpec(memory_space=pl.ANY)
    sds = jax.ShapeDtypeStruct
    normed, *rest = pl.pallas_call(
        functools.partial(norm_kernel, count, plane, pieces),
        out_shape=(
            sds((count, rows, width), BF),
            sds((8, width), F32),
            sds((w_gate.shape[0], 2 * w_gate.shape[1]), BF),
            sds(angles.shape, F32),
            sds(angles.shape, F32),
        ),
        in_specs=[vm, vm, hbm, hbm, vm],
        out_specs=(hbm, vm, hbm, vm, vm),
        scratch_shapes=[
            pltpu.VMEM((count, rows, width), BF),
            pltpu.VMEM((count, rows, width), BF),
            pltpu.VMEM((plane, 8, width // plane), F32),
            sem((2, count, pieces)),
            sem((2, count, pieces)),
            sem((plane,)),
            sem((plane,)),
            sem((count, pieces)),
            sem((2,)),
        ],
        cost_estimate=pl.CostEstimate(flops=0, bytes_accessed=270_000_000, transcendentals=0),
        compiler_params=pltpu.CompilerParams(
            collective_id=cid, has_side_effects=True, vmem_limit_bytes=58 * 1024 * 1024
        ),
    )(tokens, gains, w_gate, w_up, angles)
    return normed.reshape(count * rows, width), *rest


def wide_results_kernel(gate_in, up_in, down_in, tokens_in, block_in, sums_ref, gains_ref, gate, up, down, tokens, block, terms):
    tokens[...] = tokens_in[...]
    block[...] = block_in[...]
    terms[0:1, :] = jnp.sum(sums_ref[0:8, :], 0, keepdims=True) / gains_ref[0:1, :]
    terms[1:2, :] = jnp.sum(sums_ref[8:16, :], 0, keepdims=True) / gains_ref[1:2, :]
    gate[...] = gate_in[...].astype(F32)
    up[...] = up_in[...].astype(F32)
    down[...] = down_in[...].astype(F32).T


def wide_results(wide, grad_tokens, block_out, sums, gains, hidden):
    shard = wide.shape[0]
    tile = min(512, hidden)
    steps = hidden // tile
    sds = jax.ShapeDtypeStruct
    still = lambda shape: pl.BlockSpec(shape, lambda s: (0, 0))
    strip = pl.BlockSpec((grad_tokens.shape[0], grad_tokens.shape[1] // steps), lambda s: (0, s))
    return pl.pallas_call(
        wide_results_kernel,
        grid=(steps,),
        out_shape=(
            sds((shard, hidden), F32),
            sds((shard, hidden), F32),
            sds((hidden, shard), F32),
            sds(grad_tokens.shape, F32),
            sds(block_out.shape, BF),
            sds((2, shard), F32),
        ),
        in_specs=[pl.BlockSpec((shard, tile), lambda s, k=k: (0, k * steps + s)) for k in range(3)]
        + [strip, strip, still(sums.shape), still(gains.shape)],
        out_specs=(
            pl.BlockSpec((shard, tile), lambda s: (0, s)),
            pl.BlockSpec((shard, tile), lambda s: (0, s)),
            pl.BlockSpec((tile, shard), lambda s: (s, 0)),
            strip,
            strip,
            still((2, shard)),
        ),
        compiler_params=pltpu.CompilerParams(vmem_limit_bytes=60 * 1024 * 1024),
    )(wide, wide, wide, grad_tokens, block_out, sums, gains)


def mix_results_kernel(mix_ref, terms_ref, query, key, value, out, first, second):
    edge = query.shape[1]
    query[...] = mix_ref[:, :edge].astype(F32)
    key[...] = mix_ref[:, edge : edge + key.shape[1]].astype(F32)
    edge += key.shape[1]
    value[...] = mix_ref[:, edge : edge + value.shape[1]].astype(F32)
    edge += value.shape[1]
    out[...] = mix_ref[:, edge:].astype(F32).T
    first[...] = terms_ref[0:1, :]
    second[...] = terms_ref[1:2, :]


def mix_results(mix, terms, deep, narrow):
    shard = mix.shape[0]
    sds = jax.ShapeDtypeStruct
    vm = pl.BlockSpec(memory_space=pltpu.VMEM)
    return pl.pallas_call(
        mix_results_kernel,
        out_shape=(
            sds((shard, deep), F32),
            sds((shard, narrow), F32),
            sds((shard, narrow), F32),
            sds((deep, shard), F32),
            sds((1, shard), F32),
            sds((1, shard), F32),
        ),
        in_specs=[vm, vm],
        out_specs=(vm,) * 6,
        compiler_params=pltpu.CompilerParams(vmem_limit_bytes=60 * 1024 * 1024),
    )(mix, terms)


def body(
    count,
    plane,
    tokens,
    segments,
    positions,
    attn_gain,
    w_query,
    w_key,
    w_value,
    w_out,
    mlp_gain,
    w_gate,
    w_up,
    w_down,
    grad_out,
):
    rows, width = tokens.shape
    heads = w_query.shape[1] // HD
    groups = w_key.shape[1] // HD
    after = lax.optimization_barrier
    mix = lax.all_gather(jnp.concatenate([w_query, w_key, w_value], 1), DP, axis=0, tiled=True)
    full_out = lax.all_gather(w_out, DP, axis=1, tiled=True)
    full_down = lax.all_gather(w_down, DP, axis=1, tiled=True)
    own_gains = jnp.concatenate([jnp.stack([attn_gain, mlp_gain]).astype(F32), jnp.zeros((6, attn_gain.shape[0]), F32)])

    angles = frequencies(HD)[:, None] * positions.astype(F32)[None, :]
    normed_one, gains, both, cosine, sine = norm_and_gather(tokens, own_gains, w_gate, w_up, angles, 1, 4, count, plane)
    full_both = lax.all_gather(both, DP, axis=0, tiled=True)

    mixed, q, kt, k, v, residual, early, normed_two = attend(
        mix, normed_one, cosine, sine, segments, full_out, grad_out, tokens, gains, heads, groups, 6, rows * 5 // 8, 5, 16, count
    )
    normed_two = normed_two.reshape(count * rows, width)
    block_early, part, grad_wide, down = mlp(normed_two, grad_out, residual, early, full_both, full_down, 5, 3, 2, count)
    grad_wide = lax.psum_scatter(grad_wide, DP, scatter_dimension=0, tiled=True)
    grad_residual, terms_two, part, grad_mix, block_out = attend_back(
        part, normed_two, grad_out, gains, full_out, q, kt, k, v, cosine, sine, down, residual, block_early,
        mixed, normed_one, mix, heads, groups, 7, 2, 16, count,
    )
    grad_mix = lax.psum_scatter(grad_mix, DP, scatter_dimension=0, tiled=True)
    grad_tokens, sums = last_sums(part, normed_one, tokens, grad_residual, gains, terms_two, 4, 4, count, plane)
    grad_gate, grad_up, grad_down, grad_tokens, block_out, terms = wide_results(
        grad_wide, grad_tokens, block_out, sums, own_gains, full_down.shape[0]
    )
    grad_query, grad_key, grad_value, grad_out_proj, grad_attn_gain, grad_mlp_gain = mix_results(
        grad_mix, terms, heads * HD, groups * HD
    )
    return (
        block_out,
        grad_tokens,
        grad_attn_gain.reshape(-1),
        grad_query,
        grad_key,
        grad_value,
        grad_out_proj,
        grad_mlp_gain.reshape(-1),
        grad_gate,
        grad_up,
        grad_down,
    )


def solution(mesh):
    placed = (
        P(("dp", "tensor"), None),
        P("dp"),
        P("dp"),
        P("dp"),
        P("dp", "tensor"),
        P("dp", "tensor"),
        P("dp", "tensor"),
        P("tensor", "dp"),
        P("dp"),
        P("dp", "tensor"),
        P("dp", "tensor"),
        P("tensor", "dp"),
        P(("dp", "tensor"), None),
    )
    return jax.shard_map(
        functools.partial(body, mesh.shape["tensor"], mesh.shape["dp"]),
        mesh=mesh,
        in_specs=placed,
        out_specs=(
            P(("dp", "tensor"), None),
            P(("dp", "tensor"), None),
            P("dp"),
            P("dp", "tensor"),
            P("dp", "tensor"),
            P("dp", "tensor"),
            P("tensor", "dp"),
            P("dp"),
            P("dp", "tensor"),
            P("dp", "tensor"),
            P("tensor", "dp"),
        ),
        check_vma=False,
    )
```

```python
import functools
import math

import jax
import jax.numpy as jnp
from jax import lax
from jax.experimental import pallas as pl
from jax.experimental.pallas import tpu as pltpu
from jax.sharding import PartitionSpec as P

HD = 64
EPSILON = 1e-05
MASKED = -1e30
F32 = jnp.float32
BF = jnp.bfloat16

def turn_t(values, cosine, sine, sign):
    half=values.shape[0]//2
    first, second = values[:half], values[half:]
    return jnp.concatenate([first*cosine - sign*second*sine, second*cosine + sign*first*sine],0)

AUG=80

def thirds(x):
    one=x.astype(BF)
    rest=x-one.astype(F32)
    two=rest.astype(BF)
    three=(rest-two.astype(F32)).astype(BF)
    return [part.astype(F32) for part in (one,two,three)]

def tail_rows(rows,width):
    return jnp.concatenate(rows+[jnp.zeros((AUG-HD-len(rows),width),F32)],0)

def triangle(block):
    keys=lax.broadcasted_iota(jnp.int32,(block,block),0)
    queries=lax.broadcasted_iota(jnp.int32,(block,block),1)
    return jnp.where(keys<=queries,0.0,MASKED).astype(F32)

def attend_kernel(heads, groups, block, count, pieces, fine, mix_hbm, normed_hbm, cos_ref, sin_ref, segr_ref, wo_hbm, grad_ref, tokens_hbm, gain_ref,
                  mixed_ref, q_ref, kt_ref, k_ref, v_ref, residual_ref, rows_hbm, whole_hbm,
                  mix_ref, normed_ref, lin_ref, tri_ref, vt_ref, wo_ref, tokens_ref, part_ref, held, hs, hr, sums, total, ss, sr, moved, ms, mr, cs):
    length=normed_ref.shape[0]
    per=heads//groups
    rows=grad_ref.shape[0]
    early=held.shape[1]
    line=Line(count,pieces,rows,held=held,held_sems=(hs,hr),sub=early//pieces)
    inputs=[pltpu.make_async_copy(s,d,cs.at[4+k]) for k,(s,d) in enumerate(((normed_hbm,normed_ref),(mix_hbm,mix_ref)))]
    for copy in inputs: copy.start()
    greet(line.here,count)
    line.gather_step(0,grad_ref)
    for copy in inputs: copy.wait()
    weights=pltpu.make_async_copy(wo_hbm,wo_ref,cs.at[0])
    weights.start()
    stream=pltpu.make_async_copy(tokens_hbm,tokens_ref,cs.at[1])
    stream.start()
    lines=mix_ref.shape[1]
    cut=256 if lines%256==0 else lines
    for c in range(0,lines,cut):
        lin_ref[c:c+cut,:]=lax.dot_general(mix_ref[:,c:c+cut],normed_ref[...],(((0,),(1,)),((),())),preferred_element_type=F32)
    steps=line.gather_steps()
    done=0
    def tick():
        nonlocal done
        if done+1<steps:
            done+=1
            line.gather_step(done,grad_ref)
    cosine, sine = cos_ref[...], sin_ref[...]
    segs=segr_ref[...]
    apart=[jnp.where(segs==s,MASKED,0.0).astype(F32) for s in range(3)]
    others=[jnp.where(segs==s,0.0,1.0).astype(F32) for s in range(3)]
    ones=jnp.ones((1,length),F32)
    plain=tail_rows(apart,length).astype(BF)
    def rope(h,_):
        rows=pl.ds(pl.multiple_of(h*HD,HD),HD)
        q_ref[h,0:HD,:]=(turn_t(lin_ref[rows,:],cosine,sine,1.0).astype(BF)*jnp.asarray(0.125,BF))
        q_ref[h,HD:,:]=plain
        return 0
    lax.fori_loop(0,heads,rope,0)
    beside=tail_rows(others+[ones]*3,length)
    below=tail_rows([ones]*3,length)
    for g in range(groups):
        keys_t=turn_t(lin_ref[(heads+g)*HD:(heads+g+1)*HD,:],cosine,sine,1.0)
        kt_ref[g*HD:(g+1)*HD,:]=keys_t.astype(BF)
        k_ref[g]=jnp.concatenate([keys_t,beside],0).T.astype(BF)
        vals_t=jnp.concatenate([lin_ref[(heads+groups+g)*HD:(heads+groups+g+1)*HD,:],below],0)
        vt_ref[g]=vals_t.astype(BF)
        v_ref[g]=vals_t.T.astype(BF)
    tri_ref[...]=triangle(block)
    for start in range(0,length,block):
        cols=slice(start,start+block)
        if start in (0,2*block): tick()
        def head(h,_):
            g=h//per
            rows=pl.ds(pl.multiple_of(h*HD,HD),HD)
            query=q_ref[h,:,cols]
            parts=[jnp.dot(k_ref[g,c:c+block,:],query,preferred_element_type=F32) for c in range(0,start+block,block)]
            parts[-1]=parts[-1]+tri_ref[...]
            top=functools.reduce(jnp.maximum,[jnp.max(part,0,keepdims=True) for part in parts])
            out=functools.reduce(jnp.add,[jnp.dot(vt_ref[g,:,k*block:(k+1)*block],jnp.exp(part-top).astype(BF),preferred_element_type=F32)
                for k,part in enumerate(parts)])
            total=out[HD:HD+1]
            mixed_ref[rows,cols]=(out[:HD]/total).astype(BF)
            logs=thirds(top+jnp.log(total))
            q_ref[h,HD:,cols]=tail_rows([row[:,cols] for row in apart]+[-x for x in logs],block).astype(BF)
            return 0
        lax.fori_loop(0,heads,head,0,unroll=2)
    width=wo_ref.shape[1]
    wide=min(512,width)
    weights.wait()
    tick()
    def out(c,_):
        cols=pl.ds(pl.multiple_of(c*wide,wide),wide)
        product=lax.dot_general(mixed_ref[...],wo_ref[:,cols],(((0,),(0,)),((),())),preferred_element_type=F32).astype(BF)
        for j in range(count): part_ref[j,:,cols]=product[j*rows:(j+1)*rows]
        return 0
    lax.fori_loop(0,width//wide,out,0)
    held[line.here]=grad_ref[0:early,:]
    copy=pltpu.make_async_copy(held,rows_hbm,cs.at[2])
    stream.wait()
    sweep=Line(count,fine,rows,part_ref,sums,(ss,sr),moved,(ms,mr))
    def finish(span,total):
        residual=total[...]+tokens_ref[span,:].astype(F32)
        residual_ref[span,:]=residual
        scale=lax.rsqrt(jnp.mean(residual*residual,-1,keepdims=True)+EPSILON)
        return (residual*scale*gain_ref[1:2,:]).astype(BF)
    def step(t,_):
        sweep.sweep(t,total,finish)
        for k in range(done+1,steps):
            @pl.when(t==2*(k-done-1))
            def _(): line.gather_step(k,grad_ref)
        return 0
    lax.fori_loop(0,sweep.sweep_steps(),step,0)
    copy.start()
    last=pltpu.make_async_copy(moved,whole_hbm,cs.at[3])
    last.start()
    line.end_pieces()
    sweep.end_sums()
    sweep.end_pieces()
    copy.wait()
    last.wait()

def attend(mix, normed, cosine, sine, segments, w_out, grad_out, tokens, gain, heads, groups, cid, early, pieces, fine, count):
    length,width=normed.shape
    rows=grad_out.shape[0]
    block=min(256,length)
    sds=jax.ShapeDtypeStruct
    vm=pl.BlockSpec(memory_space=pltpu.VMEM)
    hbm=pl.BlockSpec(memory_space=pl.ANY)
    sem=pltpu.SemaphoreType.DMA
    vmem=pltpu.VMEM
    return pl.pallas_call(functools.partial(attend_kernel,heads,groups,block,count,pieces,fine),
        out_shape=(sds((heads*HD,length),BF),sds((heads,AUG,length),BF),
            sds((groups*HD,length),BF),sds((groups,length,AUG),BF),sds((groups,length,AUG),BF),
            sds((rows,width),F32),sds((count,early,width),BF),sds((count,rows,width),BF)),
        in_specs=[hbm,hbm]+[vm]*3+[hbm,vm,hbm,vm],out_specs=(vm,)*6+(hbm,hbm),
        scratch_shapes=[vmem(mix.shape,BF),vmem(normed.shape,BF),vmem((mix.shape[1],length),F32),vmem((block,block),F32),vmem((groups,AUG,length),BF),vmem(w_out.shape,BF),
            vmem(tokens.shape,BF),vmem((count,rows,width),BF),vmem((count,early,width),BF),sem((2,count,pieces)),sem((2,count,pieces)),
            vmem((count+1,rows,width),BF),vmem((rows//fine,width),F32),sem((2,count,fine)),sem((2,count,fine)),
            vmem((count,rows,width),BF),sem((2,count,fine)),sem((2,count,fine)),sem((6,))],
        cost_estimate=pl.CostEstimate(flops=30_000_000_000,bytes_accessed=500_000_000,transcendentals=8_000_000),
        compiler_params=pltpu.CompilerParams(collective_id=cid,has_side_effects=True,vmem_limit_bytes=58*1024*1024),
    )(mix,normed,cosine,sine,segments.reshape(1,length),w_out,grad_out,tokens,gain)

def attend_back_kernel(heads, groups, block, count, pieces, fine, grads_hbm, two_hbm, go_ref, gain_ref, wo_hbm, q_ref, kt_ref, k_ref, v_ref, cos_ref, sin_ref,
                  down_ref, res_ref, early_ref, mixed_hbm, normed_hbm, mix_hbm,
                  gres_ref, acc, part_hbm, grad_hbm, out_ref,
                  part_ref, normed_ref, low_ref, wide_sums, wide_total, ws, wr, hs, hr,
                  wo_ref, mixed_ref, mix_ref, turn_ref, gm_ref, tri_ref, qn_ref, gn_ref, dq_ref, dk_ref, dv_ref, sums, total, ss, sr, grad_ref, cs, gs_sem):
    length=q_ref.shape[2]
    per=heads//groups
    width=wo_ref.shape[1]
    rows=res_ref.shape[0]
    half=rows//2
    line=Line(count,pieces,half,down_ref,sums,(ss,sr))
    sweep=Line(count,fine,rows,part_ref,wide_sums,(ws,wr),low_ref,(hs,hr))
    first=pltpu.make_async_copy(grads_hbm,part_ref,cs.at[0])
    first.start()
    second=pltpu.make_async_copy(two_hbm,normed_ref,cs.at[1])
    second.start()
    late=[pltpu.make_async_copy(s,d,cs.at[2+k]) for k,(s,d) in enumerate(((mixed_hbm,mixed_ref),(mix_hbm,mix_ref),(wo_hbm,wo_ref)))]
    for copy in late: copy.start()
    greet(line.here,count)
    acc[...]=jnp.zeros_like(acc)
    out_ref[0:half,:]=early_ref[...]
    first.wait()
    def turn(span,total):
        residual=res_ref[span,:]
        scale=lax.rsqrt(jnp.mean(residual*residual,-1,keepdims=True)+EPSILON)
        unit=residual*scale
        scaled=total[...]*gain_ref[1:2,:]
        grads=go_ref[span,:].astype(F32)+scale*(scaled-unit*jnp.mean(scaled*unit,-1,keepdims=True))
        gres_ref[span,:]=grads
        return grads.astype(BF)
    def finish(span,total):
        places=pl.ds(pl.multiple_of(half+span.start,line.sub),line.sub)
        out_ref[places,:]=(res_ref[places,:]+total[...]).astype(BF)
    steps=sweep.sweep_steps()
    begun=2
    dk_ref[...]=jnp.zeros_like(dk_ref)
    dv_ref[...]=jnp.zeros_like(dv_ref)
    tri_ref[...]=triangle(block)
    def flip_query(p):
        qn=jnp.concatenate([q_ref[2*p,0:HD,:],q_ref[2*p+1,0:HD,:]],0).astype(F32).T.astype(BF)
        qn_ref[2*p]=qn[:,:HD]
        qn_ref[2*p+1]=qn[:,HD:]
    def step(t,_):
        sweep.sweep(t,wide_total,turn)
        @pl.when((t>=8)&(t<8+heads//2))
        def _(): flip_query(jnp.clip(t-8,0,heads//2-1))
        @pl.when(t==2)
        def _(): second.wait()
        @pl.when((t>=2)&(t<count+2))
        def _(): gain_terms(part_ref,normed_ref,acc,jnp.clip(t-2,0,count-1))
        for k in range(begun):
            @pl.when(t==steps-2*(begun-k))
            def _(): line.far_step(jnp.int32(k),total,finish)
        return 0
    lax.fori_loop(0,steps,step,0)
    third=pltpu.make_async_copy(normed_hbm,normed_ref,cs.at[1])
    third.start()
    ticks=[begun]
    def tick(amount=1):
        for _ in range(amount):
            if ticks[0]<line.far_steps():
                line.far_step(jnp.int32(ticks[0]),total,finish)
                ticks[0]+=1
    late[2].wait()
    whole=lambda: low_ref[...].reshape(length,width)
    cosine, sine = cos_ref[...], sin_ref[...]
    deep=heads*HD
    cut=256 if deep%256==0 else deep
    late[0].wait()
    for c in range(0,deep,cut):
        product=lax.dot_general(wo_ref[c:c+cut,:],whole(),(((1,),(1,)),((),())),preferred_element_type=F32).astype(BF)
        for h in range(c//HD,(c+cut)//HD):
            grads=product[h*HD-c:(h+1)*HD-c]
            gm_ref[h,0:HD,:]=grads
            centre=jnp.sum(grads.astype(F32)*mixed_ref[h*HD:(h+1)*HD,:].astype(F32),0,keepdims=True)
            gm_ref[h,HD:,:]=tail_rows([-x for x in thirds(centre)],length).astype(BF)
    def flip(p,_):
        gn=jnp.concatenate([gm_ref[2*p,0:HD,:],gm_ref[2*p+1,0:HD,:]],0).astype(F32).T.astype(BF)
        gn_ref[2*p]=gn[:,:HD]
        gn_ref[2*p+1]=gn[:,HD:]
        return 0
    lax.fori_loop(0,heads//2,flip,0)
    lines=(heads+2*groups)*HD
    strip=min(512,width)
    tick()
    for c in range(0,width,strip):
        grad_ref[c:c+strip,lines:]=lax.dot_general(low_ref[:,:,c:c+strip].reshape(length,strip),mixed_ref[...],(((0,),(1,)),((),())),preferred_element_type=F32).astype(BF)
    for start in range(0,length,block):
        cols=slice(start,start+block)
        spans=[slice(start,start+block)]+([slice(0,start)] if start else [])
        def head(h,_):
            g=h//per
            rows=pl.ds(pl.multiple_of(h*HD,HD),HD)
            grows=pl.ds(pl.multiple_of(g*HD,HD),HD)
            query,grads=q_ref[h,:,cols],gm_ref[h,:,cols]
            query_n,grads_n=qn_ref[h,cols,:],gn_ref[h,cols,:]
            total_q=None
            for k,span in enumerate(spans):
                scores=jnp.dot(k_ref[g,span,:],query,preferred_element_type=F32)
                if k==0: scores=scores+tri_ref[...]
                probs=jnp.exp(scores)
                dv_ref[g,span,:]+=jnp.dot(probs.astype(BF),grads_n,preferred_element_type=F32)
                gs=(probs*jnp.dot(v_ref[g,span,:],grads,preferred_element_type=F32)).astype(BF)
                dk_ref[g,span,:]+=jnp.dot(gs,query_n,preferred_element_type=F32)
                one=jnp.dot(kt_ref[grows,span],gs,preferred_element_type=F32)
                total_q=one if total_q is None else total_q+one
            dq_ref[rows,cols]=0.125*total_q
            return 0
        lax.fori_loop(0,heads,head,0,unroll=2)
        if start>0: tick()
    def back(h,_):
        rows=pl.ds(pl.multiple_of(h*HD,HD),HD)
        turn_ref[rows,:]=turn_t(dq_ref[rows,:],cosine,sine,-1.0).astype(BF)
        return 0
    lax.fori_loop(0,heads,back,0)
    dk=jnp.concatenate([dk_ref[g] for g in range(groups)],1).T
    dv=jnp.concatenate([dv_ref[g] for g in range(groups)],1).T
    for g in range(groups):
        turn_ref[(heads+g)*HD:(heads+g+1)*HD,:]=turn_t(dk[g*HD:(g+1)*HD],cosine,sine,-1.0).astype(BF)
    turn_ref[(heads+groups)*HD:,:]=dv.astype(BF)
    late[1].wait()
    sweep.end_sums()
    for c in range(0,width,strip):
        product=lax.dot_general(turn_ref[...],mix_ref[c:c+strip,:],(((0,),(1,)),((),())),preferred_element_type=F32).astype(BF)
        for j in range(count): part_ref[j,:,c:c+strip]=product[j*rows:(j+1)*rows]
    give=pltpu.make_async_copy(part_ref,part_hbm,cs.at[0])
    give.start()
    tick()
    third.wait()
    for k,c in enumerate(range(0,width,strip)):
        grad_ref[c:c+strip,0:lines]=lax.dot_general(normed_ref[:,:,c:c+strip].reshape(length,strip),turn_ref[...],(((0,),(1,)),((),())),preferred_element_type=F32).astype(BF)
        pltpu.make_async_copy(grad_ref.at[c:c+strip],grad_hbm.at[c:c+strip],gs_sem.at[k]).start()
    tick(line.far_steps())
    line.end_sums()
    sweep.end_pieces()
    give.wait()
    for k,c in enumerate(range(0,width,strip)):
        pltpu.make_async_copy(grad_ref.at[c:c+strip],grad_hbm.at[c:c+strip],gs_sem.at[k]).wait()

def attend_back(grads,two,grad_out,gain,w_out,q,kt,k,v,cosine,sine,down,residual,early,mixed,normed,mix,heads,groups,cid,pieces,fine,count):
    rows,width=residual.shape
    length=rows*count
    lines=mix.shape[1]
    block=min(256,length)
    vm=pl.BlockSpec(memory_space=pltpu.VMEM)
    hbm=pl.BlockSpec(memory_space=pl.ANY)
    vmem=pltpu.VMEM
    sds=jax.ShapeDtypeStruct
    sem=pltpu.SemaphoreType.DMA
    cut=lambda x: x.reshape(count,rows,width)
    return pl.pallas_call(functools.partial(attend_back_kernel,heads,groups,block,count,pieces,fine),
        out_shape=(sds((rows,width),F32),sds((8,width),F32),sds((count,rows,width),BF),sds((width,lines+heads*HD),BF),sds((rows,width),BF)),
        in_specs=[hbm,hbm,vm,vm,hbm]+[vm]*9+[hbm]*3,out_specs=(vm,vm,hbm,hbm,vm),
        scratch_shapes=[vmem((count,rows,width),BF),vmem((count,rows,width),BF),vmem((count,rows,width),BF),vmem((count+1,rows,width),BF),
            vmem((rows//fine,width),F32),sem((2,count,fine)),sem((2,count,fine)),sem((2,count,fine)),sem((2,count,fine)),
            vmem(w_out.shape,BF),vmem(mixed.shape,BF),vmem(mix.shape,BF),vmem((lines,length),BF),vmem((heads,AUG,length),BF),
            vmem((block,block),F32),vmem((heads,length,HD),BF),vmem((heads,length,HD),BF),
            vmem((heads*HD,length),F32),vmem((groups,length,HD),F32),vmem((groups,length,HD),F32),
            vmem((count+1,rows//2,width),BF),vmem((rows//2//pieces,width),F32),sem((2,count,pieces)),sem((2,count,pieces)),
            vmem((width,lines+heads*HD),BF),sem((5,)),sem((max(1,width//min(512,width)),))],
        cost_estimate=pl.CostEstimate(flops=60_000_000_000,bytes_accessed=550_000_000,transcendentals=8_000_000),
        compiler_params=pltpu.CompilerParams(collective_id=cid,has_side_effects=True,vmem_limit_bytes=60*1024*1024),
    )(cut(grads),cut(two),grad_out,gain,w_out,q,kt,k,v,cosine,sine,down,residual,early,mixed,cut(normed),mix)


AXIS="tensor"
DP="dp"
MESH=pl.DeviceIdType.MESH

def greet(here, count, plane=0):
    barrier=pltpu.get_barrier_semaphore()
    if plane:
        def call(k,_):
            pl.semaphore_signal(barrier,inc=1,device_id={DP:lax.rem(lax.axis_index(DP)+k,plane)},device_id_type=MESH)
            return 0
        lax.fori_loop(1,plane,call,0)
        for k in range(1,count):
            pl.semaphore_signal(barrier,inc=1,device_id={AXIS:lax.rem(here+k,count)},device_id_type=MESH)
        pl.semaphore_wait(barrier,plane+count-2)
    else:
        @pl.when(here>0)
        def _(): pl.semaphore_signal(barrier,inc=1,device_id={AXIS:here-1},device_id_type=MESH)
        @pl.when(here<count-1)
        def _(): pl.semaphore_signal(barrier,inc=1,device_id={AXIS:here+1},device_id_type=MESH)
        pl.semaphore_wait(barrier,jnp.where((here>0)&(here<count-1),2,1))

def swap(axis, count, source, landing, sends, recvs):
    me=lax.axis_index(axis)
    def copy(peer, slot, k):
        return pltpu.make_async_remote_copy(src_ref=source(peer),dst_ref=landing.at[slot],send_sem=sends.at[k],
            recv_sem=recvs.at[slot],device_id={axis:peer},device_id_type=MESH)
    def begin(k,_):
        copy(lax.rem(me+k,count),me,k).start()
        return 0
    def end(k,_):
        peer=lax.rem(me+k,count)
        copy(peer,peer,k).wait_recv()
        copy(peer,me,k).wait_send()
        return 0
    return (lambda: lax.fori_loop(1,count,begin,0)),(lambda: lax.fori_loop(1,count,end,0))

def remote(src,dst,send,recv,target):
    return pltpu.make_async_remote_copy(src_ref=src,dst_ref=dst,send_sem=send,recv_sem=recv,
        device_id={AXIS:target},device_id_type=MESH)

class Line:
    def __init__(self,count,pieces,rows,part=None,sums=None,sum_sems=None,held=None,held_sems=None,base=0,sub=None):
        self.n,self.pieces,self.rows=count,pieces,rows
        self.sub=rows//pieces if sub is None else sub
        self.base=base
        self.here=lax.axis_index(AXIS)
        self.part,self.sums,self.sum_sems=part,sums,sum_sems
        self.held,self.held_sems=held,held_sems
    def span(self,u): return pl.ds(pl.multiple_of(self.base+u*self.sub,self.sub),self.sub)
    def fits(self,u): return (u>=0)&(u<self.pieces)
    def _target(self,way):
        return lax.min(self.here+1,self.n-1) if way==0 else lax.max(self.here-1,0)
    def slot(self,way,j,device):
        return j if way==0 else jnp.where(j==device,self.n,j)
    def sum_copy(self,way,j,u,first):
        sends,recvs=self.sum_sems
        dst=self.sums.at[self.slot(way,j,self._target(way)),self.span(u)]
        src=self.part.at[j,self.span(u)] if first else self.sums.at[self.slot(way,j,self.here),self.span(u)]
        return remote(src,dst,sends.at[way,j,u],recvs.at[way,j,u],self._target(way))
    def sum_arrival(self,way,j,u):
        sends,recvs=self.sum_sems
        ref=self.sums.at[self.slot(way,j,self.here),self.span(u)]
        return remote(ref,ref,sends.at[way,j,u],recvs.at[way,j,u],self._target(way))
    def relay(self,way,j,u,begins,passes):
        @pl.when(begins)
        def _(): self.sum_copy(way,j,u,True).start()
        @pl.when(passes)
        def _():
            self.sum_arrival(way,j,u).wait_recv()
            ref=self.sums.at[j,self.span(u)]
            ref[...]=(ref[...].astype(F32)+self.part[j,self.span(u)].astype(F32)).astype(BF)
            self.sum_copy(way,j,u,False).start()
    def far_steps(self): return (self.n-1)*self.pieces+1
    def far_step(self,t,total,finish):
        here,n,S=self.here,self.n,self.pieces
        for way in (0,1):
            q=t-here if way==0 else t-(n-1-here)
            ok=(q>=0)&(q<S*(n-1-here if way==0 else here))
            q=jnp.clip(q,0,S*(n-1)-1)
            j=n-1-q//S if way==0 else q//S
            end=(here==0) if way==0 else (here==n-1)
            self.relay(way,j,q%S,ok&end,ok&jnp.logical_not(end))
        u=t-(n-2)*S-1
        @pl.when(self.fits(u))
        def _():
            self.own_sum(u,total)
            finish(self.span(u),total)
    def send_sums(self,t):
        here,n=self.here,self.n
        for k in range(n-1):
            for way,j in ((0,n-1-k),(1,k)):
                u=t-here-(n-1-j) if way==0 else t-(n-1-here)-j
                ok=self.fits(u)
                u=jnp.clip(u,0,self.pieces-1)
                begins=(here==0) if way==0 else (here==n-1)
                passes=((here>0)&(here<j)) if way==0 else ((here<n-1)&(here>j))
                self.relay(way,j,u,ok&begins,ok&passes)
    def sweep_steps(self): return self.pieces+2*(self.n-1)
    def sweep(self,t,total,finish):
        far=self.n-1
        self.send_sums(t)
        u=t-far
        @pl.when(self.fits(u))
        def _():
            self.own_sum(u,total)
            self.held[self.here,self.span(u)]=finish(self.span(u),total)
            self.send_own(u)
        self.pass_pieces(t-far)
    def own_sum(self,u,total):
        here,n=self.here,self.n
        total[...]=self.part[here,self.span(u)].astype(F32)
        for way in (0,1):
            @pl.when(here>0 if way==0 else here<n-1)
            def _():
                self.sum_arrival(way,here,u).wait_recv()
                total[...]+=self.sums[self.slot(way,here,here),self.span(u)].astype(F32)
    def end_sums(self):
        here,n=self.here,self.n
        def one(u,_):
            for k in range(n-1):
                for way,j in ((0,n-1-k),(1,k)):
                    @pl.when((here<j) if way==0 else (here>j))
                    def _(): self.sum_copy(way,j,u,False).wait_send()
            return 0
        lax.fori_loop(0,self.pieces,one,0)
    def piece_copy(self,way,c,u,src=None):
        sends,recvs=self.held_sems
        dst=self.held.at[c,self.span(u)]
        return remote(dst if src is None else src,dst,sends.at[way,c,u],recvs.at[way,c,u],self._target(way))
    def send_own(self,u,src=None):
        here,n=self.here,self.n
        for way in (0,1):
            @pl.when(here<n-1 if way==0 else here>0)
            def _(): self.piece_copy(way,here,u,src).start()
    def gather_step(self,t,source):
        if t==0:
            for u in range(min(2,self.pieces)): self.send_own(u,source.at[self.span(u),:])
        else:
            self.pass_pieces(t)
            if t+1<self.pieces: self.send_own(t+1,source.at[self.span(t+1),:])
    def gather_steps(self): return self.pieces+self.n-1
    def pass_pieces(self,t,use=None):
        here,n=self.here,self.n
        for k in range(1,n):
            u=t-k
            ok=self.fits(u)
            u=jnp.clip(u,0,self.pieces-1)
            for way in (0,1):
                c=here-k if way==0 else here+k
                there=ok&((c>=0) if way==0 else (c<n))
                c=jnp.clip(c,0,n-1)
                @pl.when(there)
                def _(): self.piece_copy(way,c,u).wait_recv()
                @pl.when(there&(here<n-1 if way==0 else here>0))
                def _(): self.piece_copy(way,c,u).start()
                if use is not None:
                    @pl.when(there)
                    def _(): use(c,u)
    def end_pieces(self):
        here,n=self.here,self.n
        def one(u,_):
            for k in range(n):
                for way in (0,1):
                    c=here-k if way==0 else here+k
                    there=(c>=0) if way==0 else (c<n)
                    c=jnp.clip(c,0,n-1)
                    @pl.when(there&(here<n-1 if way==0 else here>0))
                    def _(): self.piece_copy(way,c,u).wait_send()
            return 0
        lax.fori_loop(0,self.pieces,one,0)

def gain_terms(part,other,acc,c):
    rows=part.shape[1]
    def some(k,_):
        span=pl.ds(pl.multiple_of(k*16,16),16)
        both=part[c,span].astype(F32)*other[c,span].astype(F32)
        acc[...]+=both[:8]+both[8:]
        return 0
    lax.fori_loop(0,rows//16,some,0)

def last_kernel(count, plane, pieces, part_hbm, other_hbm, tokens_hbm, grads_hbm, gain, terms, out, shared, part, other, tokens, grads, cs, sums, total, ss, sr, acc, cut, landed, level, stacked, ds, dr, zs, zr):
    width=part.shape[2]
    line=Line(count,pieces,part.shape[1],part,sums,(ss,sr))
    loads=[pltpu.make_async_copy(s,d,cs.at[k]) for k,(s,d) in enumerate(((part_hbm,part),(other_hbm,other),(tokens_hbm,tokens),(grads_hbm,grads)))]
    for load in loads: load.start()
    greet(line.here,count,plane)
    loads[0].wait()
    acc[...]=jnp.zeros_like(acc)
    me=lax.axis_index(DP)
    piece=width//plane
    begin_dp,end_dp=swap(DP,plane,lambda p: cut.at[p],landed,ds,dr)
    begin_z,end_z=swap(AXIS,count,lambda p: level,stacked,zs,zr)
    def finish(span,total):
        stream=tokens[span,:].astype(F32)
        scale=lax.rsqrt(jnp.mean(stream*stream,-1,keepdims=True)+EPSILON)
        unit=stream*scale
        scaled=total[...]*gain[0:1,:]
        out[span,:]=grads[span,:]+scale*(scaled-unit*jnp.mean(scaled*unit,-1,keepdims=True))
    def step(t,_):
        line.far_step(t,total,finish)
        @pl.when(t==0)
        def _():
            for load in loads[1:]: load.wait()
        @pl.when(t<count)
        def _(): gain_terms(part,other,acc,jnp.clip(t,0,count-1))
        @pl.when(t==count-1)
        def _():
            for p in range(plane):
                cut[p,0:8,:]=acc[:,p*piece:(p+1)*piece]
                cut[p,8:16,:]=terms[:,p*piece:(p+1)*piece]
            landed[me]=cut[me]
            begin_dp()
        @pl.when(t==count+1)
        def _():
            end_dp()
            level[...]=jnp.sum(landed[...],0)
            stacked[line.here]=level[...]
            begin_z()
        return 0
    assert line.far_steps()>count+1
    lax.fori_loop(0,line.far_steps(),step,0)
    end_z()
    shared[...]=jnp.sum(stacked[...],0)
    line.end_sums()

def last_sums(part,other,tokens,grads,gains,terms,cid,pieces,n,plane):
    rows,D=tokens.shape
    vm=pl.BlockSpec(memory_space=pltpu.VMEM)
    hbm=pl.BlockSpec(memory_space=pl.ANY)
    sds=jax.ShapeDtypeStruct
    sem=pltpu.SemaphoreType.DMA
    w=D//plane
    return pl.pallas_call(functools.partial(last_kernel,n,plane,pieces),
        out_shape=(sds((rows,D),F32),sds((16,w),F32)),in_specs=[hbm]*4+[vm]*2,out_specs=(vm,vm),
        scratch_shapes=[pltpu.VMEM((n,rows,D),BF),pltpu.VMEM((n,rows,D),BF),pltpu.VMEM((rows,D),BF),pltpu.VMEM((rows,D),F32),sem((4,)),pltpu.VMEM((n+1,rows,D),BF),pltpu.VMEM((rows//pieces,D),F32),sem((2,n,pieces)),sem((2,n,pieces)),pltpu.VMEM((8,D),F32),
            pltpu.VMEM((plane,16,w),F32),pltpu.VMEM((plane,16,w),F32),pltpu.VMEM((16,w),F32),pltpu.VMEM((n,16,w),F32),
            sem((plane,)),sem((plane,)),sem((n,)),sem((n,))],
        cost_estimate=pl.CostEstimate(flops=0,bytes_accessed=270_000_000,transcendentals=0),
        compiler_params=pltpu.CompilerParams(collective_id=cid,has_side_effects=True,vmem_limit_bytes=56*1024*1024),
    )(part.reshape(n,rows,D),other.reshape(n,rows,D),tokens,grads,gains,terms)


def mlp_kernel(count,pieces,tile,grad_ref,res_hbm,x_hbm,early_hbm,wgu_hbm,wd_hbm,
        out_ref,part_hbm,wide_hbm,rest_hbm,x_ref,gr,product,gated,lifted,down,ring,tall,part_stage,wide_stage,res_ref,sums,total,
        hs,hr,ss,sr,ws,ts,ls,rs,xs,ps,os):
    length,hidden=product.shape
    width=x_ref.shape[1]
    rows=grad_ref.shape[0]
    half=rows//2
    first,second=hidden//tile,width//tile
    slots=ring.shape[0]
    begun=early_hbm.shape[1]
    spread=hs.shape[2]
    get=Line(count,spread,rows,held=gr,held_sems=(hs,hr),base=begun,sub=(rows-begun)//spread)
    line=Line(count,pieces,rows,down,sums,(ss,sr),sub=half//pieces)
    def strip(k,size): return pl.ds(pl.multiple_of(jnp.clip(k,0,size-1)*tile,tile),tile)
    def tall_load(k):
        slot=lax.rem(k,slots)
        @pl.when(k<2*first)
        def _(): pltpu.make_async_copy(wgu_hbm.at[:,strip(lax.rem(k,2)*first+k//2,2*first)],tall.at[slot],ts.at[slot]).start()
        @pl.when((k>=2*first)&(k<2*first+second))
        def _(): pltpu.make_async_copy(wd_hbm.at[:,strip(k-2*first,second)],tall.at[slot],ts.at[slot]).start()
    def tall_loaded(k):
        slot=lax.rem(k,slots)
        pltpu.make_async_copy(wd_hbm.at[:,pl.ds(0,tile)],tall.at[slot],ts.at[slot]).wait()
        return slot
    def load(k):
        slot=lax.rem(k,slots)
        @pl.when(k<first)
        def _(): pltpu.make_async_copy(wd_hbm.at[strip(k,first),:],ring.at[slot],ws.at[slot]).start()
        @pl.when((k>=first)&(k<first+2*second))
        def _():
            side=pl.ds(pl.multiple_of(lax.rem(k-first,2)*hidden,hidden),hidden)
            pltpu.make_async_copy(wgu_hbm.at[strip((k-first)//2,second),side],ring.at[slot],ws.at[slot]).start()
    def loaded(k):
        slot=lax.rem(k,slots)
        pltpu.make_async_copy(wd_hbm.at[pl.ds(0,tile),:],ring.at[slot],ws.at[slot]).wait()
        return slot
    def own(): return pltpu.make_async_copy(grad_ref,gr.at[get.here],ls.at[0])
    def early(c): return pltpu.make_async_copy(early_hbm.at[c],gr.at[c,pl.ds(0,begun)],ls.at[1+c])
    def rest(c): return pltpu.make_async_copy(down.at[c,pl.ds(half,half)],rest_hbm.at[c],rs.at[c])
    whole_x=pltpu.make_async_copy(x_hbm,x_ref,xs)
    whole_x.start()
    base=pltpu.make_async_copy(res_hbm.at[pl.ds(0,half)],res_ref,ls.at[1+count])
    base.start()
    for k in range(slots): tall_load(jnp.int32(k))
    greet(get.here,count)
    get.gather_step(0,grad_ref)
    own().start()
    for c in range(count):
        @pl.when(c!=get.here)
        def _(): early(c).start()
    whole_x.wait()
    hops=get.gather_steps()
    gather_marks=(1.5,2.75,4,6,8) if first==4 and second==4 and hops==6 else tuple(min(k+1,first+second) for k in range(hops-1))
    sum_marks=(0,3,5,6,7,9,12) if first==4 and second==4 and line.far_steps()==7 else tuple(min(k,first+4*second-1) for k in range(line.far_steps()))
    def gather_at(n,after=0.0):
        for k,mark in enumerate(gather_marks):
            if mark%1==after:
                @pl.when(n==int(mark))
                def _(): get.gather_step(k+1,grad_ref)
    def finish(span,total):
        out_ref[span,:]=(res_ref[span,:]+total[...]).astype(BF)
    def sum_at(n):
        for k,mark in enumerate(sum_marks):
            @pl.when(n==mark)
            def _(): line.far_step(jnp.int32(k),total,finish)
    def forward(n,_):
        gather_at(n)
        one=tall_loaded(2*n)
        two=tall_loaded(2*n+1)
        cols=strip(n,first)
        for c in range(count):
            if c: gather_at(n,c/count)
            span=slice(c*rows,(c+1)*rows)
            gate=jnp.dot(x_ref[span,:],tall[one],preferred_element_type=F32)
            up=jnp.dot(x_ref[span,:],tall[two],preferred_element_type=F32)
            sigmoid=1.0/(1.0+jnp.exp(-gate))
            active=gate*sigmoid
            product[span,cols]=(active*up).astype(BF)
            lifted[span,cols]=active.astype(BF)
            gated[span,cols]=(up*(sigmoid+active*(1.0-sigmoid))).astype(BF)
        tall_load(2*n+slots)
        tall_load(2*n+1+slots)
        return 0
    lax.fori_loop(0,first,forward,0)
    for k in range(slots): load(jnp.int32(k))
    def lower(n,_):
        gather_at(first+n)
        slot=tall_loaded(2*first+n)
        sums_here=jnp.dot(product[...],tall[slot],preferred_element_type=F32).astype(BF)
        cols=strip(n,second)
        for c in range(count): down[c,:,cols]=sums_here[c*rows:(c+1)*rows]
        tall_load(2*first+n+slots)
        return 0
    lax.fori_loop(0,second,lower,0)
    for c in range(count): rest(c).start()
    gather_at(jnp.int32(first+second))
    base.wait()
    own().wait()
    for c in range(count):
        @pl.when(c!=get.here)
        def _(): early(c).wait()
    def back(n,_):
        sum_at(n)
        slot=loaded(n)
        cols=strip(n,first)
        for c in range(count):
            span=slice(c*rows,(c+1)*rows)
            grads=lax.dot_general(gr[c],ring[slot],(((1,),(1,)),((),())),preferred_element_type=F32)
            gated[span,cols]=(grads*gated[span,cols].astype(F32)).astype(BF)
            lifted[span,cols]=(grads*lifted[span,cols].astype(F32)).astype(BF)
        load(n+slots)
        return 0
    lax.fori_loop(0,first,back,0)
    def part_copy(n):
        slot=lax.rem(n,2)
        return pltpu.make_async_copy(part_stage.at[slot],part_hbm.at[:,strip(n,second)],ps.at[slot])
    def inner(n,_):
        sum_at(first+n)
        k=first+2*n
        one=loaded(k)
        both=lax.dot_general(gated[...],ring[one],(((1,),(1,)),((),())),preferred_element_type=F32)
        load(k+slots)
        two=loaded(k+1)
        both=both+lax.dot_general(lifted[...],ring[two],(((1,),(1,)),((),())),preferred_element_type=F32)
        @pl.when(n>=2)
        def _(): part_copy(n-2).wait()
        part_stage[lax.rem(n,2)]=both.astype(BF)
        part_copy(n).start()
        load(k+1+slots)
        return 0
    lax.fori_loop(0,second,inner,0)
    def wide_copy(n):
        slot=lax.rem(n,2)
        side=pl.ds(pl.multiple_of(lax.rem(n,3)*hidden,hidden),hidden)
        return pltpu.make_async_copy(wide_stage.at[slot],wide_hbm.at[strip(n//3,second),side],os.at[slot])
    cut=hidden//2
    def weights(m,_):
        cols=strip(m,second)
        for kind in range(3):
            n=3*m+kind
            sum_at(first+second+n)
            @pl.when(n>=2)
            def _(): wide_copy(n-2).wait()
            left=gr[:,:,cols].reshape(length,tile) if kind==2 else x_ref[:,cols]
            right=(gated,lifted,product)[kind]
            for side in (0,1):
                these=slice(side*cut,(side+1)*cut)
                wide_stage[lax.rem(n,2),:,these]=lax.dot_general(left,right[:,these],(((0,),(0,)),((),())),preferred_element_type=F32).astype(BF)
            wide_copy(n).start()
        return 0
    lax.fori_loop(0,second,weights,0)
    get.end_pieces()
    line.end_sums()
    for c in range(count): rest(c).wait()
    for n in range(max(0,second-2),second): part_copy(jnp.int32(n)).wait()
    for n in range(3*second-2,3*second): wide_copy(jnp.int32(n)).wait()

def mlp(x,grad_out,residual,early,w_both,w_down,cid,spread,pieces,count):
    length,width=x.shape
    hidden=w_down.shape[0]
    rows=length//count
    tile=min(512,hidden,width)
    vm=pl.BlockSpec(memory_space=pltpu.VMEM)
    hbm=pl.BlockSpec(memory_space=pl.ANY)
    sds=jax.ShapeDtypeStruct
    sem=pltpu.SemaphoreType.DMA
    vmem=pltpu.VMEM
    half=rows//2
    return pl.pallas_call(functools.partial(mlp_kernel,count,pieces,tile),
        out_shape=(sds((half,width),BF),sds((length,width),BF),sds((width,3*hidden),BF),sds((count,half,width),BF)),
        in_specs=[vm,hbm,hbm,hbm,hbm,hbm],
        out_specs=(vm,hbm,hbm,hbm),
        scratch_shapes=[vmem((length,width),BF),vmem((count,rows,width),BF),vmem((length,hidden),BF),vmem((length,hidden),BF),vmem((length,hidden),BF),
            vmem((count,rows,width),BF),vmem((4,tile,width),BF),vmem((4,width,tile),BF),vmem((2,length,tile),BF),vmem((2,tile,hidden),BF),vmem((half,width),F32),
            vmem((count+1,half,width),BF),vmem((half//pieces,width),F32),
            sem((2,count,spread)),sem((2,count,spread)),sem((2,count,pieces)),sem((2,count,pieces)),sem((4,)),sem((4,)),sem((count+2,)),sem((count,)),sem,
            sem((2,)),sem((2,))],
        cost_estimate=pl.CostEstimate(flops=78_000_000_000,bytes_accessed=380_000_000,transcendentals=0),
        compiler_params=pltpu.CompilerParams(collective_id=cid,has_side_effects=True,vmem_limit_bytes=60*1024*1024),
    )(grad_out,residual,x,early,w_both,w_down)


def frequencies(head_size):
    inverse = 1.0 / 500000.0 ** (jnp.arange(head_size // 2, dtype=jnp.float32) * 2.0 / head_size)
    wavelength = 2.0 * math.pi / inverse
    smooth = (8192.0 / wavelength - 1.0) / 3.0
    blended = (1.0 - smooth) * inverse / 32.0 + smooth * inverse
    return jnp.where(
        wavelength > 8192.0, inverse / 32.0, jnp.where(wavelength < 2048.0, inverse, blended)
    )


def dot(left_side, right_side, left_dim, right_dim):
    return lax.dot_general(
        left_side, right_side, (((left_dim,), (right_dim,)), ((), ())), preferred_element_type=F32
    )


def norm_kernel(count, plane, pieces, tokens_ref, gains_ref, gate_hbm, up_hbm, angles_ref, normed_hbm, gains_out, both_hbm, cosine, sine, held, normed, landed, hs, hr, ds, dr, ws, bs):
    hidden = gate_hbm.shape[1]
    sides = [
        pltpu.make_async_copy(source, both_hbm.at[:, pl.ds(k * hidden, hidden)], bs.at[k])
        for k, source in enumerate((gate_hbm, up_hbm))
    ]
    line = Line(count, pieces, tokens_ref.shape[0], held=held, held_sems=(hs, hr))
    greet(line.here, count, plane)
    me = lax.axis_index(DP)
    begin, end = swap(DP, plane, lambda p: gains_ref, landed, ds, dr)
    for u in range(pieces):
        line.send_own(u, tokens_ref.at[line.span(u), :])
    begin()
    for side in sides:
        side.start()
    landed[me] = gains_ref[...]
    end()
    piece = gains_ref.shape[1]
    for p in range(plane):
        gains_out[:, p * piece : (p + 1) * piece] = landed[p]

    def give(c, u):
        return pltpu.make_async_copy(normed.at[c, line.span(u)], normed_hbm.at[c, line.span(u)], ws.at[c, u])

    def norm(rows, c, u):
        stream = rows.astype(F32)
        scale = lax.rsqrt(jnp.mean(stream * stream, -1, keepdims=True) + EPSILON)
        normed[c, line.span(u)] = (stream * scale * gains_out[0:1, :]).astype(BF)
        give(c, u).start()

    def step(t, _):
        line.pass_pieces(t)
        for k in range(1, count):
            u = t - k
            for c in (line.here - k, line.here + k):

                @pl.when(line.fits(u) & (c >= 0) & (c < count))
                def _():
                    place, piece = jnp.clip(c, 0, count - 1), jnp.clip(u, 0, pieces - 1)
                    norm(held[place, line.span(piece)], place, piece)

        @pl.when(t == 1)
        def _():
            cosine[...] = jnp.cos(angles_ref[...])
            sine[...] = jnp.sin(angles_ref[...])

        @pl.when(t < pieces)
        def _():
            u = jnp.clip(t, 0, pieces - 1)
            norm(tokens_ref[line.span(u), :], line.here, u)

        return 0

    lax.fori_loop(0, pieces + count - 1, step, 0)
    line.end_pieces()
    for side in sides:
        side.wait()
    for c in range(count):
        for u in range(pieces):
            give(c, u).wait()


def norm_and_gather(tokens, gains, w_gate, w_up, angles, cid, pieces, count, plane):
    rows, width = tokens.shape
    vm = pl.BlockSpec(memory_space=pltpu.VMEM)
    sem = pltpu.SemaphoreType.DMA
    hbm = pl.BlockSpec(memory_space=pl.ANY)
    sds = jax.ShapeDtypeStruct
    normed, *rest = pl.pallas_call(
        functools.partial(norm_kernel, count, plane, pieces),
        out_shape=(
            sds((count, rows, width), BF),
            sds((8, width), F32),
            sds((w_gate.shape[0], 2 * w_gate.shape[1]), BF),
            sds(angles.shape, F32),
            sds(angles.shape, F32),
        ),
        in_specs=[vm, vm, hbm, hbm, vm],
        out_specs=(hbm, vm, hbm, vm, vm),
        scratch_shapes=[
            pltpu.VMEM((count, rows, width), BF),
            pltpu.VMEM((count, rows, width), BF),
            pltpu.VMEM((plane, 8, width // plane), F32),
            sem((2, count, pieces)),
            sem((2, count, pieces)),
            sem((plane,)),
            sem((plane,)),
            sem((count, pieces)),
            sem((2,)),
        ],
        cost_estimate=pl.CostEstimate(flops=0, bytes_accessed=270_000_000, transcendentals=0),
        compiler_params=pltpu.CompilerParams(
            collective_id=cid, has_side_effects=True, vmem_limit_bytes=58 * 1024 * 1024
        ),
    )(tokens, gains, w_gate, w_up, angles)
    return normed.reshape(count * rows, width), *rest


def wide_results_kernel(gate_in, up_in, down_in, tokens_in, block_in, sums_ref, gains_ref, gate, up, down, tokens, block, terms):
    tokens[...] = tokens_in[...]
    block[...] = block_in[...]
    terms[0:1, :] = jnp.sum(sums_ref[0:8, :], 0, keepdims=True) / gains_ref[0:1, :]
    terms[1:2, :] = jnp.sum(sums_ref[8:16, :], 0, keepdims=True) / gains_ref[1:2, :]
    gate[...] = gate_in[...].astype(F32)
    up[...] = up_in[...].astype(F32)
    down[...] = down_in[...].astype(F32).T


def wide_results(wide, grad_tokens, block_out, sums, gains, hidden):
    shard = wide.shape[0]
    tile = min(512, hidden)
    steps = hidden // tile
    sds = jax.ShapeDtypeStruct
    still = lambda shape: pl.BlockSpec(shape, lambda s: (0, 0))
    strip = pl.BlockSpec((grad_tokens.shape[0], grad_tokens.shape[1] // steps), lambda s: (0, s))
    return pl.pallas_call(
        wide_results_kernel,
        grid=(steps,),
        out_shape=(
            sds((shard, hidden), F32),
            sds((shard, hidden), F32),
            sds((hidden, shard), F32),
            sds(grad_tokens.shape, F32),
            sds(block_out.shape, BF),
            sds((2, shard), F32),
        ),
        in_specs=[pl.BlockSpec((shard, tile), lambda s, k=k: (0, k * steps + s)) for k in range(3)]
        + [strip, strip, still(sums.shape), still(gains.shape)],
        out_specs=(
            pl.BlockSpec((shard, tile), lambda s: (0, s)),
            pl.BlockSpec((shard, tile), lambda s: (0, s)),
            pl.BlockSpec((tile, shard), lambda s: (s, 0)),
            strip,
            strip,
            still((2, shard)),
        ),
        compiler_params=pltpu.CompilerParams(vmem_limit_bytes=60 * 1024 * 1024),
    )(wide, wide, wide, grad_tokens, block_out, sums, gains)


def mix_results_kernel(mix_ref, terms_ref, query, key, value, out, first, second):
    edge = query.shape[1]
    query[...] = mix_ref[:, :edge].astype(F32)
    key[...] = mix_ref[:, edge : edge + key.shape[1]].astype(F32)
    edge += key.shape[1]
    value[...] = mix_ref[:, edge : edge + value.shape[1]].astype(F32)
    edge += value.shape[1]
    out[...] = mix_ref[:, edge:].astype(F32).T
    first[...] = terms_ref[0:1, :]
    second[...] = terms_ref[1:2, :]


def mix_results(mix, terms, deep, narrow):
    shard = mix.shape[0]
    sds = jax.ShapeDtypeStruct
    vm = pl.BlockSpec(memory_space=pltpu.VMEM)
    return pl.pallas_call(
        mix_results_kernel,
        out_shape=(
            sds((shard, deep), F32),
            sds((shard, narrow), F32),
            sds((shard, narrow), F32),
            sds((deep, shard), F32),
            sds((1, shard), F32),
            sds((1, shard), F32),
        ),
        in_specs=[vm, vm],
        out_specs=(vm,) * 6,
        compiler_params=pltpu.CompilerParams(vmem_limit_bytes=60 * 1024 * 1024),
    )(mix, terms)


def body(
    count,
    plane,
    tokens,
    segments,
    positions,
    attn_gain,
    w_query,
    w_key,
    w_value,
    w_out,
    mlp_gain,
    w_gate,
    w_up,
    w_down,
    grad_out,
):
    rows, width = tokens.shape
    heads = w_query.shape[1] // HD
    groups = w_key.shape[1] // HD
    after = lax.optimization_barrier
    mix = lax.all_gather(jnp.concatenate([w_query, w_key, w_value], 1), DP, axis=0, tiled=True)
    full_out = lax.all_gather(w_out, DP, axis=1, tiled=True)
    full_down = lax.all_gather(w_down, DP, axis=1, tiled=True)
    own_gains = jnp.concatenate([jnp.stack([attn_gain, mlp_gain]).astype(F32), jnp.zeros((6, attn_gain.shape[0]), F32)])

    angles = frequencies(HD)[:, None] * positions.astype(F32)[None, :]
    normed_one, gains, both, cosine, sine = norm_and_gather(tokens, own_gains, w_gate, w_up, angles, 1, 4, count, plane)
    full_both = lax.all_gather(both, DP, axis=0, tiled=True)

    mixed, q, kt, k, v, residual, early, normed_two = attend(
        mix, normed_one, cosine, sine, segments, full_out, grad_out, tokens, gains, heads, groups, 6, rows * 5 // 8, 5, 16, count
    )
    normed_two = normed_two.reshape(count * rows, width)
    block_early, part, grad_wide, down = mlp(normed_two, grad_out, residual, early, full_both, full_down, 5, 3, 2, count)
    grad_wide = lax.psum_scatter(grad_wide, DP, scatter_dimension=0, tiled=True)
    grad_residual, terms_two, part, grad_mix, block_out = attend_back(
        part, normed_two, grad_out, gains, full_out, q, kt, k, v, cosine, sine, down, residual, block_early,
        mixed, normed_one, mix, heads, groups, 7, 2, 16, count,
    )
    grad_mix = lax.psum_scatter(grad_mix, DP, scatter_dimension=0, tiled=True)
    grad_tokens, sums = last_sums(part, normed_one, tokens, grad_residual, gains, terms_two, 4, 4, count, plane)
    grad_gate, grad_up, grad_down, grad_tokens, block_out, terms = wide_results(
        grad_wide, grad_tokens, block_out, sums, own_gains, full_down.shape[0]
    )
    grad_query, grad_key, grad_value, grad_out_proj, grad_attn_gain, grad_mlp_gain = mix_results(
        grad_mix, terms, heads * HD, groups * HD
    )
    return (
        block_out,
        grad_tokens,
        grad_attn_gain.reshape(-1),
        grad_query,
        grad_key,
        grad_value,
        grad_out_proj,
        grad_mlp_gain.reshape(-1),
        grad_gate,
        grad_up,
        grad_down,
    )


def solution(mesh):
    placed = (
        P(("dp", "tensor"), None),
        P("dp"),
        P("dp"),
        P("dp"),
        P("dp", "tensor"),
        P("dp", "tensor"),
        P("dp", "tensor"),
        P("tensor", "dp"),
        P("dp"),
        P("dp", "tensor"),
        P("dp", "tensor"),
        P("tensor", "dp"),
        P(("dp", "tensor"), None),
    )
    return jax.shard_map(
        functools.partial(body, mesh.shape["tensor"], mesh.shape["dp"]),
        mesh=mesh,
        in_specs=placed,
        out_specs=(
            P(("dp", "tensor"), None),
            P(("dp", "tensor"), None),
            P("dp"),
            P("dp", "tensor"),
            P("dp", "tensor"),
            P("dp", "tensor"),
            P("tensor", "dp"),
            P("dp"),
            P("dp", "tensor"),
            P("dp", "tensor"),
            P("tensor", "dp"),
        ),
        check_vma=False,
    )
```

```python
import functools
import math

import jax
import jax.numpy as jnp
from jax import lax
from jax.experimental import pallas as pl
from jax.experimental.pallas import tpu as pltpu
from jax.sharding import PartitionSpec as P

HD = 64
EPSILON = 1e-05
MASKED = -1e30
F32 = jnp.float32
BF = jnp.bfloat16

def turn_t(values, cosine, sine, sign):
    half=values.shape[0]//2
    first, second = values[:half], values[half:]
    return jnp.concatenate([first*cosine - sign*second*sine, second*cosine + sign*first*sine],0)

AUG=80

def thirds(x):
    one=x.astype(BF)
    rest=x-one.astype(F32)
    two=rest.astype(BF)
    three=(rest-two.astype(F32)).astype(BF)
    return [part.astype(F32) for part in (one,two,three)]

def tail_rows(rows,width):
    return jnp.concatenate(rows+[jnp.zeros((AUG-HD-len(rows),width),F32)],0)

def triangle(block):
    keys=lax.broadcasted_iota(jnp.int32,(block,block),0)
    queries=lax.broadcasted_iota(jnp.int32,(block,block),1)
    return jnp.where(keys<=queries,0.0,MASKED).astype(F32)

def attend_kernel(heads, groups, block, count, pieces, fine, mix_hbm, normed_hbm, cos_ref, sin_ref, segr_ref, wo_hbm, grad_ref, tokens_hbm, gain_ref,
                  mixed_ref, q_ref, kt_ref, k_ref, v_ref, residual_ref, rows_hbm, whole_hbm,
                  mix_ref, normed_ref, lin_ref, tri_ref, vt_ref, wo_ref, tokens_ref, part_ref, held, hs, hr, sums, total, ss, sr, moved, ms, mr, cs):
    length=normed_ref.shape[0]
    per=heads//groups
    rows=grad_ref.shape[0]
    early=held.shape[1]
    line=Line(count,pieces,rows,held=held,held_sems=(hs,hr),sub=early//pieces)
    inputs=[pltpu.make_async_copy(s,d,cs.at[4+k]) for k,(s,d) in enumerate(((normed_hbm,normed_ref),(mix_hbm,mix_ref)))]
    for copy in inputs: copy.start()
    greet(line.here,count)
    line.gather_step(0,grad_ref)
    for copy in inputs: copy.wait()
    weights=pltpu.make_async_copy(wo_hbm,wo_ref,cs.at[0])
    weights.start()
    stream=pltpu.make_async_copy(tokens_hbm,tokens_ref,cs.at[1])
    stream.start()
    lines=mix_ref.shape[1]
    cut=256 if lines%256==0 else lines
    for c in range(0,lines,cut):
        lin_ref[c:c+cut,:]=lax.dot_general(mix_ref[:,c:c+cut],normed_ref[...],(((0,),(1,)),((),())),preferred_element_type=F32)
    steps=line.gather_steps()
    done=0
    def tick():
        nonlocal done
        if done+1<steps:
            done+=1
            line.gather_step(done,grad_ref)
    cosine, sine = cos_ref[...], sin_ref[...]
    segs=segr_ref[...]
    apart=[jnp.where(segs==s,MASKED,0.0).astype(F32) for s in range(3)]
    others=[jnp.where(segs==s,0.0,1.0).astype(F32) for s in range(3)]
    ones=jnp.ones((1,length),F32)
    plain=tail_rows(apart,length).astype(BF)
    def rope(h,_):
        rows=pl.ds(pl.multiple_of(h*HD,HD),HD)
        q_ref[h,0:HD,:]=(turn_t(lin_ref[rows,:],cosine,sine,1.0).astype(BF)*jnp.asarray(0.125,BF))
        q_ref[h,HD:,:]=plain
        return 0
    lax.fori_loop(0,heads,rope,0)
    beside=tail_rows(others+[ones]*3,length)
    below=tail_rows([ones]*3,length)
    for g in range(groups):
        keys_t=turn_t(lin_ref[(heads+g)*HD:(heads+g+1)*HD,:],cosine,sine,1.0)
        kt_ref[g*HD:(g+1)*HD,:]=keys_t.astype(BF)
        k_ref[g]=jnp.concatenate([keys_t,beside],0).T.astype(BF)
        vals_t=jnp.concatenate([lin_ref[(heads+groups+g)*HD:(heads+groups+g+1)*HD,:],below],0)
        vt_ref[g]=vals_t.astype(BF)
        v_ref[g]=vals_t.T.astype(BF)
    tri_ref[...]=triangle(block)
    for start in range(0,length,block):
        cols=slice(start,start+block)
        if start in (0,2*block): tick()
        def head(h,_):
            g=h//per
            rows=pl.ds(pl.multiple_of(h*HD,HD),HD)
            query=q_ref[h,:,cols]
            parts=[jnp.dot(k_ref[g,c:c+block,:],query,preferred_element_type=F32) for c in range(0,start+block,block)]
            parts[-1]=parts[-1]+tri_ref[...]
            top=functools.reduce(jnp.maximum,[jnp.max(part,0,keepdims=True) for part in parts])
            out=functools.reduce(jnp.add,[jnp.dot(vt_ref[g,:,k*block:(k+1)*block],jnp.exp(part-top).astype(BF),preferred_element_type=F32)
                for k,part in enumerate(parts)])
            total=out[HD:HD+1]
            mixed_ref[rows,cols]=(out[:HD]/total).astype(BF)
            logs=thirds(top+jnp.log(total))
            q_ref[h,HD:,cols]=tail_rows([row[:,cols] for row in apart]+[-x for x in logs],block).astype(BF)
            return 0
        lax.fori_loop(0,heads,head,0,unroll=2)
    width=wo_ref.shape[1]
    wide=min(512,width)
    weights.wait()
    tick()
    def out(c,_):
        cols=pl.ds(pl.multiple_of(c*wide,wide),wide)
        product=lax.dot_general(mixed_ref[...],wo_ref[:,cols],(((0,),(0,)),((),())),preferred_element_type=F32).astype(BF)
        for j in range(count): part_ref[j,:,cols]=product[j*rows:(j+1)*rows]
        return 0
    lax.fori_loop(0,width//wide,out,0)
    held[line.here]=grad_ref[0:early,:]
    copy=pltpu.make_async_copy(held,rows_hbm,cs.at[2])
    stream.wait()
    sweep=Line(count,fine,rows,part_ref,sums,(ss,sr),moved,(ms,mr))
    def finish(span,total):
        residual=total[...]+tokens_ref[span,:].astype(F32)
        residual_ref[span,:]=residual
        scale=lax.rsqrt(jnp.mean(residual*residual,-1,keepdims=True)+EPSILON)
        return (residual*scale*gain_ref[1:2,:]).astype(BF)
    def step(t,_):
        sweep.sweep(t,total,finish)
        for k in range(done+1,steps):
            @pl.when(t==2*(k-done-1))
            def _(): line.gather_step(k,grad_ref)
        return 0
    lax.fori_loop(0,sweep.sweep_steps(),step,0)
    copy.start()
    last=pltpu.make_async_copy(moved,whole_hbm,cs.at[3])
    last.start()
    line.end_pieces()
    sweep.end_sums()
    sweep.end_pieces()
    copy.wait()
    last.wait()

def attend(mix, normed, cosine, sine, segments, w_out, grad_out, tokens, gain, heads, groups, cid, early, pieces, fine, count):
    length,width=normed.shape
    rows=grad_out.shape[0]
    block=min(256,length)
    sds=jax.ShapeDtypeStruct
    vm=pl.BlockSpec(memory_space=pltpu.VMEM)
    hbm=pl.BlockSpec(memory_space=pl.ANY)
    sem=pltpu.SemaphoreType.DMA
    vmem=pltpu.VMEM
    return pl.pallas_call(functools.partial(attend_kernel,heads,groups,block,count,pieces,fine),
        out_shape=(sds((heads*HD,length),BF),sds((heads,AUG,length),BF),
            sds((groups*HD,length),BF),sds((groups,length,AUG),BF),sds((groups,length,AUG),BF),
            sds((rows,width),F32),sds((count,early,width),BF),sds((count,rows,width),BF)),
        in_specs=[hbm,hbm]+[vm]*3+[hbm,vm,hbm,vm],out_specs=(vm,)*6+(hbm,hbm),
        scratch_shapes=[vmem(mix.shape,BF),vmem(normed.shape,BF),vmem((mix.shape[1],length),F32),vmem((block,block),F32),vmem((groups,AUG,length),BF),vmem(w_out.shape,BF),
            vmem(tokens.shape,BF),vmem((count,rows,width),BF),vmem((count,early,width),BF),sem((2,count,pieces)),sem((2,count,pieces)),
            vmem((count+1,rows,width),BF),vmem((rows//fine,width),F32),sem((2,count,fine)),sem((2,count,fine)),
            vmem((count,rows,width),BF),sem((2,count,fine)),sem((2,count,fine)),sem((6,))],
        cost_estimate=pl.CostEstimate(flops=30_000_000_000,bytes_accessed=500_000_000,transcendentals=8_000_000),
        compiler_params=pltpu.CompilerParams(collective_id=cid,has_side_effects=True,vmem_limit_bytes=58*1024*1024),
    )(mix,normed,cosine,sine,segments.reshape(1,length),w_out,grad_out,tokens,gain)

def attend_back_kernel(heads, groups, block, count, pieces, fine, grads_hbm, two_hbm, go_ref, gain_ref, wo_hbm, q_ref, kt_ref, k_ref, v_ref, cos_ref, sin_ref,
                  down_ref, res_ref, early_ref, mixed_hbm, normed_hbm, mix_hbm,
                  gres_ref, acc, part_hbm, grad_hbm, out_ref,
                  part_ref, normed_ref, low_ref, wide_sums, wide_total, ws, wr, hs, hr,
                  wo_ref, mixed_ref, mix_ref, turn_ref, gm_ref, tri_ref, qn_ref, gn_ref, dq_ref, dk_ref, dv_ref, sums, total, ss, sr, grad_ref, cs, gs_sem):
    length=q_ref.shape[2]
    per=heads//groups
    width=wo_ref.shape[1]
    rows=res_ref.shape[0]
    half=rows//2
    line=Line(count,pieces,half,down_ref,sums,(ss,sr))
    sweep=Line(count,fine,rows,part_ref,wide_sums,(ws,wr),low_ref,(hs,hr))
    first=pltpu.make_async_copy(grads_hbm,part_ref,cs.at[0])
    first.start()
    second=pltpu.make_async_copy(two_hbm,normed_ref,cs.at[1])
    second.start()
    late=[pltpu.make_async_copy(s,d,cs.at[2+k]) for k,(s,d) in enumerate(((mixed_hbm,mixed_ref),(mix_hbm,mix_ref),(wo_hbm,wo_ref)))]
    for copy in late: copy.start()
    greet(line.here,count)
    acc[...]=jnp.zeros_like(acc)
    out_ref[0:half,:]=early_ref[...]
    first.wait()
    def turn(span,total):
        residual=res_ref[span,:]
        scale=lax.rsqrt(jnp.mean(residual*residual,-1,keepdims=True)+EPSILON)
        unit=residual*scale
        scaled=total[...]*gain_ref[1:2,:]
        grads=go_ref[span,:].astype(F32)+scale*(scaled-unit*jnp.mean(scaled*unit,-1,keepdims=True))
        gres_ref[span,:]=grads
        return grads.astype(BF)
    def finish(span,total):
        places=pl.ds(pl.multiple_of(half+span.start,line.sub),line.sub)
        out_ref[places,:]=(res_ref[places,:]+total[...]).astype(BF)
    steps=sweep.sweep_steps()
    begun=2
    dk_ref[...]=jnp.zeros_like(dk_ref)
    dv_ref[...]=jnp.zeros_like(dv_ref)
    tri_ref[...]=triangle(block)
    def flip_query(p):
        qn=jnp.concatenate([q_ref[2*p,0:HD,:],q_ref[2*p+1,0:HD,:]],0).astype(F32).T.astype(BF)
        qn_ref[2*p]=qn[:,:HD]
        qn_ref[2*p+1]=qn[:,HD:]
    def step(t,_):
        sweep.sweep(t,wide_total,turn)
        @pl.when((t>=8)&(t<8+heads//2))
        def _(): flip_query(jnp.clip(t-8,0,heads//2-1))
        @pl.when(t==2)
        def _(): second.wait()
        @pl.when((t>=2)&(t<count+2))
        def _(): gain_terms(part_ref,normed_ref,acc,jnp.clip(t-2,0,count-1))
        for k in range(begun):
            @pl.when(t==steps-2*(begun-k))
            def _(): line.far_step(jnp.int32(k),total,finish)
        return 0
    lax.fori_loop(0,steps,step,0)
    third=pltpu.make_async_copy(normed_hbm,normed_ref,cs.at[1])
    third.start()
    ticks=[begun]
    def tick(amount=1):
        for _ in range(amount):
            if ticks[0]<line.far_steps():
                line.far_step(jnp.int32(ticks[0]),total,finish)
                ticks[0]+=1
    late[2].wait()
    whole=lambda: low_ref[...].reshape(length,width)
    cosine, sine = cos_ref[...], sin_ref[...]
    deep=heads*HD
    cut=256 if deep%256==0 else deep
    late[0].wait()
    for c in range(0,deep,cut):
        product=lax.dot_general(wo_ref[c:c+cut,:],whole(),(((1,),(1,)),((),())),preferred_element_type=F32).astype(BF)
        for h in range(c//HD,(c+cut)//HD):
            grads=product[h*HD-c:(h+1)*HD-c]
            gm_ref[h,0:HD,:]=grads
            centre=jnp.sum(grads.astype(F32)*mixed_ref[h*HD:(h+1)*HD,:].astype(F32),0,keepdims=True)
            gm_ref[h,HD:,:]=tail_rows([-x for x in thirds(centre)],length).astype(BF)
    def flip(p,_):
        gn=jnp.concatenate([gm_ref[2*p,0:HD,:],gm_ref[2*p+1,0:HD,:]],0).astype(F32).T.astype(BF)
        gn_ref[2*p]=gn[:,:HD]
        gn_ref[2*p+1]=gn[:,HD:]
        return 0
    lax.fori_loop(0,heads//2,flip,0)
    lines=(heads+2*groups)*HD
    strip=min(512,width)
    tick()
    for c in range(0,width,strip):
        grad_ref[c:c+strip,lines:]=lax.dot_general(low_ref[:,:,c:c+strip].reshape(length,strip),mixed_ref[...],(((0,),(1,)),((),())),preferred_element_type=F32).astype(BF)
    for start in range(0,length,block):
        cols=slice(start,start+block)
        spans=[slice(start,start+block)]+([slice(0,start)] if start else [])
        def head(h,_):
            g=h//per
            rows=pl.ds(pl.multiple_of(h*HD,HD),HD)
            grows=pl.ds(pl.multiple_of(g*HD,HD),HD)
            query,grads=q_ref[h,:,cols],gm_ref[h,:,cols]
            query_n,grads_n=qn_ref[h,cols,:],gn_ref[h,cols,:]
            total_q=None
            for k,span in enumerate(spans):
                scores=jnp.dot(k_ref[g,span,:],query,preferred_element_type=F32)
                if k==0: scores=scores+tri_ref[...]
                probs=jnp.exp(scores)
                dv_ref[g,span,:]+=jnp.dot(probs.astype(BF),grads_n,preferred_element_type=F32)
                gs=(probs*jnp.dot(v_ref[g,span,:],grads,preferred_element_type=F32)).astype(BF)
                dk_ref[g,span,:]+=jnp.dot(gs,query_n,preferred_element_type=F32)
                one=jnp.dot(kt_ref[grows,span],gs,preferred_element_type=F32)
                total_q=one if total_q is None else total_q+one
            dq_ref[rows,cols]=0.125*total_q
            return 0
        lax.fori_loop(0,heads,head,0,unroll=2)
        if start>0: tick()
    def back(h,_):
        rows=pl.ds(pl.multiple_of(h*HD,HD),HD)
        turn_ref[rows,:]=turn_t(dq_ref[rows,:],cosine,sine,-1.0).astype(BF)
        return 0
    lax.fori_loop(0,heads,back,0)
    dk=jnp.concatenate([dk_ref[g] for g in range(groups)],1).T
    dv=jnp.concatenate([dv_ref[g] for g in range(groups)],1).T
    for g in range(groups):
        turn_ref[(heads+g)*HD:(heads+g+1)*HD,:]=turn_t(dk[g*HD:(g+1)*HD],cosine,sine,-1.0).astype(BF)
    turn_ref[(heads+groups)*HD:,:]=dv.astype(BF)
    late[1].wait()
    sweep.end_sums()
    for c in range(0,width,strip):
        product=lax.dot_general(turn_ref[...],mix_ref[c:c+strip,:],(((0,),(1,)),((),())),preferred_element_type=F32).astype(BF)
        for j in range(count): part_ref[j,:,c:c+strip]=product[j*rows:(j+1)*rows]
    give=pltpu.make_async_copy(part_ref,part_hbm,cs.at[0])
    give.start()
    tick()
    third.wait()
    for k,c in enumerate(range(0,width,strip)):
        grad_ref[c:c+strip,0:lines]=lax.dot_general(normed_ref[:,:,c:c+strip].reshape(length,strip),turn_ref[...],(((0,),(1,)),((),())),preferred_element_type=F32).astype(BF)
        pltpu.make_async_copy(grad_ref.at[c:c+strip],grad_hbm.at[c:c+strip],gs_sem.at[k]).start()
    tick(line.far_steps())
    line.end_sums()
    sweep.end_pieces()
    give.wait()
    for k,c in enumerate(range(0,width,strip)):
        pltpu.make_async_copy(grad_ref.at[c:c+strip],grad_hbm.at[c:c+strip],gs_sem.at[k]).wait()

def attend_back(grads,two,grad_out,gain,w_out,q,kt,k,v,cosine,sine,down,residual,early,mixed,normed,mix,heads,groups,cid,pieces,fine,count):
    rows,width=residual.shape
    length=rows*count
    lines=mix.shape[1]
    block=min(256,length)
    vm=pl.BlockSpec(memory_space=pltpu.VMEM)
    hbm=pl.BlockSpec(memory_space=pl.ANY)
    vmem=pltpu.VMEM
    sds=jax.ShapeDtypeStruct
    sem=pltpu.SemaphoreType.DMA
    cut=lambda x: x.reshape(count,rows,width)
    return pl.pallas_call(functools.partial(attend_back_kernel,heads,groups,block,count,pieces,fine),
        out_shape=(sds((rows,width),F32),sds((8,width),F32),sds((count,rows,width),BF),sds((width,lines+heads*HD),BF),sds((rows,width),BF)),
        in_specs=[hbm,hbm,vm,vm,hbm]+[vm]*9+[hbm]*3,out_specs=(vm,vm,hbm,hbm,vm),
        scratch_shapes=[vmem((count,rows,width),BF),vmem((count,rows,width),BF),vmem((count,rows,width),BF),vmem((count+1,rows,width),BF),
            vmem((rows//fine,width),F32),sem((2,count,fine)),sem((2,count,fine)),sem((2,count,fine)),sem((2,count,fine)),
            vmem(w_out.shape,BF),vmem(mixed.shape,BF),vmem(mix.shape,BF),vmem((lines,length),BF),vmem((heads,AUG,length),BF),
            vmem((block,block),F32),vmem((heads,length,HD),BF),vmem((heads,length,HD),BF),
            vmem((heads*HD,length),F32),vmem((groups,length,HD),F32),vmem((groups,length,HD),F32),
            vmem((count+1,rows//2,width),BF),vmem((rows//2//pieces,width),F32),sem((2,count,pieces)),sem((2,count,pieces)),
            vmem((width,lines+heads*HD),BF),sem((5,)),sem((max(1,width//min(512,width)),))],
        cost_estimate=pl.CostEstimate(flops=60_000_000_000,bytes_accessed=550_000_000,transcendentals=8_000_000),
        compiler_params=pltpu.CompilerParams(collective_id=cid,has_side_effects=True,vmem_limit_bytes=60*1024*1024),
    )(cut(grads),cut(two),grad_out,gain,w_out,q,kt,k,v,cosine,sine,down,residual,early,mixed,cut(normed),mix)


AXIS="tensor"
DP="dp"
MESH=pl.DeviceIdType.MESH

def greet(here, count, plane=0):
    barrier=pltpu.get_barrier_semaphore()
    if plane:
        def call(k,_):
            pl.semaphore_signal(barrier,inc=1,device_id={DP:lax.rem(lax.axis_index(DP)+k,plane)},device_id_type=MESH)
            return 0
        lax.fori_loop(1,plane,call,0)
        for k in range(1,count):
            pl.semaphore_signal(barrier,inc=1,device_id={AXIS:lax.rem(here+k,count)},device_id_type=MESH)
        pl.semaphore_wait(barrier,plane+count-2)
    else:
        @pl.when(here>0)
        def _(): pl.semaphore_signal(barrier,inc=1,device_id={AXIS:here-1},device_id_type=MESH)
        @pl.when(here<count-1)
        def _(): pl.semaphore_signal(barrier,inc=1,device_id={AXIS:here+1},device_id_type=MESH)
        pl.semaphore_wait(barrier,jnp.where((here>0)&(here<count-1),2,1))

def swap(axis, count, source, landing, sends, recvs):
    me=lax.axis_index(axis)
    def copy(peer, slot, k):
        return pltpu.make_async_remote_copy(src_ref=source(peer),dst_ref=landing.at[slot],send_sem=sends.at[k],
            recv_sem=recvs.at[slot],device_id={axis:peer},device_id_type=MESH)
    def begin(k,_):
        copy(lax.rem(me+k,count),me,k).start()
        return 0
    def end(k,_):
        peer=lax.rem(me+k,count)
        copy(peer,peer,k).wait_recv()
        copy(peer,me,k).wait_send()
        return 0
    return (lambda: lax.fori_loop(1,count,begin,0)),(lambda: lax.fori_loop(1,count,end,0))

def remote(src,dst,send,recv,target):
    return pltpu.make_async_remote_copy(src_ref=src,dst_ref=dst,send_sem=send,recv_sem=recv,
        device_id={AXIS:target},device_id_type=MESH)

class Line:
    def __init__(self,count,pieces,rows,part=None,sums=None,sum_sems=None,held=None,held_sems=None,base=0,sub=None):
        self.n,self.pieces,self.rows=count,pieces,rows
        self.sub=rows//pieces if sub is None else sub
        self.base=base
        self.here=lax.axis_index(AXIS)
        self.part,self.sums,self.sum_sems=part,sums,sum_sems
        self.held,self.held_sems=held,held_sems
    def span(self,u): return pl.ds(pl.multiple_of(self.base+u*self.sub,self.sub),self.sub)
    def fits(self,u): return (u>=0)&(u<self.pieces)
    def _target(self,way):
        return lax.min(self.here+1,self.n-1) if way==0 else lax.max(self.here-1,0)
    def slot(self,way,j,device):
        return j if way==0 else jnp.where(j==device,self.n,j)
    def sum_copy(self,way,j,u,first):
        sends,recvs=self.sum_sems
        dst=self.sums.at[self.slot(way,j,self._target(way)),self.span(u)]
        src=self.part.at[j,self.span(u)] if first else self.sums.at[self.slot(way,j,self.here),self.span(u)]
        return remote(src,dst,sends.at[way,j,u],recvs.at[way,j,u],self._target(way))
    def sum_arrival(self,way,j,u):
        sends,recvs=self.sum_sems
        ref=self.sums.at[self.slot(way,j,self.here),self.span(u)]
        return remote(ref,ref,sends.at[way,j,u],recvs.at[way,j,u],self._target(way))
    def relay(self,way,j,u,begins,passes):
        @pl.when(begins)
        def _(): self.sum_copy(way,j,u,True).start()
        @pl.when(passes)
        def _():
            self.sum_arrival(way,j,u).wait_recv()
            ref=self.sums.at[j,self.span(u)]
            ref[...]=(ref[...].astype(F32)+self.part[j,self.span(u)].astype(F32)).astype(BF)
            self.sum_copy(way,j,u,False).start()
    def far_steps(self): return (self.n-1)*self.pieces+1
    def far_step(self,t,total,finish):
        here,n,S=self.here,self.n,self.pieces
        for way in (0,1):
            q=t-here if way==0 else t-(n-1-here)
            ok=(q>=0)&(q<S*(n-1-here if way==0 else here))
            q=jnp.clip(q,0,S*(n-1)-1)
            j=n-1-q//S if way==0 else q//S
            end=(here==0) if way==0 else (here==n-1)
            self.relay(way,j,q%S,ok&end,ok&jnp.logical_not(end))
        u=t-(n-2)*S-1
        @pl.when(self.fits(u))
        def _():
            self.own_sum(u,total)
            finish(self.span(u),total)
    def send_sums(self,t):
        here,n=self.here,self.n
        for k in range(n-1):
            for way,j in ((0,n-1-k),(1,k)):
                u=t-here-(n-1-j) if way==0 else t-(n-1-here)-j
                ok=self.fits(u)
                u=jnp.clip(u,0,self.pieces-1)
                begins=(here==0) if way==0 else (here==n-1)
                passes=((here>0)&(here<j)) if way==0 else ((here<n-1)&(here>j))
                self.relay(way,j,u,ok&begins,ok&passes)
    def sweep_steps(self): return self.pieces+2*(self.n-1)
    def sweep(self,t,total,finish):
        far=self.n-1
        self.send_sums(t)
        u=t-far
        @pl.when(self.fits(u))
        def _():
            self.own_sum(u,total)
            self.held[self.here,self.span(u)]=finish(self.span(u),total)
            self.send_own(u)
        self.pass_pieces(t-far)
    def own_sum(self,u,total):
        here,n=self.here,self.n
        total[...]=self.part[here,self.span(u)].astype(F32)
        for way in (0,1):
            @pl.when(here>0 if way==0 else here<n-1)
            def _():
                self.sum_arrival(way,here,u).wait_recv()
                total[...]+=self.sums[self.slot(way,here,here),self.span(u)].astype(F32)
    def end_sums(self):
        here,n=self.here,self.n
        def one(u,_):
            for k in range(n-1):
                for way,j in ((0,n-1-k),(1,k)):
                    @pl.when((here<j) if way==0 else (here>j))
                    def _(): self.sum_copy(way,j,u,False).wait_send()
            return 0
        lax.fori_loop(0,self.pieces,one,0)
    def piece_copy(self,way,c,u,src=None):
        sends,recvs=self.held_sems
        dst=self.held.at[c,self.span(u)]
        return remote(dst if src is None else src,dst,sends.at[way,c,u],recvs.at[way,c,u],self._target(way))
    def send_own(self,u,src=None):
        here,n=self.here,self.n
        for way in (0,1):
            @pl.when(here<n-1 if way==0 else here>0)
            def _(): self.piece_copy(way,here,u,src).start()
    def gather_step(self,t,source):
        if t==0:
            for u in range(min(2,self.pieces)): self.send_own(u,source.at[self.span(u),:])
        else:
            self.pass_pieces(t)
            if t+1<self.pieces: self.send_own(t+1,source.at[self.span(t+1),:])
    def gather_steps(self): return self.pieces+self.n-1
    def pass_pieces(self,t,use=None):
        here,n=self.here,self.n
        for k in range(1,n):
            u=t-k
            ok=self.fits(u)
            u=jnp.clip(u,0,self.pieces-1)
            for way in (0,1):
                c=here-k if way==0 else here+k
                there=ok&((c>=0) if way==0 else (c<n))
                c=jnp.clip(c,0,n-1)
                @pl.when(there)
                def _(): self.piece_copy(way,c,u).wait_recv()
                @pl.when(there&(here<n-1 if way==0 else here>0))
                def _(): self.piece_copy(way,c,u).start()
                if use is not None:
                    @pl.when(there)
                    def _(): use(c,u)
    def end_pieces(self):
        here,n=self.here,self.n
        def one(u,_):
            for k in range(n):
                for way in (0,1):
                    c=here-k if way==0 else here+k
                    there=(c>=0) if way==0 else (c<n)
                    c=jnp.clip(c,0,n-1)
                    @pl.when(there&(here<n-1 if way==0 else here>0))
                    def _(): self.piece_copy(way,c,u).wait_send()
            return 0
        lax.fori_loop(0,self.pieces,one,0)

def gain_terms(part,other,acc,c):
    rows=part.shape[1]
    def some(k,_):
        span=pl.ds(pl.multiple_of(k*16,16),16)
        both=part[c,span].astype(F32)*other[c,span].astype(F32)
        acc[...]+=both[:8]+both[8:]
        return 0
    lax.fori_loop(0,rows//16,some,0)

def last_kernel(count, plane, pieces, part_hbm, other_hbm, tokens_hbm, grads_hbm, gain, terms, out, shared, part, other, tokens, grads, cs, sums, total, ss, sr, acc, cut, landed, level, stacked, ds, dr, zs, zr):
    width=part.shape[2]
    line=Line(count,pieces,part.shape[1],part,sums,(ss,sr))
    loads=[pltpu.make_async_copy(s,d,cs.at[k]) for k,(s,d) in enumerate(((part_hbm,part),(other_hbm,other),(tokens_hbm,tokens),(grads_hbm,grads)))]
    for load in loads: load.start()
    greet(line.here,count,plane)
    loads[0].wait()
    acc[...]=jnp.zeros_like(acc)
    me=lax.axis_index(DP)
    piece=width//plane
    begin_dp,end_dp=swap(DP,plane,lambda p: cut.at[p],landed,ds,dr)
    begin_z,end_z=swap(AXIS,count,lambda p: level,stacked,zs,zr)
    def finish(span,total):
        stream=tokens[span,:].astype(F32)
        scale=lax.rsqrt(jnp.mean(stream*stream,-1,keepdims=True)+EPSILON)
        unit=stream*scale
        scaled=total[...]*gain[0:1,:]
        out[span,:]=grads[span,:]+scale*(scaled-unit*jnp.mean(scaled*unit,-1,keepdims=True))
    def step(t,_):
        line.far_step(t,total,finish)
        @pl.when(t==0)
        def _():
            for load in loads[1:]: load.wait()
        @pl.when(t<count)
        def _(): gain_terms(part,other,acc,jnp.clip(t,0,count-1))
        @pl.when(t==count-1)
        def _():
            for p in range(plane):
                cut[p,0:8,:]=acc[:,p*piece:(p+1)*piece]
                cut[p,8:16,:]=terms[:,p*piece:(p+1)*piece]
            landed[me]=cut[me]
            begin_dp()
        @pl.when(t==count+1)
        def _():
            end_dp()
            level[...]=jnp.sum(landed[...],0)
            stacked[line.here]=level[...]
            begin_z()
        return 0
    assert line.far_steps()>count+1
    lax.fori_loop(0,line.far_steps(),step,0)
    end_z()
    shared[...]=jnp.sum(stacked[...],0)
    line.end_sums()

def last_sums(part,other,tokens,grads,gains,terms,cid,pieces,n,plane):
    rows,D=tokens.shape
    vm=pl.BlockSpec(memory_space=pltpu.VMEM)
    hbm=pl.BlockSpec(memory_space=pl.ANY)
    sds=jax.ShapeDtypeStruct
    sem=pltpu.SemaphoreType.DMA
    w=D//plane
    return pl.pallas_call(functools.partial(last_kernel,n,plane,pieces),
        out_shape=(sds((rows,D),F32),sds((16,w),F32)),in_specs=[hbm]*4+[vm]*2,out_specs=(vm,vm),
        scratch_shapes=[pltpu.VMEM((n,rows,D),BF),pltpu.VMEM((n,rows,D),BF),pltpu.VMEM((rows,D),BF),pltpu.VMEM((rows,D),F32),sem((4,)),pltpu.VMEM((n+1,rows,D),BF),pltpu.VMEM((rows//pieces,D),F32),sem((2,n,pieces)),sem((2,n,pieces)),pltpu.VMEM((8,D),F32),
            pltpu.VMEM((plane,16,w),F32),pltpu.VMEM((plane,16,w),F32),pltpu.VMEM((16,w),F32),pltpu.VMEM((n,16,w),F32),
            sem((plane,)),sem((plane,)),sem((n,)),sem((n,))],
        cost_estimate=pl.CostEstimate(flops=0,bytes_accessed=270_000_000,transcendentals=0),
        compiler_params=pltpu.CompilerParams(collective_id=cid,has_side_effects=True,vmem_limit_bytes=56*1024*1024),
    )(part.reshape(n,rows,D),other.reshape(n,rows,D),tokens,grads,gains,terms)


def mlp_kernel(count,pieces,tile,grad_ref,res_hbm,x_hbm,early_hbm,wgu_hbm,wd_hbm,
        out_ref,part_hbm,wide_hbm,rest_hbm,x_ref,gr,product,gated,lifted,down,ring,tall,part_stage,wide_stage,res_ref,sums,total,
        hs,hr,ss,sr,ws,ts,ls,rs,xs,ps,os):
    length,hidden=product.shape
    width=x_ref.shape[1]
    rows=grad_ref.shape[0]
    half=rows//2
    first,second=hidden//tile,width//tile
    slots=ring.shape[0]
    begun=early_hbm.shape[1]
    spread=hs.shape[2]
    get=Line(count,spread,rows,held=gr,held_sems=(hs,hr),base=begun,sub=(rows-begun)//spread)
    line=Line(count,pieces,rows,down,sums,(ss,sr),sub=half//pieces)
    def strip(k,size): return pl.ds(pl.multiple_of(jnp.clip(k,0,size-1)*tile,tile),tile)
    def tall_load(k):
        slot=lax.rem(k,slots)
        @pl.when(k<2*first)
        def _(): pltpu.make_async_copy(wgu_hbm.at[:,strip(lax.rem(k,2)*first+k//2,2*first)],tall.at[slot],ts.at[slot]).start()
        @pl.when((k>=2*first)&(k<2*first+second))
        def _(): pltpu.make_async_copy(wd_hbm.at[:,strip(k-2*first,second)],tall.at[slot],ts.at[slot]).start()
    def tall_loaded(k):
        slot=lax.rem(k,slots)
        pltpu.make_async_copy(wd_hbm.at[:,pl.ds(0,tile)],tall.at[slot],ts.at[slot]).wait()
        return slot
    def load(k):
        slot=lax.rem(k,slots)
        @pl.when(k<first)
        def _(): pltpu.make_async_copy(wd_hbm.at[strip(k,first),:],ring.at[slot],ws.at[slot]).start()
        @pl.when((k>=first)&(k<first+2*second))
        def _():
            side=pl.ds(pl.multiple_of(lax.rem(k-first,2)*hidden,hidden),hidden)
            pltpu.make_async_copy(wgu_hbm.at[strip((k-first)//2,second),side],ring.at[slot],ws.at[slot]).start()
    def loaded(k):
        slot=lax.rem(k,slots)
        pltpu.make_async_copy(wd_hbm.at[pl.ds(0,tile),:],ring.at[slot],ws.at[slot]).wait()
        return slot
    def own(): return pltpu.make_async_copy(grad_ref,gr.at[get.here],ls.at[0])
    def early(c): return pltpu.make_async_copy(early_hbm.at[c],gr.at[c,pl.ds(0,begun)],ls.at[1+c])
    def rest(c): return pltpu.make_async_copy(down.at[c,pl.ds(half,half)],rest_hbm.at[c],rs.at[c])
    whole_x=pltpu.make_async_copy(x_hbm,x_ref,xs)
    whole_x.start()
    base=pltpu.make_async_copy(res_hbm.at[pl.ds(0,half)],res_ref,ls.at[1+count])
    base.start()
    for k in range(slots): tall_load(jnp.int32(k))
    greet(get.here,count)
    get.gather_step(0,grad_ref)
    own().start()
    for c in range(count):
        @pl.when(c!=get.here)
        def _(): early(c).start()
    whole_x.wait()
    hops=get.gather_steps()
    gather_marks=(1.5,2.75,4.0,6.0,7.0,8.0) if first==4 and second==4 and hops==7 else tuple(min(k+1,first+second) for k in range(hops-1))
    sum_marks=(0,3,5,6,7,9,12) if first==4 and second==4 and line.far_steps()==7 else tuple(min(k,first+4*second-1) for k in range(line.far_steps()))
    def gather_at(n,after=0.0):
        for k,mark in enumerate(gather_marks):
            if mark%1==after:
                @pl.when(n==int(mark))
                def _(): get.gather_step(k+1,grad_ref)
    def finish(span,total):
        out_ref[span,:]=(res_ref[span,:]+total[...]).astype(BF)
    def sum_at(n):
        for k,mark in enumerate(sum_marks):
            @pl.when(n==mark)
            def _(): line.far_step(jnp.int32(k),total,finish)
    def forward(n,_):
        gather_at(n)
        one=tall_loaded(2*n)
        two=tall_loaded(2*n+1)
        cols=strip(n,first)
        for c in range(count):
            if c: gather_at(n,c/count)
            span=slice(c*rows,(c+1)*rows)
            gate=jnp.dot(x_ref[span,:],tall[one],preferred_element_type=F32)
            up=jnp.dot(x_ref[span,:],tall[two],preferred_element_type=F32)
            sigmoid=1.0/(1.0+jnp.exp(-gate))
            active=gate*sigmoid
            product[span,cols]=(active*up).astype(BF)
            lifted[span,cols]=active.astype(BF)
            gated[span,cols]=(up*(sigmoid+active*(1.0-sigmoid))).astype(BF)
        tall_load(2*n+slots)
        tall_load(2*n+1+slots)
        return 0
    lax.fori_loop(0,first,forward,0)
    for k in range(slots): load(jnp.int32(k))
    def lower(n,_):
        gather_at(first+n)
        slot=tall_loaded(2*first+n)
        sums_here=jnp.dot(product[...],tall[slot],preferred_element_type=F32).astype(BF)
        cols=strip(n,second)
        for c in range(count): down[c,:,cols]=sums_here[c*rows:(c+1)*rows]
        tall_load(2*first+n+slots)
        return 0
    lax.fori_loop(0,second,lower,0)
    for c in range(count): rest(c).start()
    gather_at(jnp.int32(first+second))
    base.wait()
    own().wait()
    for c in range(count):
        @pl.when(c!=get.here)
        def _(): early(c).wait()
    def back(n,_):
        sum_at(n)
        slot=loaded(n)
        cols=strip(n,first)
        for c in range(count):
            span=slice(c*rows,(c+1)*rows)
            grads=lax.dot_general(gr[c],ring[slot],(((1,),(1,)),((),())),preferred_element_type=F32)
            gated[span,cols]=(grads*gated[span,cols].astype(F32)).astype(BF)
            lifted[span,cols]=(grads*lifted[span,cols].astype(F32)).astype(BF)
        load(n+slots)
        return 0
    lax.fori_loop(0,first,back,0)
    def part_copy(n):
        slot=lax.rem(n,2)
        return pltpu.make_async_copy(part_stage.at[slot],part_hbm.at[:,strip(n,second)],ps.at[slot])
    def inner(n,_):
        sum_at(first+n)
        k=first+2*n
        one=loaded(k)
        both=lax.dot_general(gated[...],ring[one],(((1,),(1,)),((),())),preferred_element_type=F32)
        load(k+slots)
        two=loaded(k+1)
        both=both+lax.dot_general(lifted[...],ring[two],(((1,),(1,)),((),())),preferred_element_type=F32)
        @pl.when(n>=2)
        def _(): part_copy(n-2).wait()
        part_stage[lax.rem(n,2)]=both.astype(BF)
        part_copy(n).start()
        load(k+1+slots)
        return 0
    lax.fori_loop(0,second,inner,0)
    def wide_copy(n):
        slot=lax.rem(n,2)
        side=pl.ds(pl.multiple_of(lax.rem(n,3)*hidden,hidden),hidden)
        return pltpu.make_async_copy(wide_stage.at[slot],wide_hbm.at[strip(n//3,second),side],os.at[slot])
    cut=hidden//2
    def weights(m,_):
        cols=strip(m,second)
        for kind in range(3):
            n=3*m+kind
            sum_at(first+second+n)
            @pl.when(n>=2)
            def _(): wide_copy(n-2).wait()
            left=gr[:,:,cols].reshape(length,tile) if kind==2 else x_ref[:,cols]
            right=(gated,lifted,product)[kind]
            for side in (0,1):
                these=slice(side*cut,(side+1)*cut)
                wide_stage[lax.rem(n,2),:,these]=lax.dot_general(left,right[:,these],(((0,),(0,)),((),())),preferred_element_type=F32).astype(BF)
            wide_copy(n).start()
        return 0
    lax.fori_loop(0,second,weights,0)
    get.end_pieces()
    line.end_sums()
    for c in range(count): rest(c).wait()
    for n in range(max(0,second-2),second): part_copy(jnp.int32(n)).wait()
    for n in range(3*second-2,3*second): wide_copy(jnp.int32(n)).wait()

def mlp(x,grad_out,residual,early,w_both,w_down,cid,spread,pieces,count):
    length,width=x.shape
    hidden=w_down.shape[0]
    rows=length//count
    tile=min(512,hidden,width)
    vm=pl.BlockSpec(memory_space=pltpu.VMEM)
    hbm=pl.BlockSpec(memory_space=pl.ANY)
    sds=jax.ShapeDtypeStruct
    sem=pltpu.SemaphoreType.DMA
    vmem=pltpu.VMEM
    half=rows//2
    return pl.pallas_call(functools.partial(mlp_kernel,count,pieces,tile),
        out_shape=(sds((half,width),BF),sds((length,width),BF),sds((width,3*hidden),BF),sds((count,half,width),BF)),
        in_specs=[vm,hbm,hbm,hbm,hbm,hbm],
        out_specs=(vm,hbm,hbm,hbm),
        scratch_shapes=[vmem((length,width),BF),vmem((count,rows,width),BF),vmem((length,hidden),BF),vmem((length,hidden),BF),vmem((length,hidden),BF),
            vmem((count,rows,width),BF),vmem((4,tile,width),BF),vmem((4,width,tile),BF),vmem((2,length,tile),BF),vmem((2,tile,hidden),BF),vmem((half,width),F32),
            vmem((count+1,half,width),BF),vmem((half//pieces,width),F32),
            sem((2,count,spread)),sem((2,count,spread)),sem((2,count,pieces)),sem((2,count,pieces)),sem((4,)),sem((4,)),sem((count+2,)),sem((count,)),sem,
            sem((2,)),sem((2,))],
        cost_estimate=pl.CostEstimate(flops=78_000_000_000,bytes_accessed=380_000_000,transcendentals=0),
        compiler_params=pltpu.CompilerParams(collective_id=cid,has_side_effects=True,vmem_limit_bytes=60*1024*1024),
    )(grad_out,residual,x,early,w_both,w_down)


def frequencies(head_size):
    inverse = 1.0 / 500000.0 ** (jnp.arange(head_size // 2, dtype=jnp.float32) * 2.0 / head_size)
    wavelength = 2.0 * math.pi / inverse
    smooth = (8192.0 / wavelength - 1.0) / 3.0
    blended = (1.0 - smooth) * inverse / 32.0 + smooth * inverse
    return jnp.where(
        wavelength > 8192.0, inverse / 32.0, jnp.where(wavelength < 2048.0, inverse, blended)
    )


def dot(left_side, right_side, left_dim, right_dim):
    return lax.dot_general(
        left_side, right_side, (((left_dim,), (right_dim,)), ((), ())), preferred_element_type=F32
    )


def norm_kernel(count, plane, pieces, tokens_ref, gains_ref, gate_hbm, up_hbm, angles_ref, normed_hbm, gains_out, both_hbm, cosine, sine, held, normed, landed, hs, hr, ds, dr, ws, bs):
    hidden = gate_hbm.shape[1]
    sides = [
        pltpu.make_async_copy(source, both_hbm.at[:, pl.ds(k * hidden, hidden)], bs.at[k])
        for k, source in enumerate((gate_hbm, up_hbm))
    ]
    line = Line(count, pieces, tokens_ref.shape[0], held=held, held_sems=(hs, hr))
    greet(line.here, count, plane)
    me = lax.axis_index(DP)
    begin, end = swap(DP, plane, lambda p: gains_ref, landed, ds, dr)
    for u in range(pieces):
        line.send_own(u, tokens_ref.at[line.span(u), :])
    begin()
    for side in sides:
        side.start()
    landed[me] = gains_ref[...]
    end()
    piece = gains_ref.shape[1]
    for p in range(plane):
        gains_out[:, p * piece : (p + 1) * piece] = landed[p]

    def give(c, u):
        return pltpu.make_async_copy(normed.at[c, line.span(u)], normed_hbm.at[c, line.span(u)], ws.at[c, u])

    def norm(rows, c, u):
        stream = rows.astype(F32)
        scale = lax.rsqrt(jnp.mean(stream * stream, -1, keepdims=True) + EPSILON)
        normed[c, line.span(u)] = (stream * scale * gains_out[0:1, :]).astype(BF)
        give(c, u).start()

    def step(t, _):
        line.pass_pieces(t)
        for k in range(1, count):
            u = t - k
            for c in (line.here - k, line.here + k):

                @pl.when(line.fits(u) & (c >= 0) & (c < count))
                def _():
                    place, piece = jnp.clip(c, 0, count - 1), jnp.clip(u, 0, pieces - 1)
                    norm(held[place, line.span(piece)], place, piece)

        @pl.when(t == 1)
        def _():
            cosine[...] = jnp.cos(angles_ref[...])
            sine[...] = jnp.sin(angles_ref[...])

        @pl.when(t < pieces)
        def _():
            u = jnp.clip(t, 0, pieces - 1)
            norm(tokens_ref[line.span(u), :], line.here, u)

        return 0

    lax.fori_loop(0, pieces + count - 1, step, 0)
    line.end_pieces()
    for side in sides:
        side.wait()
    for c in range(count):
        for u in range(pieces):
            give(c, u).wait()


def norm_and_gather(tokens, gains, w_gate, w_up, angles, cid, pieces, count, plane):
    rows, width = tokens.shape
    vm = pl.BlockSpec(memory_space=pltpu.VMEM)
    sem = pltpu.SemaphoreType.DMA
    hbm = pl.BlockSpec(memory_space=pl.ANY)
    sds = jax.ShapeDtypeStruct
    normed, *rest = pl.pallas_call(
        functools.partial(norm_kernel, count, plane, pieces),
        out_shape=(
            sds((count, rows, width), BF),
            sds((8, width), F32),
            sds((w_gate.shape[0], 2 * w_gate.shape[1]), BF),
            sds(angles.shape, F32),
            sds(angles.shape, F32),
        ),
        in_specs=[vm, vm, hbm, hbm, vm],
        out_specs=(hbm, vm, hbm, vm, vm),
        scratch_shapes=[
            pltpu.VMEM((count, rows, width), BF),
            pltpu.VMEM((count, rows, width), BF),
            pltpu.VMEM((plane, 8, width // plane), F32),
            sem((2, count, pieces)),
            sem((2, count, pieces)),
            sem((plane,)),
            sem((plane,)),
            sem((count, pieces)),
            sem((2,)),
        ],
        cost_estimate=pl.CostEstimate(flops=0, bytes_accessed=270_000_000, transcendentals=0),
        compiler_params=pltpu.CompilerParams(
            collective_id=cid, has_side_effects=True, vmem_limit_bytes=58 * 1024 * 1024
        ),
    )(tokens, gains, w_gate, w_up, angles)
    return normed.reshape(count * rows, width), *rest


def wide_results_kernel(gate_in, up_in, down_in, tokens_in, block_in, sums_ref, gains_ref, gate, up, down, tokens, block, terms):
    tokens[...] = tokens_in[...]
    block[...] = block_in[...]
    terms[0:1, :] = jnp.sum(sums_ref[0:8, :], 0, keepdims=True) / gains_ref[0:1, :]
    terms[1:2, :] = jnp.sum(sums_ref[8:16, :], 0, keepdims=True) / gains_ref[1:2, :]
    gate[...] = gate_in[...].astype(F32)
    up[...] = up_in[...].astype(F32)
    down[...] = down_in[...].astype(F32).T


def wide_results(wide, grad_tokens, block_out, sums, gains, hidden):
    shard = wide.shape[0]
    tile = min(512, hidden)
    steps = hidden // tile
    sds = jax.ShapeDtypeStruct
    still = lambda shape: pl.BlockSpec(shape, lambda s: (0, 0))
    strip = pl.BlockSpec((grad_tokens.shape[0], grad_tokens.shape[1] // steps), lambda s: (0, s))
    return pl.pallas_call(
        wide_results_kernel,
        grid=(steps,),
        out_shape=(
            sds((shard, hidden), F32),
            sds((shard, hidden), F32),
            sds((hidden, shard), F32),
            sds(grad_tokens.shape, F32),
            sds(block_out.shape, BF),
            sds((2, shard), F32),
        ),
        in_specs=[pl.BlockSpec((shard, tile), lambda s, k=k: (0, k * steps + s)) for k in range(3)]
        + [strip, strip, still(sums.shape), still(gains.shape)],
        out_specs=(
            pl.BlockSpec((shard, tile), lambda s: (0, s)),
            pl.BlockSpec((shard, tile), lambda s: (0, s)),
            pl.BlockSpec((tile, shard), lambda s: (s, 0)),
            strip,
            strip,
            still((2, shard)),
        ),
        compiler_params=pltpu.CompilerParams(vmem_limit_bytes=60 * 1024 * 1024),
    )(wide, wide, wide, grad_tokens, block_out, sums, gains)


def mix_results_kernel(mix_ref, terms_ref, query, key, value, out, first, second):
    edge = query.shape[1]
    query[...] = mix_ref[:, :edge].astype(F32)
    key[...] = mix_ref[:, edge : edge + key.shape[1]].astype(F32)
    edge += key.shape[1]
    value[...] = mix_ref[:, edge : edge + value.shape[1]].astype(F32)
    edge += value.shape[1]
    out[...] = mix_ref[:, edge:].astype(F32).T
    first[...] = terms_ref[0:1, :]
    second[...] = terms_ref[1:2, :]


def mix_results(mix, terms, deep, narrow):
    shard = mix.shape[0]
    sds = jax.ShapeDtypeStruct
    vm = pl.BlockSpec(memory_space=pltpu.VMEM)
    return pl.pallas_call(
        mix_results_kernel,
        out_shape=(
            sds((shard, deep), F32),
            sds((shard, narrow), F32),
            sds((shard, narrow), F32),
            sds((deep, shard), F32),
            sds((1, shard), F32),
            sds((1, shard), F32),
        ),
        in_specs=[vm, vm],
        out_specs=(vm,) * 6,
        compiler_params=pltpu.CompilerParams(vmem_limit_bytes=60 * 1024 * 1024),
    )(mix, terms)


def body(
    count,
    plane,
    tokens,
    segments,
    positions,
    attn_gain,
    w_query,
    w_key,
    w_value,
    w_out,
    mlp_gain,
    w_gate,
    w_up,
    w_down,
    grad_out,
):
    rows, width = tokens.shape
    heads = w_query.shape[1] // HD
    groups = w_key.shape[1] // HD
    after = lax.optimization_barrier
    mix = lax.all_gather(jnp.concatenate([w_query, w_key, w_value], 1), DP, axis=0, tiled=True)
    full_out = lax.all_gather(w_out, DP, axis=1, tiled=True)
    full_down = lax.all_gather(w_down, DP, axis=1, tiled=True)
    own_gains = jnp.concatenate([jnp.stack([attn_gain, mlp_gain]).astype(F32), jnp.zeros((6, attn_gain.shape[0]), F32)])

    angles = frequencies(HD)[:, None] * positions.astype(F32)[None, :]
    normed_one, gains, both, cosine, sine = norm_and_gather(tokens, own_gains, w_gate, w_up, angles, 1, 4, count, plane)
    full_both = lax.all_gather(both, DP, axis=0, tiled=True)

    mixed, q, kt, k, v, residual, early, normed_two = attend(
        mix, normed_one, cosine, sine, segments, full_out, grad_out, tokens, gains, heads, groups, 6, rows // 2, 4, 16, count
    )
    normed_two = normed_two.reshape(count * rows, width)
    block_early, part, grad_wide, down = mlp(normed_two, grad_out, residual, early, full_both, full_down, 5, 4, 2, count)
    grad_wide = lax.psum_scatter(grad_wide, DP, scatter_dimension=0, tiled=True)
    grad_residual, terms_two, part, grad_mix, block_out = attend_back(
        part, normed_two, grad_out, gains, full_out, q, kt, k, v, cosine, sine, down, residual, block_early,
        mixed, normed_one, mix, heads, groups, 7, 2, 16, count,
    )
    grad_mix = lax.psum_scatter(grad_mix, DP, scatter_dimension=0, tiled=True)
    grad_tokens, sums = last_sums(part, normed_one, tokens, grad_residual, gains, terms_two, 4, 4, count, plane)
    grad_gate, grad_up, grad_down, grad_tokens, block_out, terms = wide_results(
        grad_wide, grad_tokens, block_out, sums, own_gains, full_down.shape[0]
    )
    grad_query, grad_key, grad_value, grad_out_proj, grad_attn_gain, grad_mlp_gain = mix_results(
        grad_mix, terms, heads * HD, groups * HD
    )
    return (
        block_out,
        grad_tokens,
        grad_attn_gain.reshape(-1),
        grad_query,
        grad_key,
        grad_value,
        grad_out_proj,
        grad_mlp_gain.reshape(-1),
        grad_gate,
        grad_up,
        grad_down,
    )


def solution(mesh):
    placed = (
        P(("dp", "tensor"), None),
        P("dp"),
        P("dp"),
        P("dp"),
        P("dp", "tensor"),
        P("dp", "tensor"),
        P("dp", "tensor"),
        P("tensor", "dp"),
        P("dp"),
        P("dp", "tensor"),
        P("dp", "tensor"),
        P("tensor", "dp"),
        P(("dp", "tensor"), None),
    )
    return jax.shard_map(
        functools.partial(body, mesh.shape["tensor"], mesh.shape["dp"]),
        mesh=mesh,
        in_specs=placed,
        out_specs=(
            P(("dp", "tensor"), None),
            P(("dp", "tensor"), None),
            P("dp"),
            P("dp", "tensor"),
            P("dp", "tensor"),
            P("dp", "tensor"),
            P("tensor", "dp"),
            P("dp"),
            P("dp", "tensor"),
            P("dp", "tensor"),
            P("tensor", "dp"),
        ),
        check_vma=False,
    )
```
